32 devices in a mesh: section: 2 (over x), dp: 4 (over y, core), seq: 4 (over z).
Axes of the slice: x: 2, y: 2, z: 4, core: 2. Of those that a mesh axis runs over, the one named last changes fastest.
Arguments:
- boundary: bfloat16 [2, 2, 4, 672, 384], P('section', None, 'dp', 'seq'), may hold values from -6 to 6
- lengths: int32 [2, 4, 4], P(None, 'dp'), may hold values from 1 to 168, 577 in all within a row
- w_qkv: bfloat16 [2, 384, 1152], P('section', ('dp', 'seq')), may hold values from -0.3125 to 0.3125
- w_out: bfloat16 [2, 384, 384], P('section', ('dp', 'seq')), may hold values from -3.5 to 3.5
- w_fc1: bfloat16 [2, 384, 1536], P('section', ('dp', 'seq')), may hold values from -0.3125 to 0.3125
- w_fc2: bfloat16 [2, 1536, 384], P('section', ('dp', 'seq')), may hold values from -0.15625 to 0.15625
- gains: bfloat16 [2, 768], P('section', ('dp', 'seq')), may hold values from 0.5 to 1.5
- shifts: bfloat16 [2, 2304], P('section', ('dp', 'seq')), may hold values from -2 to 2
- fc1_bias: bfloat16 [2, 1536], P('section', ('dp', 'seq')), may hold values from -2 to 2
Outputs:
- boundary_out: bfloat16 [2, 2, 4, 672, 384], P('section', None, 'dp', 'seq')
- grad_qkv: float32 [2, 384, 1152], P('section', ('dp', 'seq'))
- grad_out: float32 [2, 384, 384], P('section', ('dp', 'seq'))
- grad_fc1: float32 [2, 384, 1536], P('section', ('dp', 'seq'))
- grad_fc2: float32 [2, 1536, 384], P('section', ('dp', 'seq'))
- grad_gains: float32 [2, 768], P('section', ('dp', 'seq'))
- grad_shifts: float32 [2, 2304], P('section', ('dp', 'seq'))
- grad_fc1_bias: float32 [2, 1536], P('section', ('dp', 'seq'))
The draws below stay inside these ranges and needn't reach their ends.
Inputs may be any that keep to these rules, and one draw needn't show every extreme that they name: `lengths`: for each micro-batch and image the 4 entries are the token counts of consecutive ranges in index order, together 577; an index holds its range in its first slots, each entry is at least 1, and in every image one entry is exactly 168.
All inputs are finite; a program needn't handle non-finite values.
Results may differ from the reference program's by a relative error of at most 0.022.
Values may be sent and summed in bfloat16 or wider, within the bound.
No kernel may reach another device: no remote copies, remote signals or barrier semaphores. Data moves between devices by JAX's collectives and lax.ppermute only.
A program may use at most 128 MiB of HBM per device.

```python
import math
import jax
import jax.numpy as jnp
import numpy as np
from jax import lax

D = 384
FF = 1536
HEADS = 6
IMG_TOK = 577
MICRO = 2
CAP = 168
SLOTS = 672
IMAGES = 4
N_SEQ = 4


def level_of(own_key, shape, pieces, low, top_value):
    level, own = 1.0, jax.random.fold_in(own_key, 6)
    for position, shards_of in pieces:
        draws = jnp.exp(jax.random.uniform(jax.random.fold_in(own, position), (shards_of,), jnp.float32, low / len(pieces), top_value / len(pieces)))
        level = level * jnp.repeat(draws, shape[position] // shards_of).reshape([-1 if axis == position else 1 for axis in range(len(shape))])
    return level


def profile(count, total, bound, slope):
    loads = [(1 << 20) // math.isqrt(grade ** slope) + 1 for grade in range(2, count + 1)]
    rest, counts = total - bound - (count - 1), [1] * (count - 1)
    while rest > 0:
        movable = [i for i in range(count - 1) if counts[i] < bound]
        mass, budget = sum([loads[i] for i in movable]), rest
        for i in movable:
            extra = min(bound - counts[i], max(1, budget * loads[i] // mass), rest)
            counts[i] = counts[i] + extra
            rest = rest - extra
    return np.array([bound] + counts)


def ragged(stream_key, number_of, total, limit, lean):
    if number_of == 2:
        one = jax.random.randint(stream_key, (), max(1, total - limit), min(limit, total - 1) + 1)
        return jnp.stack([one, total - one])
    sizes = jnp.asarray(profile(number_of, total, limit, lean), jnp.int32)
    pairs = (number_of - 1) // 2
    source_of, taker = sizes[1:1 + 2 * pairs:2], sizes[2:2 + 2 * pairs:2]
    margin = jnp.minimum(source_of - 1, limit - taker)
    passed = jax.random.randint(jax.random.fold_in(stream_key, 1), (pairs,), 0, 1 << 20) % (margin + 1)
    sizes = sizes.at[1:1 + 2 * pairs:2].set(source_of - passed).at[2:2 + 2 * pairs:2].set(taker + passed)
    return sizes[jax.random.permutation(jax.random.fold_in(stream_key, 2), number_of)]


def scatter_about(own_key, shape, width, bound, shards=(), kind=jnp.bfloat16):
    factor_of = level_of(own_key, shape, shards, -0.22, 0.18) if shards else 1.0
    result = jax.random.normal(own_key, shape, jnp.float32) * width * factor_of
    return jnp.minimum(jnp.maximum(result, -bound), bound).astype(kind)


def setup_inputs(seed: int = 0) -> dict:
    streams_of = jax.random.split(jax.random.key(seed), 10)
    return {
        "boundary": scatter_about(streams_of[0], (2, MICRO, IMAGES, SLOTS, D), 1.0, 6.0, ((0, 2), (2, 4), (3, 4))),
        "lengths": jax.vmap(lambda own: ragged(own, N_SEQ, IMG_TOK, CAP, 2))(jax.random.split(streams_of[1], MICRO * IMAGES)).reshape((MICRO, IMAGES, N_SEQ)).astype(jnp.int32),
        "w_qkv": scatter_about(streams_of[2], (2, D, 3 * D), D ** -0.5, 0.3125, ((0, 2), (1, 16))),
        "w_out": scatter_about(streams_of[3], (2, D, D), (max(D // 128, 1)) ** -0.5, 3.5, ((0, 2), (1, 16))),
        "w_fc1": scatter_about(streams_of[4], (2, D, FF), D ** -0.5, 0.3125, ((0, 2), (1, 16))),
        "w_fc2": scatter_about(streams_of[5], (2, FF, D), FF ** -0.5, 0.15625, ((0, 2), (1, 16))),
        "gains": jnp.clip(1.0 + 0.1 * jax.random.normal(streams_of[6], (2, 2 * D), jnp.float32), 0.5, 1.5).astype(jnp.bfloat16),
        "shifts": scatter_about(streams_of[7], (2, 6 * D), 0.3, 2.0, ((0, 2), (1, 16))),
        "fc1_bias": scatter_about(streams_of[8], (2, FF), 0.3, 2.0, ((0, 2), (1, 16))),
    }


norm_eps = 1e-06

@jax.custom_vjp
def low(v):
    return lax.optimization_barrier(v.astype(jnp.bfloat16)).astype(jnp.float32)

@jax.custom_vjp
def low_back(v):
    return v

def low_keep(v):
    return (low(v), None)

def low_pass(kept, grad):
    return (grad,)

def back_keep(v):
    return (v, None)

def back_low(kept, grad):
    return (low(grad),)
low.defvjp(low_keep, low_pass)
low_back.defvjp(back_keep, back_low)

def norm_rows(rows_in, gain, shift):
    centre = lax.optimization_barrier(jnp.mean(rows_in, axis=-1, keepdims=True))
    centred = rows_in - centre
    spread = lax.optimization_barrier(jnp.mean(centred * centred, axis=-1, keepdims=True))
    return centred * lax.rsqrt(spread + norm_eps) * gain + shift

def matmul(left, right):
    return jnp.dot(left, right, precision=lax.Precision.HIGHEST)

def slot_valid(lengths_img):
    positions = jnp.arange(N_SEQ * CAP, dtype=jnp.int32)
    owners = positions // CAP
    places = positions % CAP
    reached = lengths_img[owners]
    return (places < reached).astype(jnp.float32)

def encoder(block_in, row_valid, params):
    w_qkv, w_out, w_fc1, w_fc2, gains, shifts, fc1_bias = params
    model_width = w_out.shape[0]
    head_dim = model_width // HEADS
    score_scale = head_dim ** (-0.5)
    gains = gains.reshape(2, model_width)
    shifts = shifts.reshape(6, model_width)
    slot_total = block_in.shape[0]
    block_in = block_in * row_valid[:, None]
    normed = low(norm_rows(block_in, gains[0], shifts[0]))
    projected = matmul(normed, w_qkv)
    queries = low(low_back(projected[:, :model_width] + shifts[2]))
    own_keys = low(low_back(projected[:, model_width:2 * model_width]))
    own_values = low(low_back(projected[:, 2 * model_width:] + shifts[3]))
    query_heads = queries.reshape(slot_total, HEADS, head_dim)
    key_heads = own_keys.reshape(slot_total, HEADS, head_dim)
    value_heads = own_values.reshape(slot_total, HEADS, head_dim)
    scores = jnp.einsum('qhd,khd->hqk', query_heads, key_heads, precision=lax.Precision.HIGHEST) * score_scale
    scores = low_back(jnp.where(row_valid[None, None, :] > 0, scores, -1e+30))
    attn_probs = low(jax.nn.softmax(scores, axis=-1))
    attended = jnp.einsum('hqk,khd->qhd', attn_probs, value_heads, precision=lax.Precision.HIGHEST)
    attended = low(low_back(attended.reshape(slot_total, model_width)))
    branch = low_back(matmul(attended, w_out) + shifts[4])
    middle = block_in + branch
    normed_two = low(norm_rows(middle, gains[1], shifts[1]))
    hidden = low_back(matmul(normed_two, w_fc1) + fc1_bias)
    active = low(jax.nn.gelu(hidden, approximate=False))
    block_out = middle + low_back(matmul(active, w_fc2) + shifts[5])
    return block_out * row_valid[:, None]

def both_layers(image_in, row_valid, first, second):
    middle_out = low(low_back(encoder(image_in, row_valid, first)))
    return encoder(middle_out, row_valid, second)

def reference(boundary, lengths, w_qkv, w_out, w_fc1, w_fc2, gains, shifts, fc1_bias):
    slot_total = N_SEQ * CAP
    model_width = w_out.shape[1]
    images_in = boundary[0].astype(jnp.float32).reshape(-1, slot_total, model_width)
    cotangent = boundary[1].astype(jnp.float32).reshape(-1, slot_total, model_width)
    valid = jax.vmap(slot_valid)(lengths.reshape(-1, N_SEQ))
    stacked = tuple((member.astype(jnp.float32) for member in (w_qkv, w_out, w_fc1, w_fc2, gains, shifts, fc1_bias)))
    one_image = jax.checkpoint(both_layers)

    def forward(images_all, params_all):
        first = tuple((member[0] for member in params_all))
        second = tuple((member[1] for member in params_all))

        def per_image(image_item):
            return one_image(image_item[0], image_item[1], first, second)
        return lax.map(per_image, (images_all, valid))
    outputs, pullback = jax.vjp(forward, images_in, stacked)
    grad_in, grad_params = pullback(cotangent)
    full_shape = boundary.shape[1:]
    boundary_out = jnp.stack([grad_in.reshape(full_shape), outputs.reshape(full_shape)]).astype(jnp.bfloat16)
    return (boundary_out, grad_params[0], grad_params[1], grad_params[2], grad_params[3], grad_params[4], grad_params[5], grad_params[6])
```

```python
import functools
import math
import jax
import jax.numpy as jnp
from jax import lax
from jax.experimental import pallas as pl
from jax.experimental.pallas import tpu as pltpu
from jax.sharding import PartitionSpec as P

HEADS = 6
norm_eps = 1e-06
F32 = jnp.float32
BF16 = jnp.bfloat16


def mul(left, right, left_dim=1, right_dim=0):
    return lax.dot_general(
        left, right, (((left_dim,), (right_dim,)), ((), ())), preferred_element_type=F32
    )


def norm_parts(rows_in):
    centre = jnp.mean(rows_in, axis=-1, keepdims=True)
    centred = rows_in - centre
    spread = jnp.mean(centred * centred, axis=-1, keepdims=True)
    scale = lax.rsqrt(spread + norm_eps)
    return centred * scale, scale


def norm_grad(grad, gain, unit, scale):
    scaled = grad * gain
    inner = jnp.mean(scaled * unit, axis=-1, keepdims=True)
    return scale * (scaled - jnp.mean(scaled, axis=-1, keepdims=True) - unit * inner)


def gelu_parts(hidden):
    cdf = 0.5 + 0.5 * lax.erf(hidden * math.sqrt(0.5))
    return cdf


def layer_kernel(backward, grads, own, *refs):
    refs = list(refs)
    x_ref, mask_ref, w_ref, vec_ref = refs[:4]
    refs = refs[4:]
    if backward:
        dy_ref = refs.pop(0)
    y_ref = refs.pop(0)
    if backward:
        du_ref = refs.pop(0)
    if grads:
        gw_ref, gv_ref = refs[:2]
        refs = refs[2:]
    q_s, k_s, v_s, vt_s, ot_s, mid_s, c_s, acc_s = refs[:8]
    refs = refs[8:]
    if backward:
        kt_s, p_s, do_s, dq_s, dk_s, dv_s, h_s = refs
    total, width = x_ref.shape
    pairs = k_s.shape[0]
    slabs = (w_ref.shape[0] - 4) // 2
    head_dim = width // HEADS
    score_scale = head_dim ** (-0.5)

    def vec(index):
        return vec_ref[index : index + 1, :]

    mask = mask_ref[...]
    unit1, scale1 = norm_parts(x_ref[...].astype(F32) * mask)
    normed = (unit1 * vec(0) + vec(2)).astype(BF16)
    queries = (mul(normed[:own], w_ref[0]) + vec(4)).astype(BF16)
    queries = (queries.astype(F32) * score_scale).astype(BF16)
    keys = mul(normed, w_ref[1]).astype(BF16)
    values = (mul(normed, w_ref[2]) + vec(5)).astype(BF16)
    for j in range(pairs):
        lanes = slice(j * 128, (j + 1) * 128)
        q_s[j] = queries[:, lanes]
        k_s[j] = keys[:, lanes]
        v_s[j] = values[:, lanes]
        vt_s[j] = values[:, lanes].T
        if backward:
            kt_s[j] = keys[:, lanes].T
    lane = lax.broadcasted_iota(jnp.int32, (1, 128), 1)
    first_half = (lane < head_dim).astype(BF16)
    halves = (first_half, 1 - first_half)

    @pl.loop(0, pairs)
    def _(j):
        bias = (mask_ref[...] - 1.0) * 1e30
        for e in range(2):
            score = mul(k_s[j], q_s[j] * halves[e], 1, 1) + bias
            top = jnp.max(score, axis=0, keepdims=True)
            expo = jnp.exp(score - top)
            probs = (expo * (1.0 / jnp.sum(expo, axis=0, keepdims=True))).astype(BF16)
            rows = slice(e * head_dim, (e + 1) * head_dim)
            ot_s[j, rows, :] = mul(vt_s[j, rows, :], probs).astype(BF16)
            if backward:
                p_s[2 * j + e] = probs

    attended = jnp.concatenate([ot_s[j].T for j in range(pairs)], axis=1)
    mid_s[...] = x_ref[:own, :].astype(F32) * mask[:own] + mul(attended, w_ref[3]) + vec(6)
    unit2, scale2 = norm_parts(mid_s[...])
    c_s[...] = (unit2 * vec(1) + vec(3)).astype(BF16)
    acc_s[...] = jnp.zeros_like(acc_s)

    @pl.loop(0, slabs)
    def _(k):
        hidden = mul(c_s[...], w_ref[4 + k]) + vec_ref[pl.ds(8 + k, 1), :]
        if backward:
            h_s[k] = hidden
        active = (hidden * gelu_parts(hidden)).astype(BF16)
        acc_s[...] += mul(active, w_ref[4 + slabs + k])

    y_ref[...] = ((mid_s[...] + acc_s[...] + vec(7)) * mask[:own]).astype(BF16)
    if not backward:
        return

    grad_y = dy_ref[...].astype(F32) * mask[:own]
    grad_second = grad_y.astype(BF16)
    c_now = c_s[...]
    c_turned = c_now.T if grads else None
    acc_s[...] = jnp.zeros_like(acc_s)

    @pl.loop(0, slabs)
    def _(k):
        hidden = h_s[k]
        cdf = gelu_parts(hidden)
        slope = cdf + hidden * jnp.exp(-0.5 * hidden * hidden) * (1.0 / math.sqrt(2 * math.pi))
        grad_second = (dy_ref[...].astype(F32) * mask_ref[:own, :]).astype(BF16)
        grad_hidden = mul(grad_second, w_ref[4 + slabs + k], 1, 1) * slope
        grad_low = grad_hidden.astype(BF16)
        acc_s[...] += mul(grad_low, w_ref[4 + k], 1, 1)
        if grads:
            active = (hidden * cdf).astype(BF16)
            gw_ref[4 + k] = mul(c_s[...], grad_low, 0, 0).astype(BF16)
            gw_ref[4 + slabs + k] = mul(active, grad_second, 0, 0).astype(BF16)
            gv_ref[pl.ds(8 + k, 1), :] = jnp.sum(grad_low.astype(F32), axis=0, keepdims=True)

    def total_of(rows):
        return jnp.sum(rows, axis=0, keepdims=True)

    grad_c = acc_s[...]
    unit2, scale2 = norm_parts(mid_s[...])
    grad_mid = grad_y + norm_grad(grad_c, vec(1), unit2, scale2)
    grad_branch = grad_mid.astype(BF16)
    grad_att = mul(grad_branch, w_ref[3], 1, 1).astype(BF16)
    if grads:
        gv_ref[1:2, :] = total_of(grad_c * unit2)
        gv_ref[3:4, :] = total_of(grad_c)
        gv_ref[6:7, :] = total_of(grad_branch.astype(F32))
        gv_ref[7:8, :] = total_of(grad_second.astype(F32))
        for j in range(pairs):
            gw_ref[3, j * 128 : (j + 1) * 128, :] = mul(ot_s[j], grad_branch).astype(BF16)
    for j in range(pairs):
        do_s[j] = grad_att[:, j * 128 : (j + 1) * 128]
    mid_s[...] = grad_mid

    @pl.loop(0, pairs)
    def _(j):
        grad_k = None
        for e in range(2):
            half_do = do_s[j] * halves[e]
            half_q = q_s[j] * halves[e]
            grad_p = mul(v_s[j], half_do, 1, 1)
            probs_low = p_s[2 * j + e]
            probs = probs_low.astype(F32)
            row_dot = jnp.sum(probs * grad_p, axis=0, keepdims=True)
            grad_s = (probs * (grad_p - row_dot)).astype(BF16)
            rows = slice(e * head_dim, (e + 1) * head_dim)
            dq_s[j, rows, :] = (mul(kt_s[j, rows, :], grad_s) * score_scale).astype(BF16)
            part_k = mul(grad_s, half_q)
            part_v = mul(probs_low, half_do)
            grad_k, grad_v = (part_k, part_v) if grad_k is None else (grad_k + part_k, grad_v + part_v)
        dk_s[j] = grad_k.astype(BF16)
        dv_s[j] = grad_v.astype(BF16)

    grad_q = jnp.concatenate([dq_s[j].T for j in range(pairs)], axis=1)
    grad_k = jnp.concatenate([dk_s[j] for j in range(pairs)], axis=1)
    grad_v = jnp.concatenate([dv_s[j] for j in range(pairs)], axis=1)
    unit1, scale1 = norm_parts(x_ref[...].astype(F32) * mask)
    if grads:
        normed = (unit1 * vec(0) + vec(2)).astype(BF16)
        gw_ref[0] = mul(normed[:own], grad_q, 0, 0).astype(BF16)
        turned = normed.T
        gw_ref[1] = mul(turned, grad_k).astype(BF16)
        gw_ref[2] = mul(turned, grad_v).astype(BF16)
        gv_ref[4:5, :] = total_of(grad_q.astype(F32))
        gv_ref[5:6, :] = total_of(grad_v.astype(F32))
    grad_n = mul(grad_k, w_ref[1], 1, 1) + mul(grad_v, w_ref[2], 1, 1)
    grad_n = jnp.concatenate([grad_n[:own] + mul(grad_q, w_ref[0], 1, 1), grad_n[own:]], axis=0)
    if grads:
        gv_ref[0:1, :] = total_of(grad_n * unit1)
        gv_ref[2:3, :] = total_of(grad_n)
    grad_u = norm_grad(grad_n, vec(0), unit1, scale1)
    grad_u = jnp.concatenate([grad_u[:own] + mid_s[...], grad_u[own:]], axis=0)
    du_ref[...] = (grad_u * mask).astype(BF16)


def run_layer(x_all, mask, weights, vectors, own, grad_out=None, grads=False):
    backward = grad_out is not None
    total, width = x_all.shape
    pairs = width // 128
    slabs = (weights.shape[0] - 4) // 2
    operands = [x_all, mask, weights, vectors]
    shapes = [jax.ShapeDtypeStruct((own, width), BF16)]
    scratch = [
        pltpu.VMEM((pairs, own, 128), BF16),
        pltpu.VMEM((pairs, total, 128), BF16),
        pltpu.VMEM((pairs, total, 128), BF16),
        pltpu.VMEM((pairs, 128, total), BF16),
        pltpu.VMEM((pairs, 128, own), BF16),
        pltpu.VMEM((own, width), F32),
        pltpu.VMEM((own, width), BF16),
        pltpu.VMEM((own, width), F32),
    ]
    if backward:
        operands.append(grad_out)
        shapes.append(jax.ShapeDtypeStruct((total, width), BF16))
        scratch += [
            pltpu.VMEM((pairs, 128, total), BF16),
            pltpu.VMEM((HEADS, total, own), BF16),
            pltpu.VMEM((pairs, own, 128), BF16),
            pltpu.VMEM((pairs, 128, own), BF16),
            pltpu.VMEM((pairs, total, 128), BF16),
            pltpu.VMEM((pairs, total, 128), BF16),
            pltpu.VMEM((slabs, own, width), F32),
        ]
    if grads:
        shapes.append(jax.ShapeDtypeStruct(weights.shape, BF16))
        shapes.append(jax.ShapeDtypeStruct((16, width), F32))
    whole = pl.BlockSpec(memory_space=pltpu.VMEM)
    return pl.pallas_call(
        functools.partial(layer_kernel, backward, grads, own),
        out_shape=shapes,
        in_specs=[whole] * len(operands),
        out_specs=[whole] * len(shapes),
        scratch_shapes=scratch,
        compiler_params=pltpu.CompilerParams(vmem_limit_bytes=50 * 1024 * 1024),
        cost_estimate=pl.CostEstimate(flops=2 * 10**9, bytes_accessed=4 * 10**6, transcendentals=2 * 10**6),
    )(*operands)


def axis_sizes():
    return lax.axis_size("dp"), lax.axis_size("seq")


def core_pairs(dp_count):
    return [(index, index ^ 1) for index in range(dp_count)]


def swap_core(value):
    return lax.ppermute(value, "dp", core_pairs(lax.axis_size("dp")))


def turn_outer(value, steps):
    count = lax.axis_size("dp")
    return lax.ppermute(value, "dp", [(d, (d + 2 * steps) % count) for d in range(count)])


def joint_permute(value, moves):
    seq_count = lax.axis_size("seq")
    pairs = [(a[0] * seq_count + a[1], b[0] * seq_count + b[1]) for a, b in moves]
    return lax.ppermute(value, ("dp", "seq"), pairs)


def along_line(value, steps):
    count = lax.axis_size("seq")
    return lax.ppermute(
        value, "seq", [(z, z + steps) for z in range(count) if 0 <= z + steps < count]
    )


def in_order(relative, index, count):
    return lax.dynamic_slice_in_dim(jnp.stack(relative), count - 1 - index, count, 0)


def gather_pieces(piece):
    dp_count, seq_count = axis_sizes()
    outer_count = dp_count // 2
    d, z = lax.axis_index("dp"), lax.axis_index("seq")
    o, c = d // 2, d % 2
    ups, downs = [piece], [piece]
    for step in range(1, seq_count):
        ups.append(along_line(ups[-1], 1))
        downs.append(along_line(downs[-1], -1))
    line = in_order(ups[:0:-1] + [piece] + downs[1:], z, seq_count)
    others = [line] + [turn_outer(line, k) for k in range(1, outer_count)]
    relative = [others[(outer_count - 1 - i) % outer_count] for i in range(2 * outer_count - 1)]
    mine = in_order(relative, o, outer_count)
    theirs = swap_core(mine)
    both = jnp.stack([jnp.where(c == 0, mine, theirs), jnp.where(c == 0, theirs, mine)], axis=1)
    return both.reshape((dp_count * seq_count,) + piece.shape)


def scatter_pieces(pieces):
    dp_count, seq_count = axis_sizes()
    outer_count = dp_count // 2
    d, z = lax.axis_index("dp"), lax.axis_index("seq")
    o, c = d // 2, d % 2
    shape = pieces.shape[1:]
    pieces = pieces.reshape((outer_count, 2, seq_count) + shape)
    kept = lax.dynamic_index_in_dim(pieces, c, 1, keepdims=False)
    sent = lax.dynamic_index_in_dim(pieces, 1 - c, 1, keepdims=False)
    now = kept.astype(F32) + swap_core(sent).astype(F32)
    low = now.astype(BF16)
    total = lax.dynamic_index_in_dim(now, o, 0, keepdims=False)
    for k in range(1, outer_count):
        sent = lax.dynamic_index_in_dim(low, (o + k) % outer_count, 0, keepdims=False)
        total = total + turn_outer(sent, k).astype(F32)
    low = total.astype(BF16)
    result = lax.dynamic_index_in_dim(total, z, 0, keepdims=False)
    for k in range(1, seq_count):
        sent = lax.dynamic_index_in_dim(low, (z + k) % seq_count, 0, keepdims=False)
        moved = lax.ppermute(sent, "seq", [(i, (i + k) % seq_count) for i in range(seq_count)])
        result = result + moved.astype(F32)
    return result


def pack_rows(w_qkv, w_out, w_fc1, w_fc2, gains, shifts, fc1_bias):
    rows, width = w_out.shape
    parts = [
        w_qkv.reshape(rows, 3, width).transpose(1, 0, 2).reshape(-1, width),
        w_out,
        w_fc1.reshape(rows, -1, width).transpose(1, 0, 2).reshape(-1, width),
        w_fc2,
    ]
    vector = jnp.concatenate([gains, shifts, fc1_bias])
    used = sum(part.shape[0] for part in parts)
    padded = -(-(used + 1) // 16) * 16
    tail = jnp.pad(vector[None], ((0, padded - used - 1), (0, width - vector.shape[0])))
    return jnp.concatenate(parts + [tail], axis=0)


def unpack_gathered(gathered, rows, lengths):
    count, padded, width = gathered.shape
    slabs = 4
    wide = gathered[:, : 8 * rows].reshape(count, 8, rows, width)
    wide = wide.transpose(1, 0, 2, 3).reshape(8, count * rows, width)
    tall = gathered[:, 8 * rows : 12 * rows].reshape(slabs, width, width)
    weights = jnp.concatenate([wide, tall], axis=0)
    vector = gathered[:, 12 * rows, :].astype(F32)
    parts, start = [], 0
    for length in lengths:
        parts.append(vector[:, start : start + length].reshape(-1, width))
        start += length
    vectors = jnp.concatenate(parts + [jnp.zeros((4, width), F32)], axis=0)
    return weights, vectors


def pack_grads(grad_weights, grad_vectors, rows, lengths):
    width = grad_weights.shape[-1]
    count = width // rows
    wide = grad_weights[:8].reshape(8, count, rows, width).transpose(1, 0, 2, 3)
    wide = wide.reshape(count, 8 * rows, width)
    tall = grad_weights[8:].reshape(count, 4 * rows, width)
    parts, start = [], 0
    for length in lengths:
        used = length * count // width
        parts.append(grad_vectors[start : start + used].reshape(count, length))
        start += used
    vector = jnp.concatenate(parts, axis=1).astype(BF16)
    padded = -(-(12 * rows + 1) // 16) * 16
    tail = jnp.pad(
        vector[:, None], ((0, 0), (0, padded - 12 * rows - 1), (0, width - vector.shape[1]))
    )
    return jnp.concatenate([wide, tall, tail], axis=1)


def unpack_scattered(piece, rows, lengths):
    width = piece.shape[1]
    qkv = piece[: 3 * rows].reshape(3, rows, width).transpose(1, 0, 2).reshape(rows, 3 * width)
    out = piece[3 * rows : 4 * rows]
    fc1 = piece[4 * rows : 8 * rows].reshape(4, rows, width).transpose(1, 0, 2)
    fc1 = fc1.reshape(rows, 4 * width)
    fc2 = piece[8 * rows : 12 * rows]
    parts, start = [], 0
    for length in lengths:
        parts.append(piece[12 * rows, start : start + length])
        start += length
    return [member[None] for member in (qkv, out, fc1, fc2, *parts)]


def image_moves(step):
    dp_count, seq_count = axis_sizes()
    block = seq_count // 4
    moves = []
    for d in range(dp_count):
        for z in range(seq_count):
            micro = (step + z) % 2
            rank = z // 2
            target = (d - d % 2 + rank % 2, (2 * micro + d % 2) * block + rank // 2)
            moves.append(((d, z), target))
    return moves


def to_images(blocks):
    seq_count = lax.axis_size("seq")
    z = lax.axis_index("seq")
    micro = z // (seq_count // 4) // 2
    arrived = []
    for step in range(2):
        sent = jnp.where((step + z) % 2 == 0, blocks[0], blocks[1])
        arrived.append(joint_permute(sent, image_moves(step)))
    low = jnp.where(micro == 0, arrived[0], arrived[1])
    high = jnp.where(micro == 0, arrived[1], arrived[0])
    return jnp.concatenate([low, high], axis=0)


def from_images(rows_own):
    seq_count = lax.axis_size("seq")
    z = lax.axis_index("seq")
    micro = z // (seq_count // 4) // 2
    half = rows_own.shape[0] // 2
    low, high = rows_own[:half], rows_own[half:]
    arrived = []
    for step in range(2):
        sent = jnp.where(micro == step, low, high)
        arrived.append(joint_permute(sent, [(b, a) for a, b in image_moves(step)]))
    return jnp.stack(
        [jnp.where(z % 2 == m, arrived[0], arrived[1]) for m in range(2)]
    )


def group_members():
    block = lax.axis_size("seq") // 4
    return [(turn, flip) for turn in range(block) for flip in range(2)][1:]


def group_moves(turn, flip):
    dp_count, seq_count = axis_sizes()
    block = seq_count // 4
    moves = []
    for d in range(dp_count):
        for z in range(seq_count):
            base = z - z % block
            moves.append(((d ^ flip, base + (z % block + turn) % block), (d, z)))
    return moves


def gather_group(own_rows):
    arrived = [joint_permute(own_rows, group_moves(*member)) for member in group_members()]
    return jnp.concatenate([own_rows] + arrived, axis=0)


def scatter_group(partial, own):
    total = partial[:own].astype(F32)
    for place, member in enumerate(group_members()):
        sent = partial[(place + 1) * own : (place + 2) * own]
        back = [(b, a) for a, b in group_moves(*member)]
        total = total + joint_permute(sent, back).astype(F32)
    return total.astype(BF16)


def slot_mask(lengths, slot_count):
    seq_count = lax.axis_size("seq")
    block = seq_count // 4
    d, z = lax.axis_index("dp"), lax.axis_index("seq")
    c, group = d % 2, z // block
    theirs = swap_core(lengths[:, 0])
    counts = jnp.where(group % 2 == c, lengths[:, 0], theirs)
    counts = jnp.where(group // 2 == 0, counts[0], counts[1])
    places = jnp.arange(slot_count, dtype=jnp.int32)
    parts = []
    for turn, flip in [(0, 0)] + group_members():
        rank = (z % block + turn) % block * 2 + (c ^ flip)
        picked = lax.dynamic_slice_in_dim(counts, 2 * rank, 2, 0)
        parts.append((places[None, :] < picked[:, None]).astype(F32).reshape(-1, 1))
    return jnp.concatenate(parts, axis=0)


def to_section(value, steps):
    return lax.ppermute(value, "section", [(0, 1)] if steps == 1 else [(1, 0)])


def on_device(boundary, lengths, w_qkv, w_out, w_fc1, w_fc2, gains, shifts, fc1_bias):
    section = lax.axis_index("section")
    slot_count = boundary.shape[3]
    own = 2 * slot_count
    rows = w_out.shape[1]
    lens = (gains.shape[1], shifts.shape[1], fc1_bias.shape[1])
    own_start = to_images(boundary[0, :, 0])
    piece = pack_rows(
        w_qkv[0], w_out[0], w_fc1[0], w_fc2[0], gains[0], shifts[0], fc1_bias[0]
    )
    mask = slot_mask(lengths, slot_count)
    weights, vectors = unpack_gathered(gather_pieces(piece), rows, lens)
    all_start = gather_group(own_start)
    (middle,) = run_layer(all_start, mask, weights, vectors, own)
    arrived = gather_group(to_section(middle, 1))
    layer_in = jnp.where(section == 0, all_start, arrived)
    layer_out, partial = run_layer(layer_in, mask, weights, vectors, own, own_start)
    returned = to_section(scatter_group(partial, own), -1)
    grad_out = jnp.where(section == 0, returned, own_start)
    unused, partial, grad_weights, grad_vectors = run_layer(
        layer_in, mask, weights, vectors, own, grad_out, True
    )
    grad_in = scatter_group(partial, own)
    rows_out = from_images(jnp.where(section == 0, grad_in, layer_out))
    summed = scatter_pieces(pack_grads(grad_weights, grad_vectors, rows, lens))
    return (rows_out[None, :, None], *unpack_scattered(summed, rows, lens))


def solution(mesh):
    sharded = P("section", ("dp", "seq"), None)
    vector = P("section", ("dp", "seq"))
    images = P("section", None, "dp", "seq", None)
    grads = (sharded, sharded, sharded, sharded, vector, vector, vector)
    return jax.shard_map(
        on_device,
        mesh=mesh,
        in_specs=(images, P(None, "dp", None), *grads),
        out_specs=(images, *grads),
        check_vma=False,
    )
```

```python
import functools
import math
import jax
import jax.numpy as jnp
from jax import lax
from jax.experimental import pallas as pl
from jax.experimental.pallas import tpu as pltpu
from jax.sharding import PartitionSpec as P

HEADS = 6
norm_eps = 1e-06
F32 = jnp.float32
BF16 = jnp.bfloat16


def mul(left, right, left_dim=1, right_dim=0):
    return lax.dot_general(
        left, right, (((left_dim,), (right_dim,)), ((), ())), preferred_element_type=F32
    )


def total_of(rows):
    return jnp.sum(rows, axis=0, keepdims=True)


def norm_parts(rows_in):
    centre = jnp.mean(rows_in, axis=-1, keepdims=True)
    centred = rows_in - centre
    spread = jnp.mean(centred * centred, axis=-1, keepdims=True)
    scale = lax.rsqrt(spread + norm_eps)
    return centred * scale, scale


def norm_grad(grad, gain, unit, scale):
    scaled = grad * gain
    inner = jnp.mean(scaled * unit, axis=-1, keepdims=True)
    return scale * (scaled - jnp.mean(scaled, axis=-1, keepdims=True) - unit * inner)


def gelu_cdf(hidden):
    return 0.5 + 0.5 * lax.erf(hidden * math.sqrt(0.5))


def row_of(vec_ref, index):
    return vec_ref[index : index + 1, :]


def head_halves(head_dim):
    lane = lax.broadcasted_iota(jnp.int32, (1, 128), 1)
    first_half = (lane < head_dim).astype(BF16)
    return (first_half, 1 - first_half)


def attend_forward(x_ref, mask_ref, wa_ref, vec_ref, refs, mid_ref):
    q_s, k_s, v_s, vt_s, ot_s, kt_s, p_s = refs
    own = q_s.shape[1]
    width = x_ref.shape[1]
    pairs = k_s.shape[0]
    head_dim = width // HEADS
    mask = mask_ref[...]
    masked = x_ref[...].astype(F32) * mask
    unit, _ = norm_parts(masked)
    normed = (unit * row_of(vec_ref, 0) + row_of(vec_ref, 2)).astype(BF16)
    queries = (mul(normed[:own], wa_ref[0]) + row_of(vec_ref, 4)).astype(BF16)
    queries = (queries.astype(F32) * head_dim ** (-0.5)).astype(BF16)
    keys = mul(normed, wa_ref[1]).astype(BF16)
    values = (mul(normed, wa_ref[2]) + row_of(vec_ref, 5)).astype(BF16)
    for j in range(pairs):
        lanes = slice(j * 128, (j + 1) * 128)
        q_s[j] = queries[:, lanes]
        k_s[j] = keys[:, lanes]
        v_s[j] = values[:, lanes]
        vt_s[j] = values[:, lanes].T
        if kt_s is not None:
            kt_s[j] = keys[:, lanes].T
    halves = head_halves(head_dim)

    @pl.loop(0, pairs)
    def _(j):
        bias = (mask_ref[...] - 1.0) * 1e30
        for e in range(2):
            score = mul(k_s[j], q_s[j] * halves[e], 1, 1) + bias
            top = jnp.max(score, axis=0, keepdims=True)
            expo = jnp.exp(score - top)
            probs = (expo * (1.0 / total_of(expo))).astype(BF16)
            rows = slice(e * head_dim, (e + 1) * head_dim)
            ot_s[j, rows, :] = mul(vt_s[j, rows, :], probs).astype(BF16)
            if p_s is not None:
                p_s[2 * j + e] = probs

    attended = jnp.concatenate([ot_s[j].T for j in range(pairs)], axis=1)
    mid_ref[...] = masked[:own] + mul(attended, wa_ref[3]) + row_of(vec_ref, 6)


def feed_forward(mid_ref, mask_ref, w1_ref, w2_ref, vec_ref, c_s, acc_s, h_s, y_ref):
    own, width = mid_ref.shape
    unit, _ = norm_parts(mid_ref[...])
    c_s[...] = (unit * row_of(vec_ref, 1) + row_of(vec_ref, 3)).astype(BF16)
    acc_s[...] = jnp.zeros_like(acc_s)

    @pl.loop(0, w1_ref.shape[0])
    def _(k):
        hidden = mul(c_s[...], w1_ref[k]) + vec_ref[pl.ds(8 + k, 1), :]
        if h_s is not None:
            h_s[k] = hidden
        active = (hidden * gelu_cdf(hidden)).astype(BF16)
        rows = pl.ds(pl.multiple_of(k * width, 128), width)
        acc_s[...] += mul(active, w2_ref[rows, :])

    y_ref[...] = (
        (mid_ref[...] + acc_s[...] + row_of(vec_ref, 7)) * mask_ref[:own, :]
    ).astype(BF16)


def feed_backward(
    mid_ref, mask_ref, dy_ref, w1_ref, w2_ref, vec_ref, c_s, acc_s, h_s, gmid_ref, grads
):
    own, width = mid_ref.shape
    acc_s[...] = jnp.zeros_like(acc_s)
    g1_s, g2_s, gv_ref = grads or (None, None, None)

    @pl.loop(0, w1_ref.shape[0])
    def _(k):
        if h_s is None:
            hidden = mul(c_s[...], w1_ref[k]) + vec_ref[pl.ds(8 + k, 1), :]
        else:
            hidden = h_s[k]
        cdf = gelu_cdf(hidden)
        slope = cdf + hidden * jnp.exp(-0.5 * hidden * hidden) * (1.0 / math.sqrt(2 * math.pi))
        grad_second = (dy_ref[...].astype(F32) * mask_ref[:own, :]).astype(BF16)
        rows = pl.ds(pl.multiple_of(k * width, 128), width)
        grad_hidden = (mul(grad_second, w2_ref[rows, :], 1, 1) * slope).astype(BF16)
        acc_s[...] += mul(grad_hidden, w1_ref[k], 1, 1)
        if grads is not None:
            active = (hidden * cdf).astype(BF16)
            g1_s[k] = mul(c_s[...], grad_hidden, 0, 0).astype(BF16)
            g2_s[rows, :] = mul(active, grad_second, 0, 0).astype(BF16)
            gv_ref[pl.ds(8 + k, 1), :] = total_of(grad_hidden.astype(F32))

    grad_y = dy_ref[...].astype(F32) * mask_ref[:own, :]
    grad_c = acc_s[...]
    unit, scale = norm_parts(mid_ref[...])
    grad_mid = grad_y + norm_grad(grad_c, row_of(vec_ref, 1), unit, scale)
    gmid_ref[...] = grad_mid
    if grads is not None:
        gv_ref[1:2, :] = total_of(grad_c * unit)
        gv_ref[3:4, :] = total_of(grad_c)
        gv_ref[6:7, :] = total_of(grad_mid.astype(BF16).astype(F32))
        gv_ref[7:8, :] = total_of(grad_y.astype(BF16).astype(F32))


def attend_backward(x_ref, mask_ref, wa_ref, vec_ref, kept, scratch, gmid_ref, du_ref, grads):
    q_s, k_s, v_s, ot_s, kt_s, p_s = kept
    do_s, dq_s, dk_s, dv_s = scratch
    own, width = gmid_ref.shape
    pairs = k_s.shape[0]
    head_dim = width // HEADS
    grad_branch = gmid_ref[...].astype(BF16)
    grad_att = mul(grad_branch, wa_ref[3], 1, 1).astype(BF16)
    for j in range(pairs):
        do_s[j] = grad_att[:, j * 128 : (j + 1) * 128]
    if grads is not None:
        ga_s, gv_ref = grads
        for j in range(pairs):
            ga_s[3, j * 128 : (j + 1) * 128, :] = mul(ot_s[j], grad_branch).astype(BF16)
    halves = head_halves(head_dim)

    @pl.loop(0, pairs)
    def _(j):
        grad_k = None
        for e in range(2):
            half_do = do_s[j] * halves[e]
            half_q = q_s[j] * halves[e]
            grad_p = mul(v_s[j], half_do, 1, 1)
            probs_low = p_s[2 * j + e]
            probs = probs_low.astype(F32)
            row_dot = total_of(probs * grad_p)
            grad_s = (probs * (grad_p - row_dot)).astype(BF16)
            rows = slice(e * head_dim, (e + 1) * head_dim)
            dq_s[j, rows, :] = (mul(kt_s[j, rows, :], grad_s) * head_dim ** (-0.5)).astype(BF16)
            part_k = mul(grad_s, half_q)
            part_v = mul(probs_low, half_do)
            grad_k, grad_v = (part_k, part_v) if grad_k is None else (grad_k + part_k, grad_v + part_v)
        dk_s[j] = grad_k.astype(BF16)
        dv_s[j] = grad_v.astype(BF16)

    grad_q = jnp.concatenate([dq_s[j].T for j in range(pairs)], axis=1)
    grad_k = jnp.concatenate([dk_s[j] for j in range(pairs)], axis=1)
    grad_v = jnp.concatenate([dv_s[j] for j in range(pairs)], axis=1)
    mask = mask_ref[...]
    unit, scale = norm_parts(x_ref[...].astype(F32) * mask)
    if grads is not None:
        normed = (unit * row_of(vec_ref, 0) + row_of(vec_ref, 2)).astype(BF16)
        ga_s[0] = mul(normed[:own], grad_q, 0, 0).astype(BF16)
        turned = normed.T
        ga_s[1] = mul(turned, grad_k).astype(BF16)
        ga_s[2] = mul(turned, grad_v).astype(BF16)
        gv_ref[4:5, :] = total_of(grad_q.astype(F32))
        gv_ref[5:6, :] = total_of(grad_v.astype(F32))
    grad_n = mul(grad_k, wa_ref[1], 1, 1) + mul(grad_v, wa_ref[2], 1, 1)
    grad_n = jnp.concatenate([grad_n[:own] + mul(grad_q, wa_ref[0], 1, 1), grad_n[own:]], axis=0)
    if grads is not None:
        gv_ref[0:1, :] = total_of(grad_n * unit)
        gv_ref[2:3, :] = total_of(grad_n)
    grad_u = norm_grad(grad_n, row_of(vec_ref, 0), unit, scale)
    grad_u = jnp.concatenate([grad_u[:own] + gmid_ref[...], grad_u[own:]], axis=0)
    du_ref[...] = (grad_u * mask).astype(BF16)


def piece_groups(place_ref, mine, theirs):
    outer, core, line = place_ref[0], place_ref[1], place_ref[2]
    count = mine[0].shape[0]
    for side, members in enumerate((mine, theirs)):
        for turn, ref in enumerate(members):
            index = lax.rem(outer + (len(mine) - turn), len(mine)) * 2 + (core if side == 0 else 1 - core)
            blocks = [
                ref[lax.rem(line - z + count, count)].astype(F32) for z in range(count)
            ]
            yield index, blocks


def first_kernel(loose, rows, *refs):
    refs = list(refs)
    place_ref, x_ref, mask_ref = refs[:3]
    refs = refs[3:]
    if loose:
        mine, theirs = refs[:loose], refs[loose : 2 * loose]
        refs = refs[2 * loose :]
        mid_ref, wa_ref, vec_ref, *scratch = refs
        width = x_ref.shape[1]
        vector = None
        for index, blocks in piece_groups(place_ref, mine, theirs):
            span = rows * len(blocks)
            start = pl.multiple_of(index * span, 16)
            for s in range(4):
                group = jnp.concatenate([b[s * rows : (s + 1) * rows] for b in blocks], axis=0)
                wa_ref[s, pl.ds(start, span), :] = group.astype(BF16)
            for b in blocks:
                tail = b[4 * rows : 4 * rows + 16]
                vector = tail if vector is None else vector + tail
        vec_ref[...] = vector
    else:
        wa_ref, vec_ref, mid_ref, *scratch = refs
    attend_forward(x_ref, mask_ref, wa_ref, vec_ref, (*scratch, None, None), mid_ref)


def second_kernel(loose, rows, *refs):
    refs = list(refs)
    place_ref, mid_ref, mask_ref, vec_ref = refs[:4]
    refs = refs[4:]
    if loose:
        mine, theirs = refs[:loose], refs[loose : 2 * loose]
        refs = refs[2 * loose :]
        y_ref, w1_ref, w2_ref, c_s, acc_s = refs
        for index, blocks in piece_groups(place_ref, mine, theirs):
            span = rows * len(blocks)
            start = pl.multiple_of(index * span, 16)
            for s in range(4):
                group = jnp.concatenate([b[s * rows : (s + 1) * rows] for b in blocks], axis=0)
                w1_ref[s, pl.ds(start, span), :] = group.astype(BF16)
            group = jnp.concatenate([b[4 * rows : 8 * rows] for b in blocks], axis=0)
            w2_ref[pl.ds(pl.multiple_of(4 * start, 16), 4 * span), :] = group.astype(BF16)
    else:
        w1_ref, w2_ref, y_ref, c_s, acc_s = refs
    feed_forward(mid_ref, mask_ref, w1_ref, w2_ref, vec_ref, c_s, acc_s, None, y_ref)


def middle_kernel(*refs):
    x_ref, mask_ref, dy_ref, wa_ref, w1_ref, w2_ref, vec_ref = refs[:7]
    y_ref, du_ref, mid_ref, q_s, k_s, v_s, ot_s, kt_s, p_s = refs[7:16]
    vt_s, c_s, acc_s, h_s, gmid_s, do_s, dq_s, dk_s, dv_s = refs[16:]
    attend_forward(
        x_ref, mask_ref, wa_ref, vec_ref, (q_s, k_s, v_s, vt_s, ot_s, kt_s, p_s), mid_ref
    )
    feed_forward(mid_ref, mask_ref, w1_ref, w2_ref, vec_ref, c_s, acc_s, h_s, y_ref)
    feed_backward(
        mid_ref, mask_ref, dy_ref, w1_ref, w2_ref, vec_ref, c_s, acc_s, h_s, gmid_s, None
    )
    attend_backward(
        x_ref, mask_ref, wa_ref, vec_ref, (q_s, k_s, v_s, ot_s, kt_s, p_s),
        (do_s, dq_s, dk_s, dv_s), gmid_s, du_ref, None,
    )


def share_out(core, blocks_of, outer_count, start, size, kept_ref, sent_ref):
    for o in range(outer_count):
        even, odd = blocks_of(2 * o), blocks_of(2 * o + 1)
        kept_ref[o, start : start + size, :] = jnp.where(core == 0, even, odd)
        sent_ref[o, start : start + size, :] = jnp.where(core == 0, odd, even)


def feed_grad_kernel(*refs):
    place_ref, mid_ref, mask_ref, dy_ref, w1_ref, w2_ref, vec_ref = refs[:7]
    gmid_ref, gv_ref, kept_ref, sent_ref = refs[7:11]
    c_s, acc_s, g1_s, g2_s = refs[11:]
    outer_count = kept_ref.shape[0]
    span = w1_ref.shape[1] // (2 * outer_count)
    unit, _ = norm_parts(mid_ref[...])
    c_s[...] = (unit * row_of(vec_ref, 1) + row_of(vec_ref, 3)).astype(BF16)
    gv_ref[...] = jnp.zeros_like(gv_ref)
    feed_backward(
        mid_ref, mask_ref, dy_ref, w1_ref, w2_ref, vec_ref, c_s, acc_s, None, gmid_ref,
        (g1_s, g2_s, gv_ref),
    )
    core = place_ref[1]
    for s in range(4):
        share_out(
            core, lambda d: g1_s[s, d * span : (d + 1) * span, :], outer_count,
            s * span, span, kept_ref, sent_ref,
        )
    share_out(
        core, lambda d: g2_s[4 * d * span : 4 * (d + 1) * span, :], outer_count,
        4 * span, 4 * span, kept_ref, sent_ref,
    )


def attend_grad_kernel(*refs):
    place_ref, x_ref, mask_ref, wa_ref, vec_ref = refs[:5]
    q_s, k_s, v_s, ot_s, kt_s, p_s, gmid_ref, gv_in_ref = refs[5:13]
    du_ref, kept_ref, sent_ref = refs[13:16]
    do_s, dq_s, dk_s, dv_s, ga_s, gv_s = refs[16:]
    outer_count = kept_ref.shape[0]
    span = wa_ref.shape[1] // (2 * outer_count)
    gv_s[...] = gv_in_ref[...]
    attend_backward(
        x_ref, mask_ref, wa_ref, vec_ref, (q_s, k_s, v_s, ot_s, kt_s, p_s),
        (do_s, dq_s, dk_s, dv_s), gmid_ref, du_ref, (ga_s, gv_s),
    )
    core = place_ref[1]
    for s in range(4):
        share_out(
            core, lambda d: ga_s[s, d * span : (d + 1) * span, :], outer_count,
            s * span, span, kept_ref, sent_ref,
        )
    tail = gv_s[...].astype(BF16)
    for o in range(outer_count):
        kept_ref[o, 4 * span :, :] = tail
        sent_ref[o, 4 * span :, :] = tail


def call(kernel, operands, shapes, scratch, flops, scalars=0):
    whole = pl.BlockSpec(memory_space=pltpu.VMEM)
    scalar = pl.BlockSpec(memory_space=pltpu.SMEM)
    return pl.pallas_call(
        kernel,
        out_shape=[jax.ShapeDtypeStruct(*shape) for shape in shapes],
        in_specs=[scalar] * scalars + [whole] * (len(operands) - scalars),
        out_specs=[whole] * len(shapes),
        scratch_shapes=[pltpu.VMEM(*shape) for shape in scratch],
        compiler_params=pltpu.CompilerParams(vmem_limit_bytes=VMEM_LIMIT),
        cost_estimate=pl.CostEstimate(flops=flops, bytes_accessed=4 * 10**6, transcendentals=10**6),
    )(*operands)


VMEM_LIMIT = 32 * 1024 * 1024


def axis_sizes():
    return lax.axis_size("dp"), lax.axis_size("seq")


def swap_core(value):
    return lax.ppermute(value, "dp", [(d, d ^ 1) for d in range(lax.axis_size("dp"))])


def turn_outer(value, steps):
    count = lax.axis_size("dp")
    return lax.ppermute(value, "dp", [(d, (d + 2 * steps) % count) for d in range(count)])


def turn_line(value, steps):
    count = lax.axis_size("seq")
    return lax.ppermute(value, "seq", [(z, (z + steps) % count) for z in range(count)])


def joint_permute(value, moves):
    seq_count = lax.axis_size("seq")
    pairs = [(a[0] * seq_count + a[1], b[0] * seq_count + b[1]) for a, b in moves]
    return lax.ppermute(value, ("dp", "seq"), pairs)


def gather_line(piece):
    return [piece] + [turn_line(piece, k) for k in range(1, lax.axis_size("seq"))]


def gather_rest(line):
    outer_count = lax.axis_size("dp") // 2
    stacked = jnp.stack(line)
    mine = [stacked] + [turn_outer(stacked, k) for k in range(1, outer_count)]
    return mine, [swap_core(member) for member in mine]


def assemble(mine, theirs):
    outer_count, seq_count = len(mine), lax.axis_size("seq")
    d, z = lax.axis_index("dp"), lax.axis_index("seq")
    o, c = d // 2, d % 2
    turned = jnp.stack([jnp.stack(mine), jnp.stack(theirs)])
    sides = (jnp.arange(2) + c) % 2
    outers = (o - jnp.arange(outer_count)) % outer_count
    lines = (z - jnp.arange(seq_count)) % seq_count
    ordered = turned[sides][:, outers][:, :, lines]
    return ordered.transpose(1, 0, 2, 3, 4).reshape((-1,) + mine[0].shape[1:])


def scatter_sum(kept, sent, take):
    d, z = lax.axis_index("dp"), lax.axis_index("seq")
    outer_count, seq_count = lax.axis_size("dp") // 2, lax.axis_size("seq")
    o = d // 2
    came = swap_core(sent)

    def both(index):
        return lax.dynamic_index_in_dim(kept, index, 0, keepdims=False).astype(
            F32
        ) + lax.dynamic_index_in_dim(came, index, 0, keepdims=False).astype(F32)

    total = both(o)
    for k in range(1, outer_count):
        total = total + turn_outer(both((o + k) % outer_count).astype(BF16), k).astype(F32)
    low = total.astype(BF16)
    result = take(total, z)
    for k in range(1, seq_count):
        result = result + turn_line(take(low, (z + k) % seq_count), k).astype(F32)
    return result


def image_moves(step):
    dp_count, seq_count = axis_sizes()
    block = seq_count // 4
    moves = []
    for d in range(dp_count):
        for z in range(seq_count):
            micro = (step + z) % 2
            rank = z // 2
            target = (d - d % 2 + rank % 2, (2 * micro + d % 2) * block + rank // 2)
            moves.append(((d, z), target))
    return moves


def to_images(blocks):
    z = lax.axis_index("seq")
    micro = z // (lax.axis_size("seq") // 4) // 2
    arrived = []
    for step in range(2):
        sent = jnp.where((step + z) % 2 == 0, blocks[0], blocks[1])
        arrived.append(joint_permute(sent, image_moves(step)))
    low = jnp.where(micro == 0, arrived[0], arrived[1])
    high = jnp.where(micro == 0, arrived[1], arrived[0])
    return jnp.concatenate([low, high], axis=0)


def from_images(rows_own):
    z = lax.axis_index("seq")
    micro = z // (lax.axis_size("seq") // 4) // 2
    half = rows_own.shape[0] // 2
    low, high = rows_own[:half], rows_own[half:]
    arrived = []
    for step in range(2):
        sent = jnp.where(micro == step, low, high)
        arrived.append(joint_permute(sent, [(b, a) for a, b in image_moves(step)]))
    return jnp.stack([jnp.where(z % 2 == m, arrived[0], arrived[1]) for m in range(2)])


def group_members():
    block = lax.axis_size("seq") // 4
    return [(turn, flip) for turn in range(block) for flip in range(2)][1:]


def group_moves(turn, flip):
    dp_count, seq_count = axis_sizes()
    block = seq_count // 4
    moves = []
    for d in range(dp_count):
        for z in range(seq_count):
            base = z - z % block
            moves.append(((d ^ flip, base + (z % block + turn) % block), (d, z)))
    return moves


def gather_group(own_rows):
    arrived = [joint_permute(own_rows, group_moves(*member)) for member in group_members()]
    return jnp.concatenate([own_rows] + arrived, axis=0)


def scatter_group(partial, own):
    total = partial[:own].astype(F32)
    for place, member in enumerate(group_members()):
        sent = partial[(place + 1) * own : (place + 2) * own]
        back = [(b, a) for a, b in group_moves(*member)]
        total = total + joint_permute(sent, back).astype(F32)
    return total.astype(BF16)


def slot_mask(lengths, slot_count):
    block = lax.axis_size("seq") // 4
    d, z = lax.axis_index("dp"), lax.axis_index("seq")
    c, group = d % 2, z // block
    theirs = swap_core(lengths[:, 0])
    counts = jnp.where(group % 2 == c, lengths[:, 0], theirs)
    counts = jnp.where(group // 2 == 0, counts[0], counts[1])
    places = jnp.arange(slot_count, dtype=jnp.int32)
    parts = []
    for turn, flip in [(0, 0)] + group_members():
        rank = (z % block + turn) % block * 2 + (c ^ flip)
        picked = lax.dynamic_slice_in_dim(counts, 2 * rank, 2, 0)
        parts.append((places[None, :] < picked[:, None]).astype(F32).reshape(-1, 1))
    return jnp.concatenate(parts, axis=0)


def to_section(value, steps):
    return lax.ppermute(value, "section", [(0, 1)] if steps == 1 else [(1, 0)])


def vector_slots(members, width):
    index = lax.axis_index("dp") * lax.axis_size("seq") + lax.axis_index("seq")
    count = lax.axis_size("dp") * lax.axis_size("seq")
    parts = []
    for member in members:
        length = member.shape[0]
        spread = jnp.zeros((count * length,), BF16)
        spread = lax.dynamic_update_slice_in_dim(spread, member, index * length, 0)
        parts.append(spread.reshape(-1, width))
    parts.append(jnp.zeros((4, width), BF16))
    return jnp.concatenate(parts, axis=0)


def own_slots(vectors, lengths):
    index = lax.axis_index("dp") * lax.axis_size("seq") + lax.axis_index("seq")
    count = lax.axis_size("dp") * lax.axis_size("seq")
    parts, start = [], 0
    for length in lengths:
        used = length * count // vectors.shape[1]
        flat = vectors[start : start + used].reshape(-1)
        parts.append(lax.dynamic_slice_in_dim(flat, index * length, length, 0))
        start += used
    return parts


def by_column(member, width):
    rows = member.shape[0]
    return member.reshape(rows, -1, width).transpose(1, 0, 2).reshape(-1, width)


def from_columns(block, rows):
    width = block.shape[1]
    return block.reshape(-1, rows, width).transpose(1, 0, 2).reshape(rows, -1)


def on_device(boundary, lengths, w_qkv, w_out, w_fc1, w_fc2, gains, shifts, fc1_bias):
    section = lax.axis_index("section")
    dp_count, seq_count = axis_sizes()
    outer_count = dp_count // 2
    d = lax.axis_index("dp")
    place = jnp.stack([d // 2, d % 2, lax.axis_index("seq")]).astype(jnp.int32)
    slot_count = boundary.shape[3]
    own = 2 * slot_count
    total = lengths.shape[2] * slot_count
    rows, width = w_out.shape[1:]
    hidden = rows * 4 * dp_count * seq_count
    pairs = width // 128
    span = width // dp_count
    lens = (gains.shape[1], shifts.shape[1], fc1_bias.shape[1])
    piece_a = jnp.concatenate(
        [by_column(w_qkv[0], width), w_out[0], vector_slots((gains[0], shifts[0], fc1_bias[0]), width)]
    )
    piece_b = jnp.concatenate([by_column(w_fc1[0], width), w_fc2[0]])
    line_a = gather_line(piece_a)
    own_start = to_images(boundary[0, :, 0])
    line_b = gather_line(piece_b)
    mask = slot_mask(lengths, slot_count)
    all_start = gather_group(own_start)
    mine_a, theirs_a = gather_rest(line_a)
    mine_b, theirs_b = gather_rest(line_b)
    loose = outer_count if rows % 8 == 0 else 0

    w_shape = ((4, width, width), BF16)
    tall_shape = ((hidden, width), BF16)
    vec_shape = ((16, width), F32)
    mid_shape = ((own, width), F32)
    low_shape = ((own, width), BF16)
    all_shape = ((total, width), BF16)
    q_shape = ((pairs, own, 128), BF16)
    k_shape = ((pairs, total, 128), BF16)
    qt_shape = ((pairs, 128, own), BF16)
    kt_shape = ((pairs, 128, total), BF16)
    p_shape = ((HEADS, total, own), BF16)
    h_shape = ((4, own, width), F32)
    shared_b = ((outer_count, 8 * span, width), BF16)
    shared_a = ((outer_count, 4 * span + 16, width), BF16)

    head_scratch = [q_shape, k_shape, k_shape, kt_shape, qt_shape]
    if loose:
        middle, w_a, vectors = call(
            functools.partial(first_kernel, loose, rows),
            [place, all_start, mask, *mine_a, *theirs_a],
            [mid_shape, w_shape, vec_shape], head_scratch, 10**9, 1,
        )
        first_out, w_1, w_2 = call(
            functools.partial(second_kernel, loose, rows),
            [place, middle, mask, vectors, *mine_b, *theirs_b],
            [low_shape, w_shape, tall_shape], [low_shape, mid_shape], 10**9, 1,
        )
    else:
        ordered = assemble(mine_a, theirs_a)
        w_a = ordered[:, : 4 * rows].reshape(-1, 4, rows, width).transpose(1, 0, 2, 3)
        w_a = w_a.reshape(4, width, width)
        vectors = jnp.sum(ordered[:, 4 * rows :].astype(F32), axis=0)
        ordered = assemble(mine_b, theirs_b)
        w_1 = ordered[:, : 4 * rows].reshape(-1, 4, rows, width).transpose(1, 0, 2, 3)
        w_1 = w_1.reshape(4, width, width)
        w_2 = ordered[:, 4 * rows :].reshape(hidden, width)
        (middle,) = call(
            functools.partial(first_kernel, loose, rows),
            [place, all_start, mask, w_a, vectors], [mid_shape], head_scratch, 10**9, 1,
        )
        (first_out,) = call(
            functools.partial(second_kernel, loose, rows),
            [place, middle, mask, vectors, w_1, w_2],
            [low_shape], [low_shape, mid_shape], 10**9, 1,
        )
    arrived = gather_group(to_section(first_out, 1))
    layer_in = jnp.where(section == 0, all_start, arrived)
    grad_scratch = [q_shape, qt_shape, k_shape, k_shape]
    layer_out, partial, middle, *kept = call(
        middle_kernel,
        [layer_in, mask, own_start, w_a, w_1, w_2, vectors],
        [low_shape, all_shape, mid_shape, q_shape, k_shape, k_shape, qt_shape, kt_shape, p_shape],
        [kt_shape, low_shape, mid_shape, h_shape, mid_shape, *grad_scratch], 4 * 10**9,
    )
    returned = to_section(scatter_group(partial, own), -1)
    grad_out = jnp.where(section == 0, returned, own_start)
    grad_mid, grad_vectors, kept_b, sent_b = call(
        feed_grad_kernel,
        [place, middle, mask, grad_out, w_1, w_2, vectors],
        [mid_shape, vec_shape, shared_b, shared_b],
        [low_shape, mid_shape, w_shape, tall_shape], 2 * 10**9, 1,
    )
    partial, kept_a, sent_a = call(
        attend_grad_kernel,
        [place, layer_in, mask, w_a, vectors, *kept, grad_mid, grad_vectors],
        [all_shape, shared_a, shared_a],
        [*grad_scratch, w_shape, vec_shape], 2 * 10**9, 1,
    )

    def line_block(wide, index):
        split = wide.reshape(4, seq_count, rows, width)
        return lax.dynamic_index_in_dim(split, index, 1, keepdims=False).reshape(-1, width)

    def take_b(value, index):
        tall = value[4 * span :].reshape(seq_count, 4 * rows, width)
        tall = lax.dynamic_index_in_dim(tall, index, 0, keepdims=False)
        return jnp.concatenate([line_block(value[: 4 * span], index), tall])

    def take_a(value, index):
        return jnp.concatenate([line_block(value[: 4 * span], index), value[4 * span :]])

    summed_b = scatter_sum(kept_b, sent_b, take_b)
    grad_in = scatter_group(partial, own)
    rows_out = from_images(jnp.where(section == 0, grad_in, layer_out))
    summed_a = scatter_sum(kept_a, sent_a, take_a)
    grads = (
        from_columns(summed_a[: 3 * rows], rows),
        summed_a[3 * rows : 4 * rows],
        from_columns(summed_b[: 4 * rows], rows),
        summed_b[4 * rows :],
        *own_slots(summed_a[4 * rows :], lens),
    )
    return (rows_out[None, :, None], *[member[None] for member in grads])


def solution(mesh):
    sharded = P("section", ("dp", "seq"), None)
    vector = P("section", ("dp", "seq"))
    images = P("section", None, "dp", "seq", None)
    grads = (sharded, sharded, sharded, sharded, vector, vector, vector)
    return jax.shard_map(
        on_device,
        mesh=mesh,
        in_specs=(images, P(None, "dp", None), *grads),
        out_specs=(images, *grads),
        check_vma=False,
    )
```

```python
import functools
import math
import jax
import jax.numpy as jnp
from jax import lax
from jax.experimental import pallas as pl
from jax.experimental.pallas import tpu as pltpu
from jax.sharding import PartitionSpec as P

HEADS = 6
norm_eps = 1e-06
F32 = jnp.float32
BF16 = jnp.bfloat16


def mul(left, right, left_dim=1, right_dim=0):
    return lax.dot_general(
        left, right, (((left_dim,), (right_dim,)), ((), ())), preferred_element_type=F32
    )


def total_of(rows):
    return jnp.sum(rows, axis=0, keepdims=True)


def norm_parts(rows_in):
    centre = jnp.mean(rows_in, axis=-1, keepdims=True)
    centred = rows_in - centre
    spread = jnp.mean(centred * centred, axis=-1, keepdims=True)
    scale = lax.rsqrt(spread + norm_eps)
    return centred * scale, scale


def norm_grad(grad, gain, unit, scale):
    scaled = grad * gain
    inner = jnp.mean(scaled * unit, axis=-1, keepdims=True)
    return scale * (scaled - jnp.mean(scaled, axis=-1, keepdims=True) - unit * inner)


def gelu_cdf(hidden):
    return 0.5 + 0.5 * lax.erf(hidden * math.sqrt(0.5))


def row_of(vec_ref, index):
    return vec_ref[index : index + 1, :]


def head_halves(head_dim):
    lane = lax.broadcasted_iota(jnp.int32, (1, 128), 1)
    first_half = (lane < head_dim).astype(BF16)
    return (first_half, 1 - first_half)


def attend_forward(x_ref, mask_ref, wa_ref, vec_ref, refs, mid_ref):
    q_s, k_s, v_s, vt_s, ot_s, kt_s, p_s = refs
    own = q_s.shape[1]
    width = x_ref.shape[1]
    pairs = k_s.shape[0]
    head_dim = width // HEADS
    mask = mask_ref[:, :1]
    masked = x_ref[...].astype(F32) * mask
    unit, _ = norm_parts(masked)
    normed = (unit * row_of(vec_ref, 0) + row_of(vec_ref, 2)).astype(BF16)
    queries = (mul(normed[:own], wa_ref[0]) + row_of(vec_ref, 4)).astype(BF16)
    queries = (queries.astype(F32) * head_dim ** (-0.5)).astype(BF16)
    keys = mul(normed, wa_ref[1]).astype(BF16)
    values = (mul(normed, wa_ref[2]) + row_of(vec_ref, 5)).astype(BF16)
    for j in range(pairs):
        lanes = slice(j * 128, (j + 1) * 128)
        q_s[j] = queries[:, lanes]
        k_s[j] = keys[:, lanes]
        v_s[j] = values[:, lanes]
        vt_s[j] = values[:, lanes].T
        if kt_s is not None:
            kt_s[j] = keys[:, lanes].T
    halves = head_halves(head_dim)

    for j in range(pairs):
        bias = (mask_ref[:, :1] - 1.0) * 1e30
        for e in range(2):
            score = mul(k_s[j], q_s[j] * halves[e], 1, 1) + bias
            top = jnp.max(score, axis=0, keepdims=True)
            expo = jnp.exp(score - top)
            probs = (expo * (1.0 / total_of(expo))).astype(BF16)
            rows = slice(e * head_dim, (e + 1) * head_dim)
            ot_s[j, rows, :] = mul(vt_s[j, rows, :], probs).astype(BF16)
            if p_s is not None:
                p_s[2 * j + e] = probs

    attended = jnp.concatenate([ot_s[j].T for j in range(pairs)], axis=1)
    mid_ref[...] = masked[:own] + mul(attended, wa_ref[3]) + row_of(vec_ref, 6)


def feed_forward(mid_ref, mask_ref, w1_ref, w2_ref, vec_ref, c_s, acc_s, h_s, y_ref):
    own, width = mid_ref.shape
    unit, _ = norm_parts(mid_ref[...])
    c_s[...] = (unit * row_of(vec_ref, 1) + row_of(vec_ref, 3)).astype(BF16)
    acc_s[...] = jnp.zeros_like(acc_s)

    @pl.loop(0, w1_ref.shape[0])
    def _(k):
        hidden = mul(c_s[...], w1_ref[k]) + vec_ref[pl.ds(8 + k, 1), :]
        if h_s is not None:
            h_s[k] = hidden
        active = (hidden * gelu_cdf(hidden)).astype(BF16)
        rows = pl.ds(pl.multiple_of(k * width, 128), width)
        acc_s[...] += mul(active, w2_ref[rows, :])

    y_ref[...] = (
        (mid_ref[...] + acc_s[...] + row_of(vec_ref, 7)) * mask_ref[:own, :1]
    ).astype(BF16)


def feed_backward(
    mid_ref, mask_ref, dy_ref, w1_ref, w2_ref, vec_ref, c_s, acc_s, h_s, gmid_ref, grads
):
    own, width = mid_ref.shape
    acc_s[...] = jnp.zeros_like(acc_s)
    g1_s, g2_s, gv_ref = grads or (None, None, None)

    @pl.loop(0, w1_ref.shape[0])
    def _(k):
        if h_s is None:
            hidden = mul(c_s[...], w1_ref[k]) + vec_ref[pl.ds(8 + k, 1), :]
        else:
            hidden = h_s[k]
        cdf = gelu_cdf(hidden)
        slope = cdf + hidden * jnp.exp(-0.5 * hidden * hidden) * (1.0 / math.sqrt(2 * math.pi))
        grad_second = (dy_ref[...].astype(F32) * mask_ref[:own, :1]).astype(BF16)
        rows = pl.ds(pl.multiple_of(k * width, 128), width)
        grad_hidden = (mul(grad_second, w2_ref[rows, :], 1, 1) * slope).astype(BF16)
        acc_s[...] += mul(grad_hidden, w1_ref[k], 1, 1)
        if grads is not None:
            active = (hidden * cdf).astype(BF16)
            g1_s[k] = mul(c_s[...], grad_hidden, 0, 0).astype(BF16)
            g2_s[rows, :] = mul(active, grad_second, 0, 0).astype(BF16)
            gv_ref[pl.ds(8 + k, 1), :] = total_of(grad_hidden.astype(F32))

    grad_y = dy_ref[...].astype(F32) * mask_ref[:own, :1]
    grad_c = acc_s[...]
    unit, scale = norm_parts(mid_ref[...])
    grad_mid = grad_y + norm_grad(grad_c, row_of(vec_ref, 1), unit, scale)
    gmid_ref[...] = grad_mid
    if grads is not None:
        gv_ref[1:2, :] = total_of(grad_c * unit)
        gv_ref[3:4, :] = total_of(grad_c)
        gv_ref[6:7, :] = total_of(grad_mid.astype(BF16).astype(F32))
        gv_ref[7:8, :] = total_of(grad_y.astype(BF16).astype(F32))


def attend_backward(x_ref, mask_ref, wa_ref, vec_ref, kept, scratch, gmid_ref, du_ref, grads):
    q_s, k_s, v_s, ot_s, kt_s, p_s = kept
    do_s, dq_s, dk_s, dv_s = scratch
    own, width = gmid_ref.shape
    pairs = do_s.shape[0]
    head_dim = width // HEADS
    grad_branch = gmid_ref[...].astype(BF16)
    grad_att = mul(grad_branch, wa_ref[3], 1, 1).astype(BF16)
    for j in range(pairs):
        do_s[j] = grad_att[:, j * 128 : (j + 1) * 128]
    if grads is not None:
        ga_s, gv_ref = grads
        for j in range(pairs):
            ga_s[3, j * 128 : (j + 1) * 128, :] = mul(ot_s[j], grad_branch).astype(BF16)
    halves = head_halves(head_dim)

    for j in range(pairs):
        grad_k = None
        for e in range(2):
            half_do = do_s[j] * halves[e]
            half_q = q_s[j] * halves[e]
            grad_p = mul(v_s[j], half_do, 1, 1)
            probs_low = p_s[2 * j + e]
            probs = probs_low.astype(F32)
            row_dot = total_of(probs * grad_p)
            grad_s = (probs * (grad_p - row_dot)).astype(BF16)
            rows = slice(e * head_dim, (e + 1) * head_dim)
            dq_s[j, rows, :] = (mul(kt_s[j, rows, :], grad_s) * head_dim ** (-0.5)).astype(BF16)
            part_k = mul(grad_s, half_q)
            part_v = mul(probs_low, half_do)
            grad_k, grad_v = (part_k, part_v) if grad_k is None else (grad_k + part_k, grad_v + part_v)
        dk_s[j] = grad_k.astype(BF16)
        dv_s[j] = grad_v.astype(BF16)

    grad_q = jnp.concatenate([dq_s[j].T for j in range(pairs)], axis=1)
    grad_k = jnp.concatenate([dk_s[j] for j in range(pairs)], axis=1)
    grad_v = jnp.concatenate([dv_s[j] for j in range(pairs)], axis=1)
    mask = mask_ref[:, :1]
    unit, scale = norm_parts(x_ref[...].astype(F32) * mask)
    if grads is not None:
        normed = (unit * row_of(vec_ref, 0) + row_of(vec_ref, 2)).astype(BF16)
        ga_s[0] = mul(normed[:own], grad_q, 0, 0).astype(BF16)
        turned = normed.T
        ga_s[1] = mul(turned, grad_k).astype(BF16)
        ga_s[2] = mul(turned, grad_v).astype(BF16)
        gv_ref[4:5, :] = total_of(grad_q.astype(F32))
        gv_ref[5:6, :] = total_of(grad_v.astype(F32))
    grad_n = mul(grad_k, wa_ref[1], 1, 1) + mul(grad_v, wa_ref[2], 1, 1)
    grad_n = jnp.concatenate([grad_n[:own] + mul(grad_q, wa_ref[0], 1, 1), grad_n[own:]], axis=0)
    if grads is not None:
        gv_ref[0:1, :] = total_of(grad_n * unit)
        gv_ref[2:3, :] = total_of(grad_n)
    grad_u = norm_grad(grad_n, row_of(vec_ref, 0), unit, scale)
    grad_u = jnp.concatenate([grad_u[:own] + gmid_ref[...], grad_u[own:]], axis=0)
    du_ref[...] = (grad_u * mask).astype(BF16)


def pack_kernel(place_ref, qkv_ref, out_ref, fc1_ref, fc2_ref, gains_ref, shifts_ref, bias_ref, a_ref, b_ref):
    rows, width = out_ref.shape
    index = place_ref[3]

    def columns(ref, count):
        wide = ref[...].astype(F32)
        return [wide[:, s * width : (s + 1) * width] for s in range(count)]

    lane = lax.broadcasted_iota(jnp.int32, (1, width), 1)
    row = lax.broadcasted_iota(jnp.int32, (16, width), 0)
    tail, base = jnp.zeros((16, width), F32), 0
    for ref, used in ((gains_ref, 2), (shifts_ref, 6), (bias_ref, 4)):
        length = ref.shape[1]
        start = index * length
        first, offset = start // width, lax.rem(start, width)
        spread = jnp.concatenate(
            [ref[...].astype(F32), jnp.zeros((1, width - length), F32)], axis=1
        )
        spread = pltpu.roll(jnp.broadcast_to(spread, (8, width)), offset, 1)[:1]
        target = base + first + jnp.where(lane < offset, 1, 0)
        tail = tail + jnp.where(row == target, spread, 0.0)
        base += used
    blocks = columns(qkv_ref, 3) + [out_ref[...].astype(F32), tail]
    a_ref[...] = jnp.concatenate(blocks, axis=0).astype(BF16)
    blocks = columns(fc1_ref, 4) + [fc2_ref[...].astype(F32)]
    b_ref[...] = jnp.concatenate(blocks, axis=0).astype(BF16)


def piece_groups(place_ref, mine, theirs):
    outer, core, line = place_ref[0], place_ref[1], place_ref[2]
    count = mine[0].shape[0]
    for side, members in enumerate((mine, theirs)):
        for turn, ref in enumerate(members):
            index = lax.rem(outer + (len(mine) - turn), len(mine)) * 2 + (core if side == 0 else 1 - core)
            blocks = [
                ref[lax.rem(line - z + count, count)].astype(F32) for z in range(count)
            ]
            yield index, blocks


def first_kernel(loose, rows, ins, outs, scratch):
    place_ref, x_ref, mask_ref = ins[:3]
    if loose:
        mine, theirs = ins[3 : 3 + loose], ins[3 + loose :]
        mid_ref, wa_out, vec_out = outs
        wa_ref, vec_ref = wa_out, vec_out
        vector = None
        for index, blocks in piece_groups(place_ref, mine, theirs):
            span = rows * len(blocks)
            start = pl.multiple_of(index * span, 16)
            for s in range(4):
                group = jnp.concatenate([b[s * rows : (s + 1) * rows] for b in blocks], axis=0)
                wa_ref[s, pl.ds(start, span), :] = group.astype(BF16)
            for b in blocks:
                tail = b[4 * rows : 4 * rows + 16]
                vector = tail if vector is None else vector + tail
        vec_ref[...] = vector
    else:
        wa_ref, vec_ref = (member for member in ins[3:])
        (mid_ref,) = outs
    attend_forward(x_ref, mask_ref, wa_ref, vec_ref, (*scratch, None, None), mid_ref)


def second_kernel(loose, rows, ins, outs, scratch):
    place_ref, mid_ref = ins[:2]
    c_s, acc_s = scratch
    if loose:
        mine, theirs = ins[4 : 4 + loose], ins[4 + loose :]
        y_ref, w1_out, w2_out = outs
        w1_ref, w2_ref = w1_out, w2_out
        for index, blocks in piece_groups(place_ref, mine, theirs):
            span = rows * len(blocks)
            start = pl.multiple_of(index * span, 16)
            for s in range(4):
                group = jnp.concatenate([b[s * rows : (s + 1) * rows] for b in blocks], axis=0)
                w1_ref[s, pl.ds(start, span), :] = group.astype(BF16)
            group = jnp.concatenate([b[4 * rows : 8 * rows] for b in blocks], axis=0)
            w2_ref[pl.ds(pl.multiple_of(4 * start, 16), 4 * span), :] = group.astype(BF16)
    else:
        w1_ref, w2_ref = (member for member in ins[4:])
        (y_ref,) = outs
    mask_ref, vec_ref = ins[2], ins[3]
    feed_forward(mid_ref, mask_ref, w1_ref, w2_ref, vec_ref, c_s, acc_s, None, y_ref)


def middle_kernel(ins, outs, scratch):
    x_ref, mask_in, vec_in, wa_in, w1_in, w2_in, dy_in = ins
    du_ref, y_out, mid_out, *kept = outs
    vt_s, c_s, acc_s, h_s, gmid_s, do_s, dq_s, dk_s, dv_s = scratch
    q_s, k_s, v_s, ot_s, kt_s, p_s = [member for member in kept]
    mid_ref, y_ref = mid_out, y_out
    mask_ref, vec_ref, wa_ref = mask_in, vec_in, wa_in
    attend_forward(
        x_ref, mask_ref, wa_ref, vec_ref, (q_s, k_s, v_s, vt_s, ot_s, kt_s, p_s), mid_ref
    )
    w1_ref, w2_ref = w1_in, w2_in
    feed_forward(mid_ref, mask_ref, w1_ref, w2_ref, vec_ref, c_s, acc_s, h_s, y_ref)
    feed_backward(
        mid_ref, mask_ref, dy_in, w1_ref, w2_ref, vec_ref, c_s, acc_s, h_s, gmid_s, None
    )
    attend_backward(
        x_ref, mask_ref, wa_ref, vec_ref, (q_s, k_s, v_s, ot_s, kt_s, p_s),
        (do_s, dq_s, dk_s, dv_s), gmid_s, du_ref, None,
    )


def share_out(core, blocks_of, outer_count, start, size, kept_ref, sent_ref):
    for o in range(outer_count):
        even, odd = blocks_of(2 * o), blocks_of(2 * o + 1)
        kept_ref[o, start : start + size, :] = jnp.where(core == 0, even, odd)
        sent_ref[o, start : start + size, :] = jnp.where(core == 0, odd, even)


def feed_grad_kernel(ins, outs, scratch):
    place_ref, dy_ref, mid_in, vec_in, mask_in, w1_in, w2_in = ins
    kept_ref, sent_ref, gmid_out, gv_out = outs
    c_s, acc_s, g1_s, g2_s = scratch
    gmid_ref, gv_ref = gmid_out, gv_out
    mid_ref, vec_ref = mid_in, vec_in
    unit, _ = norm_parts(mid_ref[...])
    c_s[...] = (unit * row_of(vec_ref, 1) + row_of(vec_ref, 3)).astype(BF16)
    gv_ref[...] = jnp.zeros_like(gv_ref)
    mask_ref, w1_ref, w2_ref = mask_in, w1_in, w2_in
    outer_count = kept_ref.shape[0]
    span = w1_ref.shape[1] // (2 * outer_count)
    feed_backward(
        mid_ref, mask_ref, dy_ref, w1_ref, w2_ref, vec_ref, c_s, acc_s, None, gmid_ref,
        (g1_s, g2_s, gv_ref),
    )
    core = place_ref[1]
    for s in range(4):
        share_out(
            core, lambda d: g1_s[s, d * span : (d + 1) * span, :], outer_count,
            s * span, span, kept_ref, sent_ref,
        )
    share_out(
        core, lambda d: g2_s[4 * d * span : 4 * (d + 1) * span, :], outer_count,
        4 * span, 4 * span, kept_ref, sent_ref,
    )


def attend_grad_kernel(ins, outs, scratch):
    place_ref, gmid_in, wa_in, ot_in, v_in, q_in, kt_in, p_in, k_in, x_in, mask_in, vec_in, gv_in = ins
    du_ref, kept_ref, sent_ref = outs
    do_s, dq_s, dk_s, dv_s, ga_s, gv_s = scratch
    gmid_ref, wa_ref, ot_s = gmid_in, wa_in, ot_in
    outer_count = kept_ref.shape[0]
    span = wa_ref.shape[1] // (2 * outer_count)
    gv_s[...] = gv_in[...]
    attend_backward(
        x_in, mask_in, wa_ref, vec_in, (q_in, k_in, v_in, ot_s, kt_in, p_in),
        (do_s, dq_s, dk_s, dv_s), gmid_ref, du_ref, (ga_s, gv_s),
    )
    core = place_ref[1]
    for s in range(4):
        share_out(
            core, lambda d: ga_s[s, d * span : (d + 1) * span, :], outer_count,
            s * span, span, kept_ref, sent_ref,
        )
    tail = gv_s[...].astype(BF16)
    for o in range(outer_count):
        kept_ref[o, 4 * span :, :] = tail
        sent_ref[o, 4 * span :, :] = tail


def call(kernel, operands, results, scratch, flops, after=()):
    space = {"s": pltpu.SMEM, "v": pltpu.VMEM}

    def body(*refs):
        refs = list(refs[len(after) :])
        given, refs = refs[: len(operands)], refs[len(operands) :]
        kernel(given, refs[: len(results)], refs[len(results) :])

    return pl.pallas_call(
        body,
        out_shape=[jax.ShapeDtypeStruct(*result) for result in results],
        in_specs=[pl.BlockSpec(memory_space=pl.ANY)] * len(after)
        + [pl.BlockSpec(memory_space=space[kind]) for kind, _ in operands],
        out_specs=[pl.BlockSpec(memory_space=pltpu.VMEM)] * len(results),
        scratch_shapes=[pltpu.VMEM(*shape) for shape in scratch],
        compiler_params=pltpu.CompilerParams(vmem_limit_bytes=VMEM_LIMIT),
        cost_estimate=pl.CostEstimate(flops=flops, bytes_accessed=4 * 10**6, transcendentals=10**6),
    )(*after, *[array for _, array in operands])


def call_whole(kernel, operands, shapes):
    def block(shape):
        return pl.BlockSpec(shape, lambda i: (0,) * len(shape))

    return pl.pallas_call(
        kernel,
        grid=(1,),
        out_shape=[jax.ShapeDtypeStruct(*shape) for shape in shapes],
        in_specs=[pl.BlockSpec(memory_space=pltpu.SMEM)]
        + [block(operand.shape) for operand in operands[1:]],
        out_specs=[block(shape[0]) for shape in shapes],
    )(*operands)


VMEM_LIMIT = 24 * 1024 * 1024


def axis_sizes():
    return lax.axis_size("dp"), lax.axis_size("seq")


def places(lengths):
    dp_count, seq_count = axis_sizes()
    outer_count = dp_count // 2
    d, z = lax.axis_index("dp"), lax.axis_index("seq")
    o, index = d // 2, d * seq_count + z
    block = seq_count // 4

    def unsigned(value):
        return value.astype(jnp.uint32)

    return {
        "first": lax.axis_index("section") == 0,
        "operand": jnp.stack([o, d % 2, z, index]).astype(jnp.int32),
        "outer": [unsigned((o + k) % outer_count) for k in range(outer_count)],
        "line": [unsigned((z + k) % seq_count) for k in range(seq_count)],
        "even": z % 2 == 0,
        "micro": z // block // 2 == 0,
        "slots": [unsigned(index * length) for length in lengths],
    }


def swap_core(value):
    return lax.ppermute(value, "dp", [(d, d ^ 1) for d in range(lax.axis_size("dp"))])


def turn_outer(value, steps):
    count = lax.axis_size("dp")
    return lax.ppermute(value, "dp", [(d, (d + 2 * steps) % count) for d in range(count)])


def turn_line(value, steps):
    count = lax.axis_size("seq")
    return lax.ppermute(value, "seq", [(z, (z + steps) % count) for z in range(count)])


def joint_permute(value, moves):
    seq_count = lax.axis_size("seq")
    pairs = [(a[0] * seq_count + a[1], b[0] * seq_count + b[1]) for a, b in moves]
    return lax.ppermute(value, ("dp", "seq"), pairs)


def gather_line(piece):
    return [piece] + [turn_line(piece, k) for k in range(1, lax.axis_size("seq"))]


def gather_outer(stacked):
    return [stacked] + [turn_outer(stacked, k) for k in range(1, lax.axis_size("dp") // 2)]


def assemble(mine, theirs):
    outer_count, seq_count = len(mine), lax.axis_size("seq")
    d, z = lax.axis_index("dp"), lax.axis_index("seq")
    o, c = d // 2, d % 2
    turned = jnp.stack([jnp.stack(mine), jnp.stack(theirs)])
    sides = (jnp.arange(2) + c) % 2
    outers = (o - jnp.arange(outer_count)) % outer_count
    lines = (z - jnp.arange(seq_count)) % seq_count
    ordered = turned[sides][:, outers][:, :, lines]
    return ordered.transpose(1, 0, 2, 3, 4).reshape((-1,) + mine[0].shape[1:])


def scatter_core(kept, sent, at):
    came = swap_core(sent)

    def both(index):
        return lax.dynamic_index_in_dim(kept, index, 0, keepdims=False).astype(
            F32
        ) + lax.dynamic_index_in_dim(came, index, 0, keepdims=False).astype(F32)

    return both(at["outer"][0]), [both(index).astype(BF16) for index in at["outer"][1:]]


def scatter_outer(total, sent):
    for k, member in enumerate(sent):
        total = total + turn_outer(member, k + 1).astype(F32)
    return total


def scatter_line(total, take, at):
    low = total.astype(BF16)
    result = take(total, at["line"][0])
    for k in range(1, len(at["line"])):
        result = result + turn_line(take(low, at["line"][k]), k).astype(F32)
    return result


def image_moves(step):
    dp_count, seq_count = axis_sizes()
    block = seq_count // 4
    moves = []
    for d in range(dp_count):
        for z in range(seq_count):
            micro = (step + z) % 2
            rank = z // 2
            target = (d - d % 2 + rank % 2, (2 * micro + d % 2) * block + rank // 2)
            moves.append(((d, z), target))
    return moves


def to_images(blocks, at):
    arrived = []
    for step in range(2):
        sent = jnp.where(at["even"], blocks[step], blocks[1 - step])
        arrived.append(joint_permute(sent, image_moves(step)))
    low = jnp.where(at["micro"], arrived[0], arrived[1])
    high = jnp.where(at["micro"], arrived[1], arrived[0])
    return jnp.concatenate([low, high], axis=0)


def from_images(rows_own, at):
    half = rows_own.shape[0] // 2
    low, high = rows_own[:half], rows_own[half:]
    arrived = []
    for step in range(2):
        sent = jnp.where(at["micro"], *((low, high) if step == 0 else (high, low)))
        arrived.append(joint_permute(sent, [(b, a) for a, b in image_moves(step)]))
    return jnp.stack([jnp.where(at["even"], arrived[m], arrived[1 - m]) for m in range(2)])


def group_members():
    block = lax.axis_size("seq") // 4
    return [(turn, flip) for turn in range(block) for flip in range(2)][1:]


def group_moves(turn, flip):
    dp_count, seq_count = axis_sizes()
    block = seq_count // 4
    moves = []
    for d in range(dp_count):
        for z in range(seq_count):
            base = z - z % block
            moves.append(((d ^ flip, base + (z % block + turn) % block), (d, z)))
    return moves


def gather_group(own_rows):
    arrived = [joint_permute(own_rows, group_moves(*member)) for member in group_members()]
    return jnp.concatenate([own_rows] + arrived, axis=0)


def scatter_group(partial, own):
    total = partial[:own].astype(F32)
    for place, member in enumerate(group_members()):
        sent = partial[(place + 1) * own : (place + 2) * own]
        back = [(b, a) for a, b in group_moves(*member)]
        total = total + joint_permute(sent, back).astype(F32)
    return total.astype(BF16)


def slot_mask(lengths, slot_count):
    block = lax.axis_size("seq") // 4
    d, z = lax.axis_index("dp"), lax.axis_index("seq")
    c, group = d % 2, z // block
    theirs = swap_core(lengths[:, 0])
    counts = jnp.where(group % 2 == c, lengths[:, 0], theirs)
    counts = jnp.where(group // 2 == 0, counts[0], counts[1])
    places = jnp.arange(slot_count, dtype=jnp.int32)
    parts = []
    for turn, flip in [(0, 0)] + group_members():
        rank = (z % block + turn) % block * 2 + (c ^ flip)
        picked = lax.dynamic_slice_in_dim(counts, 2 * rank, 2, 0)
        parts.append((places[None, :] < picked[:, None]).astype(F32).reshape(-1, 1))
    return jnp.broadcast_to(jnp.concatenate(parts, axis=0), (len(parts) * 2 * slot_count, 128))


def to_section(value, steps):
    return lax.ppermute(value, "section", [(0, 1)] if steps == 1 else [(1, 0)])


def vector_slots(members, width):
    index = lax.axis_index("dp") * lax.axis_size("seq") + lax.axis_index("seq")
    count = lax.axis_size("dp") * lax.axis_size("seq")
    parts = []
    for member in members:
        length = member.shape[0]
        spread = jnp.zeros((count * length,), BF16)
        spread = lax.dynamic_update_slice_in_dim(spread, member, index * length, 0)
        parts.append(spread.reshape(-1, width))
    parts.append(jnp.zeros((4, width), BF16))
    return jnp.concatenate(parts, axis=0)


def own_slots(vectors, lengths, at):
    parts, start = [], 0
    for length, used, place in zip(lengths, (2, 6, 4), at["slots"]):
        flat = vectors[start : start + used].reshape(-1)
        parts.append(lax.dynamic_slice_in_dim(flat, place, length, 0))
        start += used
    return parts


def by_column(member, width):
    rows = member.shape[0]
    return member.reshape(rows, -1, width).transpose(1, 0, 2).reshape(-1, width)


def from_columns(block, rows):
    width = block.shape[1]
    return block.reshape(-1, rows, width).transpose(1, 0, 2).reshape(rows, -1)


def on_device(boundary, lengths, w_qkv, w_out, w_fc1, w_fc2, gains, shifts, fc1_bias):
    dp_count, seq_count = axis_sizes()
    outer_count = dp_count // 2
    lens = (gains.shape[1], shifts.shape[1], fc1_bias.shape[1])
    at = places(lens)
    place = at["operand"]
    slot_count = boundary.shape[3]
    own = 2 * slot_count
    total = lengths.shape[2] * slot_count
    rows, width = w_out.shape[1:]
    hidden = rows * 4 * dp_count * seq_count
    pairs = width // 128
    span = width // dp_count
    loose = outer_count if rows % 8 == 0 else 0
    own_start = to_images(boundary[0, :, 0], at)
    if loose:
        piece_a, piece_b = call_whole(
            pack_kernel,
            [place, w_qkv[0], w_out[0], w_fc1[0], w_fc2[0], gains, shifts, fc1_bias],
            [((4 * rows + 16, width), BF16), ((8 * rows, width), BF16)],
        )
    else:
        tail = vector_slots((gains[0], shifts[0], fc1_bias[0]), width)
        piece_a = jnp.concatenate([by_column(w_qkv[0], width), w_out[0], tail])
        piece_b = jnp.concatenate([by_column(w_fc1[0], width), w_fc2[0]])
    piece_a, at = lax.optimization_barrier((piece_a, at))
    line_a = jnp.stack(gather_line(piece_a))
    line_a, piece_b, own_start = lax.optimization_barrier((line_a, piece_b, own_start))
    line_b = jnp.stack(gather_line(piece_b))
    mine_a = gather_outer(line_a)
    line_b, *mine_a = lax.optimization_barrier((line_b, *mine_a))
    mine_b = gather_outer(line_b)
    mask = slot_mask(lengths, slot_count)
    all_start = gather_group(own_start)
    theirs_a = [swap_core(member) for member in mine_a]

    w_shape = ((4, width, width), BF16)
    tall_shape = ((hidden, width), BF16)
    vec_shape = ((16, width), F32)
    mid_shape = ((own, width), F32)
    low_shape = ((own, width), BF16)
    all_shape = ((total, width), BF16)
    q_shape = ((pairs, own, 128), BF16)
    k_shape = ((pairs, total, 128), BF16)
    qt_shape = ((pairs, 128, own), BF16)
    kt_shape = ((pairs, 128, total), BF16)
    p_shape = ((HEADS, total, own), BF16)
    h_shape = ((4, own, width), F32)
    shared_b = ((outer_count, 8 * span, width), BF16)
    shared_a = ((outer_count, 4 * span + 16, width), BF16)

    head_scratch = [q_shape, k_shape, k_shape, kt_shape, qt_shape]
    if loose:
        middle, w_a, vectors = call(
            functools.partial(first_kernel, loose, rows),
            [("s", place), ("v", all_start), ("v", mask)]
            + [("v", member) for member in (*mine_a, *theirs_a)],
            [mid_shape, w_shape, vec_shape],
            head_scratch, 10**9, [line_b],
        )
        middle, *mine_b = lax.optimization_barrier((middle, *mine_b))
        theirs_b = [swap_core(member) for member in mine_b]
        first_out, w_1, w_2 = call(
            functools.partial(second_kernel, loose, rows),
            [("s", place), ("v", middle), ("v", mask), ("v", vectors)]
            + [("v", member) for member in (*mine_b, *theirs_b)],
            [low_shape, w_shape, tall_shape],
            [low_shape, mid_shape], 10**9,
        )
    else:
        theirs_b = [swap_core(member) for member in mine_b]
        ordered = assemble(mine_a, theirs_a)
        w_a = ordered[:, : 4 * rows].reshape(-1, 4, rows, width).transpose(1, 0, 2, 3)
        w_a = w_a.reshape(4, width, width)
        vectors = jnp.sum(ordered[:, 4 * rows :].astype(F32), axis=0)
        ordered = assemble(mine_b, theirs_b)
        w_1 = ordered[:, : 4 * rows].reshape(-1, 4, rows, width).transpose(1, 0, 2, 3)
        w_1 = w_1.reshape(4, width, width)
        w_2 = ordered[:, 4 * rows :].reshape(hidden, width)
        (middle,) = call(
            functools.partial(first_kernel, loose, rows),
            [("s", place), ("v", all_start), ("v", mask), ("v", w_a), ("v", vectors)],
            [mid_shape], head_scratch, 10**9,
        )
        (first_out,) = call(
            functools.partial(second_kernel, loose, rows),
            [("s", place), ("v", middle), ("v", mask), ("v", vectors), ("v", w_1), ("v", w_2)],
            [low_shape], [low_shape, mid_shape], 10**9,
        )
    arrived = gather_group(to_section(first_out, 1))
    layer_in = jnp.where(at["first"], all_start, arrived)
    grad_scratch = [q_shape, qt_shape, k_shape, k_shape]
    saved = [mid_shape, q_shape, k_shape, k_shape, qt_shape, kt_shape, p_shape]
    partial, layer_out, middle, q, k, v, ot, kt, p = call(
        middle_kernel,
        [("v", layer_in)]
        + [("v", member) for member in (mask, vectors, w_a, w_1, w_2, own_start)],
        [all_shape, low_shape, *saved],
        [kt_shape, low_shape, mid_shape, h_shape, mid_shape, *grad_scratch], 4 * 10**9,
    )
    returned = to_section(scatter_group(partial, own), -1)
    grad_out = jnp.where(at["first"], returned, own_start)
    kept_b, sent_b, grad_mid, grad_vectors = call(
        feed_grad_kernel,
        [("s", place), ("v", grad_out)]
        + [("v", member) for member in (middle, vectors, mask, w_1, w_2)],
        [shared_b, shared_b, mid_shape, vec_shape],
        [low_shape, mid_shape, w_shape, tall_shape], 2 * 10**9,
    )
    kept_b, sent_b = scatter_core(kept_b, sent_b, at)
    partial, kept_a, sent_a = call(
        attend_grad_kernel,
        [("s", place)]
        + [
            ("v", member)
            for member in (
                grad_mid, w_a, ot, v, q, kt, p, k, layer_in, mask, vectors, grad_vectors
            )
        ],
        [all_shape, shared_a, shared_a],
        [*grad_scratch, w_shape, vec_shape], 10**10, sent_b,
    )

    def line_block(wide, index):
        split = wide.reshape(4, seq_count, rows, width)
        return lax.dynamic_index_in_dim(split, index, 1, keepdims=False).reshape(-1, width)

    def take_b(value, index):
        tall = value[4 * span :].reshape(seq_count, 4 * rows, width)
        tall = lax.dynamic_index_in_dim(tall, index, 0, keepdims=False)
        return jnp.concatenate([line_block(value[: 4 * span], index), tall])

    def take_a(value, index):
        return jnp.concatenate([line_block(value[: 4 * span], index), value[4 * span :]])

    total_b = scatter_outer(kept_b, sent_b)
    grad_in = scatter_group(partial, own)
    rows_out = from_images(jnp.where(at["first"], grad_in, layer_out), at)
    total_b, sent_a = lax.optimization_barrier((total_b, sent_a))
    kept_a, sent_a = scatter_core(kept_a, sent_a, at)
    total_a = scatter_outer(kept_a, sent_a)
    summed_b = scatter_line(total_b, take_b, at)
    summed_a = scatter_line(total_a, take_a, at)
    grads = (
        from_columns(summed_a[: 3 * rows], rows),
        summed_a[3 * rows : 4 * rows],
        from_columns(summed_b[: 4 * rows], rows),
        summed_b[4 * rows :],
        *own_slots(summed_a[4 * rows :], lens, at),
    )
    return (rows_out[None, :, None], *[member[None] for member in grads])


def solution(mesh):
    sharded = P("section", ("dp", "seq"), None)
    vector = P("section", ("dp", "seq"))
    images = P("section", None, "dp", "seq", None)
    grads = (sharded, sharded, sharded, sharded, vector, vector, vector)
    return jax.shard_map(
        on_device,
        mesh=mesh,
        in_specs=(images, P(None, "dp", None), *grads),
        out_specs=(images, *grads),
        check_vma=False,
    )
```

```python
import functools
import math
import jax
import jax.numpy as jnp
import numpy as np
from jax import lax
from jax.experimental import pallas as pl
from jax.experimental.pallas import tpu as pltpu
from jax.sharding import PartitionSpec as P

HEADS = 6
norm_eps = 1e-06
F32 = jnp.float32
BF16 = jnp.bfloat16


def mul(left, right, left_dim=1, right_dim=0):
    return lax.dot_general(
        left, right, (((left_dim,), (right_dim,)), ((), ())), preferred_element_type=F32
    )


def total_of(rows):
    return jnp.sum(rows, axis=0, keepdims=True)


def norm_parts(rows_in):
    centre = jnp.mean(rows_in, axis=-1, keepdims=True)
    centred = rows_in - centre
    spread = jnp.mean(centred * centred, axis=-1, keepdims=True)
    scale = lax.rsqrt(spread + norm_eps)
    return centred * scale, scale


def norm_grad(grad, gain, unit, scale):
    scaled = grad * gain
    inner = jnp.mean(scaled * unit, axis=-1, keepdims=True)
    return scale * (scaled - jnp.mean(scaled, axis=-1, keepdims=True) - unit * inner)


def gelu_cdf(hidden):
    return 0.5 + 0.5 * lax.erf(hidden * math.sqrt(0.5))


def row_of(vec_ref, index):
    return vec_ref[index : index + 1, :]


def head_halves(head_dim):
    lane = lax.broadcasted_iota(jnp.int32, (1, 128), 1)
    first_half = (lane < head_dim).astype(BF16)
    return (first_half, 1 - first_half)


def attend_forward(x_ref, mask_ref, wa_ref, vec_ref, refs, mid_ref):
    q_s, k_s, v_s, vt_s, ot_s, kt_s, p_s = refs
    own = q_s.shape[1]
    width = x_ref.shape[1]
    pairs = k_s.shape[0]
    head_dim = width // HEADS
    mask = mask_ref[:, :1]
    masked = x_ref[...].astype(F32) * mask
    unit, _ = norm_parts(masked)
    normed = (unit * row_of(vec_ref, 0) + row_of(vec_ref, 2)).astype(BF16)
    queries = (mul(normed[:own], wa_ref[0]) + row_of(vec_ref, 4)).astype(BF16)
    queries = (queries.astype(F32) * head_dim ** (-0.5)).astype(BF16)
    keys = mul(normed, wa_ref[1]).astype(BF16)
    values = (mul(normed, wa_ref[2]) + row_of(vec_ref, 5)).astype(BF16)
    for j in range(pairs):
        lanes = slice(j * 128, (j + 1) * 128)
        q_s[j] = queries[:, lanes]
        k_s[j] = keys[:, lanes]
        v_s[j] = values[:, lanes]
        vt_s[j] = values[:, lanes].T
        if kt_s is not None:
            kt_s[j] = keys[:, lanes].T
    halves = head_halves(head_dim)

    for j in range(pairs):
        bias = (mask_ref[:, :1] - 1.0) * 1e30
        for e in range(2):
            score = mul(k_s[j], q_s[j] * halves[e], 1, 1) + bias
            top = jnp.max(score, axis=0, keepdims=True)
            expo = jnp.exp(score - top)
            probs = (expo * (1.0 / total_of(expo))).astype(BF16)
            rows = slice(e * head_dim, (e + 1) * head_dim)
            ot_s[j, rows, :] = mul(vt_s[j, rows, :], probs).astype(BF16)
            if p_s is not None:
                p_s[2 * j + e] = probs

    attended = jnp.concatenate([ot_s[j].T for j in range(pairs)], axis=1)
    mid_ref[...] = masked[:own] + mul(attended, wa_ref[3]) + row_of(vec_ref, 6)


def gelu_slope(hidden, cdf):
    return cdf + hidden * jnp.exp(-0.5 * hidden * hidden) * (1.0 / math.sqrt(2 * math.pi))


def feed_forward(mid_ref, mask_ref, w1_ref, w2_ref, vec_ref, c_s, acc_s, stored, y_ref):
    own, width = mid_ref.shape
    unit, _ = norm_parts(mid_ref[...])
    c_s[...] = (unit * row_of(vec_ref, 1) + row_of(vec_ref, 3)).astype(BF16)
    acc_s[...] = jnp.zeros_like(acc_s)

    @pl.loop(0, w1_ref.shape[0])
    def _(k):
        hidden = mul(c_s[...], w1_ref[k]) + vec_ref[pl.ds(8 + k, 1), :]
        cdf = gelu_cdf(hidden)
        active = (hidden * cdf).astype(BF16)
        if stored is not None:
            stored[0][k] = active
            stored[1][k] = gelu_slope(hidden, cdf)
        rows = pl.ds(pl.multiple_of(k * width, 128), width)
        acc_s[...] += mul(active, w2_ref[rows, :])

    y_ref[...] = (
        (mid_ref[...] + acc_s[...] + row_of(vec_ref, 7)) * mask_ref[:own, :1]
    ).astype(BF16)


def feed_backward(
    mid_ref, mask_ref, dy_ref, w1_ref, w2_ref, vec_ref, c_s, acc_s, stored, gmid_ref, grads
):
    own, width = mid_ref.shape
    acc_s[...] = jnp.zeros_like(acc_s)
    g1_s, g2_s, gv_ref = grads or (None, None, None)

    @pl.loop(0, w1_ref.shape[0])
    def _(k):
        if stored is None:
            hidden = mul(c_s[...], w1_ref[k]) + vec_ref[pl.ds(8 + k, 1), :]
            slope = gelu_slope(hidden, gelu_cdf(hidden))
        else:
            slope = stored[1][k]
        grad_second = (dy_ref[...].astype(F32) * mask_ref[:own, :1]).astype(BF16)
        rows = pl.ds(pl.multiple_of(k * width, 128), width)
        grad_hidden = (mul(grad_second, w2_ref[rows, :], 1, 1) * slope).astype(BF16)
        acc_s[...] += mul(grad_hidden, w1_ref[k], 1, 1)
        if grads is not None:
            active = stored[0][k]
            g1_s[k] = mul(c_s[...], grad_hidden, 0, 0).astype(BF16)
            g2_s[rows, :] = mul(active, grad_second, 0, 0).astype(BF16)
            gv_ref[pl.ds(8 + k, 1), :] = total_of(grad_hidden.astype(F32))

    grad_y = dy_ref[...].astype(F32) * mask_ref[:own, :1]
    grad_c = acc_s[...]
    unit, scale = norm_parts(mid_ref[...])
    grad_mid = grad_y + norm_grad(grad_c, row_of(vec_ref, 1), unit, scale)
    gmid_ref[...] = grad_mid
    if grads is not None:
        gv_ref[1:2, :] = total_of(grad_c * unit)
        gv_ref[3:4, :] = total_of(grad_c)
        gv_ref[6:7, :] = total_of(grad_mid.astype(BF16).astype(F32))
        gv_ref[7:8, :] = total_of(grad_y.astype(BF16).astype(F32))


def attend_backward(x_ref, mask_ref, wa_ref, vec_ref, kept, scratch, gmid_ref, du_ref, grads):
    q_s, k_s, v_s, ot_s, kt_s, p_s = kept
    do_s, dq_s, dk_s, dv_s = scratch
    own, width = gmid_ref.shape
    pairs = do_s.shape[0]
    head_dim = width // HEADS
    grad_branch = gmid_ref[...].astype(BF16)
    grad_att = mul(grad_branch, wa_ref[3], 1, 1).astype(BF16)
    for j in range(pairs):
        do_s[j] = grad_att[:, j * 128 : (j + 1) * 128]
    if grads is not None:
        ga_s, gv_ref = grads
        for j in range(pairs):
            ga_s[3, j * 128 : (j + 1) * 128, :] = mul(ot_s[j], grad_branch).astype(BF16)
    halves = head_halves(head_dim)

    for j in range(pairs):
        grad_k = None
        for e in range(2):
            half_do = do_s[j] * halves[e]
            half_q = q_s[j] * halves[e]
            grad_p = mul(v_s[j], half_do, 1, 1)
            probs_low = p_s[2 * j + e]
            probs = probs_low.astype(F32)
            row_dot = total_of(probs * grad_p)
            grad_s = (probs * (grad_p - row_dot)).astype(BF16)
            rows = slice(e * head_dim, (e + 1) * head_dim)
            dq_s[j, rows, :] = (mul(kt_s[j, rows, :], grad_s) * head_dim ** (-0.5)).astype(BF16)
            part_k = mul(grad_s, half_q)
            part_v = mul(probs_low, half_do)
            grad_k, grad_v = (part_k, part_v) if grad_k is None else (grad_k + part_k, grad_v + part_v)
        dk_s[j] = grad_k.astype(BF16)
        dv_s[j] = grad_v.astype(BF16)

    grad_q = jnp.concatenate([dq_s[j].T for j in range(pairs)], axis=1)
    grad_k = jnp.concatenate([dk_s[j] for j in range(pairs)], axis=1)
    grad_v = jnp.concatenate([dv_s[j] for j in range(pairs)], axis=1)
    mask = mask_ref[:, :1]
    unit, scale = norm_parts(x_ref[...].astype(F32) * mask)
    if grads is not None:
        normed = (unit * row_of(vec_ref, 0) + row_of(vec_ref, 2)).astype(BF16)
        ga_s[0] = mul(normed[:own], grad_q, 0, 0).astype(BF16)
        turned = normed.T
        ga_s[1] = mul(turned, grad_k).astype(BF16)
        ga_s[2] = mul(turned, grad_v).astype(BF16)
        gv_ref[4:5, :] = total_of(grad_q.astype(F32))
        gv_ref[5:6, :] = total_of(grad_v.astype(F32))
    grad_n = mul(grad_k, wa_ref[1], 1, 1) + mul(grad_v, wa_ref[2], 1, 1)
    grad_n = jnp.concatenate([grad_n[:own] + mul(grad_q, wa_ref[0], 1, 1), grad_n[own:]], axis=0)
    if grads is not None:
        gv_ref[0:1, :] = total_of(grad_n * unit)
        gv_ref[2:3, :] = total_of(grad_n)
    grad_u = norm_grad(grad_n, row_of(vec_ref, 0), unit, scale)
    grad_u = jnp.concatenate([grad_u[:own] + gmid_ref[...], grad_u[own:]], axis=0)
    du_ref[...] = (grad_u * mask).astype(BF16)


def pack_kernel(place_ref, qkv_ref, out_ref, fc1_ref, fc2_ref, gains_ref, shifts_ref, bias_ref, a_ref, b_ref, c_ref):
    rows, width = out_ref.shape
    index = place_ref[3]

    def columns(ref, count):
        wide = ref[...].astype(F32)
        return [wide[:, s * width : (s + 1) * width] for s in range(count)]

    lane = lax.broadcasted_iota(jnp.int32, (1, width), 1)
    row = lax.broadcasted_iota(jnp.int32, (16, width), 0)
    tail, base = jnp.zeros((16, width), F32), 0
    for ref, used in ((gains_ref, 2), (shifts_ref, 6), (bias_ref, 4)):
        length = ref.shape[1]
        start = index * length
        first, offset = start // width, lax.rem(start, width)
        spread = jnp.concatenate(
            [ref[...].astype(F32), jnp.zeros((1, width - length), F32)], axis=1
        )
        spread = pltpu.roll(jnp.broadcast_to(spread, (8, width)), offset, 1)[:1]
        target = base + first + jnp.where(lane < offset, 1, 0)
        tail = tail + jnp.where(row == target, spread, 0.0)
        base += used
    blocks = columns(qkv_ref, 3) + [out_ref[...].astype(F32), tail]
    a_ref[...] = jnp.concatenate(blocks, axis=0).astype(BF16)
    b_ref[...] = jnp.concatenate(columns(fc1_ref, 4), axis=0).astype(BF16)
    c_ref[...] = fc2_ref[...]


def piece_groups(place_ref, mine, theirs, turns):
    outer, core, line = place_ref[0], place_ref[1], place_ref[2]
    count = mine[0].shape[0]
    for side, members in enumerate((mine, theirs)):
        for turn in range(turns):
            index = lax.rem(outer + (turns - turn), turns) * 2 + (core if side == 0 else 1 - core)
            yield index, [
                members[turn][turned_bits(line ^ z, count)].astype(F32) for z in range(count)
            ]


def halved_groups(place_ref, mine, theirs, turns):
    outer, core, line = place_ref[0], place_ref[1], place_ref[2]
    count = mine[0].shape[0] // turns * 2
    for side, (even, odd) in enumerate((mine, theirs)):
        for turn in range(turns):
            index = lax.rem(outer + (turns - turn), turns) * 2 + (core if side == 0 else 1 - core)
            blocks = []
            for z in range(count):
                entry = turned_bits((line ^ z) // 2, count // 2) * turns + turn
                blocks.append(jnp.where((line ^ z) % 2 == 0, even[entry], odd[entry]).astype(F32))
            yield index, blocks


def first_kernel(loose, rows, ins, outs, scratch):
    place_ref, x_ref, mask_ref = ins[:3]
    if loose:
        mine, theirs = ins[3 : 3 + loose], ins[3 + loose :]
        mid_ref, wa_out, vec_out = outs
        wa_ref, vec_ref = wa_out, vec_out
        vector = None
        for index, blocks in piece_groups(place_ref, mine, theirs, loose):
            span = rows * len(blocks)
            start = pl.multiple_of(index * span, 16)
            for s in range(4):
                group = jnp.concatenate([b[s * rows : (s + 1) * rows] for b in blocks], axis=0)
                wa_ref[s, pl.ds(start, span), :] = group.astype(BF16)
            for b in blocks:
                tail = b[4 * rows : 4 * rows + 16]
                vector = tail if vector is None else vector + tail
        vec_ref[...] = vector
    else:
        wa_ref, vec_ref = (member for member in ins[3:])
        (mid_ref,) = outs
    attend_forward(x_ref, mask_ref, wa_ref, vec_ref, (*scratch, None, None), mid_ref)


def second_kernel(loose, rows, ins, outs, scratch):
    place_ref, mid_ref, mask_ref, vec_ref = ins[:4]
    c_s, acc_s = scratch
    if loose:
        sets = [ins[4 : 4 + loose], ins[4 + loose : 4 + 2 * loose], ins[-4:-2], ins[-2:]]
        y_ref, w1_ref, w2_ref = outs
        for index, blocks in piece_groups(place_ref, sets[0], sets[1], loose):
            span = rows * len(blocks)
            start = pl.multiple_of(index * span, 16)
            for s in range(4):
                group = jnp.concatenate([b[s * rows : (s + 1) * rows] for b in blocks], axis=0)
                w1_ref[s, pl.ds(start, span), :] = group.astype(BF16)
        for index, blocks in halved_groups(place_ref, sets[2], sets[3], loose):
            span = 4 * rows * len(blocks)
            group = jnp.concatenate(blocks, axis=0)
            w2_ref[pl.ds(pl.multiple_of(index * span, 16), span), :] = group.astype(BF16)
    else:
        w1_ref, w2_ref = ins[4:]
        (y_ref,) = outs
    feed_forward(mid_ref, mask_ref, w1_ref, w2_ref, vec_ref, c_s, acc_s, None, y_ref)


def middle_kernel(ins, outs, scratch):
    x_ref, mask_ref, vec_ref, wa_ref, w1_ref, w2_ref, dy_ref = ins
    du_ref, mid_ref, c_s, *kept = outs
    vt_s, acc_s, gmid_s, *grad_scratch = scratch
    q_s, k_s, v_s, ot_s, kt_s, p_s = kept
    attend_forward(
        x_ref, mask_ref, wa_ref, vec_ref, (q_s, k_s, v_s, vt_s, ot_s, kt_s, p_s), mid_ref
    )
    unit, _ = norm_parts(mid_ref[...])
    c_s[...] = (unit * row_of(vec_ref, 1) + row_of(vec_ref, 3)).astype(BF16)
    feed_backward(
        mid_ref, mask_ref, dy_ref, w1_ref, w2_ref, vec_ref, c_s, acc_s, None, gmid_s, None
    )
    attend_backward(x_ref, mask_ref, wa_ref, vec_ref, kept, grad_scratch, gmid_s, du_ref, None)


def output_kernel(ins, outs, scratch):
    mid_ref, mask_ref, vec_ref, w1_ref, w2_ref = ins
    y_ref, active_ref, slope_ref = outs
    feed_forward(
        mid_ref, mask_ref, w1_ref, w2_ref, vec_ref, *scratch, (active_ref, slope_ref), y_ref
    )


def share_out(core, blocks_of, outer_count, start, size, kept_ref, sent_ref):
    for o in range(outer_count):
        even, odd = blocks_of(2 * o), blocks_of(2 * o + 1)
        kept_ref[o, start : start + size, :] = jnp.where(core == 0, even, odd)
        sent_ref[o, start : start + size, :] = jnp.where(core == 0, odd, even)


def feed_grad_kernel(ins, outs, scratch):
    place_ref, dy_ref, mid_ref, vec_ref, mask_ref, w1_ref, w2_ref, c_ref, active_ref, slope_ref = ins
    kept_ref, sent_ref, gmid_ref, gv_ref = outs
    acc_s, g1_s, g2_s = scratch
    gv_ref[...] = jnp.zeros_like(gv_ref)
    outer_count = kept_ref.shape[0]
    span = w1_ref.shape[1] // (2 * outer_count)
    feed_backward(
        mid_ref, mask_ref, dy_ref, w1_ref, w2_ref, vec_ref, c_ref, acc_s,
        (active_ref, slope_ref), gmid_ref, (g1_s, g2_s, gv_ref),
    )
    core = place_ref[1]
    for s in range(4):
        share_out(
            core, lambda d: g1_s[s, d * span : (d + 1) * span, :], outer_count,
            s * span, span, kept_ref, sent_ref,
        )
    share_out(
        core, lambda d: g2_s[4 * d * span : 4 * (d + 1) * span, :], outer_count,
        4 * span, 4 * span, kept_ref, sent_ref,
    )


def attend_grad_kernel(ins, outs, scratch):
    place_ref, gmid_in, wa_in, ot_in, v_in, q_in, kt_in, p_in, k_in, x_in, mask_in, vec_in, gv_in = ins
    du_ref, kept_ref, sent_ref = outs
    do_s, dq_s, dk_s, dv_s, ga_s, gv_s = scratch
    gmid_ref, wa_ref, ot_s = gmid_in, wa_in, ot_in
    outer_count = kept_ref.shape[0]
    span = wa_ref.shape[1] // (2 * outer_count)
    gv_s[...] = gv_in[...]
    attend_backward(
        x_in, mask_in, wa_ref, vec_in, (q_in, k_in, v_in, ot_s, kt_in, p_in),
        (do_s, dq_s, dk_s, dv_s), gmid_ref, du_ref, (ga_s, gv_s),
    )
    core = place_ref[1]
    for s in range(4):
        share_out(
            core, lambda d: ga_s[s, d * span : (d + 1) * span, :], outer_count,
            s * span, span, kept_ref, sent_ref,
        )
    tail = gv_s[...].astype(BF16)
    for o in range(outer_count):
        kept_ref[o, 4 * span :, :] = tail
        sent_ref[o, 4 * span :, :] = tail


def call(kernel, operands, results, scratch, flops, after=()):
    space = {"s": pltpu.SMEM, "v": pltpu.VMEM}

    def body(*refs):
        refs = list(refs[len(after) :])
        given, refs = refs[: len(operands)], refs[len(operands) :]
        kernel(given, refs[: len(results)], refs[len(results) :])

    return pl.pallas_call(
        body,
        out_shape=[jax.ShapeDtypeStruct(*result) for result in results],
        in_specs=[pl.BlockSpec(memory_space=pl.ANY)] * len(after)
        + [pl.BlockSpec(memory_space=space[kind]) for kind, _ in operands],
        out_specs=[pl.BlockSpec(memory_space=pltpu.VMEM)] * len(results),
        scratch_shapes=[pltpu.VMEM(*shape) for shape in scratch],
        compiler_params=pltpu.CompilerParams(vmem_limit_bytes=VMEM_LIMIT),
        cost_estimate=pl.CostEstimate(flops=flops, bytes_accessed=4 * 10**6, transcendentals=10**6),
    )(*after, *[array for _, array in operands])


def call_whole(kernel, operands, shapes):
    def block(shape):
        return pl.BlockSpec(shape, lambda i: (0,) * len(shape))

    return pl.pallas_call(
        kernel,
        grid=(1,),
        out_shape=[jax.ShapeDtypeStruct(*shape) for shape in shapes],
        in_specs=[pl.BlockSpec(memory_space=pltpu.SMEM)]
        + [block(operand.shape) for operand in operands[1:]],
        out_specs=[block(shape[0]) for shape in shapes],
    )(*operands)


VMEM_LIMIT = 24 * 1024 * 1024


def axis_sizes():
    return lax.axis_size("dp"), lax.axis_size("seq")


def places(lengths):
    dp_count, seq_count = axis_sizes()
    outer_count = dp_count // 2
    d, z = lax.axis_index("dp"), lax.axis_index("seq")
    o, index = d // 2, d * seq_count + z
    block = seq_count // 4

    def unsigned(value):
        return value.astype(jnp.uint32)

    return {
        "first": lax.axis_index("section") == 0,
        "operand": jnp.stack([o, d % 2, z, index]).astype(jnp.int32),
        "outer": [unsigned((o + k) % outer_count) for k in range(outer_count)],
                "bits": [
            (unsigned(z // step % 2), unsigned(1 - z // step % 2)) for step in reversed(line_steps())
        ],
        "even": z % 2 == 0,
        "micro": z // block // 2 == 0,
        "slots": [unsigned(index * length) for length in lengths],
    }


def pick(value, index, axis, rows=None):
    starts = [np.uint32(0)] * value.ndim
    starts[axis] = index
    sizes = list(value.shape)
    sizes[axis] = 1
    if rows is not None:
        starts[axis + 1], sizes[axis + 1] = np.uint32(rows[0]), rows[1] - rows[0]
    return lax.dynamic_slice(value, starts, sizes).reshape(sizes[:axis] + sizes[axis + 1 :])


def swap_core(value):
    return lax.ppermute(value, "dp", [(d, d ^ 1) for d in range(lax.axis_size("dp"))])


def turn_outer(value, steps):
    count = lax.axis_size("dp")
    return lax.ppermute(value, "dp", [(d, (d + 2 * steps) % count) for d in range(count)])


def turn_line(value, steps):
    count = lax.axis_size("seq")
    return lax.ppermute(value, "seq", [(z, (z + steps) % count) for z in range(count)])


def joint_permute(value, moves):
    seq_count = lax.axis_size("seq")
    pairs = [(a[0] * seq_count + a[1], b[0] * seq_count + b[1]) for a, b in moves]
    return lax.ppermute(value, ("dp", "seq"), pairs)


def line_steps():
    count, steps = lax.axis_size("seq"), []
    while count > 1:
        count //= 2
        steps.append(count)
    return steps


def cross_line(value, distance):
    count = lax.axis_size("seq")
    return lax.ppermute(value, "seq", [(z, z ^ distance) for z in range(count)])


def gather_step(pieces, step):
    return jnp.concatenate([pieces, cross_line(pieces, line_steps()[step])])


def gather_from(pieces, step, stop=None):
    for later in range(step, len(line_steps()) if stop is None else stop):
        pieces = gather_step(pieces, later)
    return pieces


def turned_bits(value, count):
    result, low, high = value * 0, 1, count // 2
    while high:
        result = result + (value // high) % 2 * low
        low, high = low * 2, high // 2
    return result


def gather_outer(stacked):
    return [stacked] + [turn_outer(stacked, k) for k in range(1, lax.axis_size("dp") // 2)]


def assemble(mine, theirs):
    outer_count, seq_count = len(mine), lax.axis_size("seq")
    d, z = lax.axis_index("dp"), lax.axis_index("seq")
    o, c = d // 2, d % 2
    turned = jnp.stack([jnp.stack(mine), jnp.stack(theirs)])
    sides = (jnp.arange(2) + c) % 2
    outers = (o - jnp.arange(outer_count)) % outer_count
    lines = turned_bits(z ^ jnp.arange(seq_count), seq_count)
    ordered = turned[sides][:, outers][:, :, lines]
    return ordered.transpose(1, 0, 2, 3, 4).reshape((-1,) + mine[0].shape[1:])


def scatter_core(kept, came, at, rows):
    def both(index):
        mine, theirs = (
            pick(member, index, 0, rows).astype(F32) for member in (kept, came)
        )
        return mine + theirs

    return both(at["outer"][0]), [both(index).astype(BF16) for index in at["outer"][1:]]


def scatter_outer(total, sent):
    for k, member in enumerate(sent):
        total = total + turn_outer(member, k + 1).astype(F32)
    return total


def line_blocks(total, lead, tail=0):
    body, rest = total[: total.shape[0] - tail], total[total.shape[0] - tail :]
    return body.reshape(lead, lax.axis_size("seq"), -1, total.shape[1]), rest


def halve_parts(state, at, step):
    body, rest = state
    mine, other = at["bits"][step]
    lead, count, _, width = body.shape
    halves = body.reshape(lead, count // 2, 2, -1, width)
    body, sent = pick(halves, mine, 2), pick(halves, other, 2).reshape(-1, width)
    if rest.shape[0]:
        sent = jnp.concatenate([sent, rest])
    return (body, rest), sent.astype(BF16)


def halve_sum(state, sent, step):
    body, rest = state
    came = cross_line(sent, line_steps()[-1 - step]).astype(F32)
    tail = rest.shape[0]
    body = body + came[: came.shape[0] - tail].reshape(body.shape)
    return body, rest + came[came.shape[0] - tail :]


def halve_line(state, at, step):
    return halve_sum(*halve_parts(state, at, step), step)


def halve_rest(state, at, step):
    for later in range(step, len(at["bits"])):
        state = halve_line(state, at, later)
    return state


def image_moves(step):
    dp_count, seq_count = axis_sizes()
    block = seq_count // 4
    moves = []
    for d in range(dp_count):
        for z in range(seq_count):
            micro = (step + z) % 2
            rank = z // 2
            target = (d - d % 2 + rank % 2, (2 * micro + d % 2) * block + rank // 2)
            moves.append(((d, z), target))
    return moves


def to_images(blocks, at):
    arrived = []
    for step in range(2):
        sent = jnp.where(at["even"], blocks[step], blocks[1 - step])
        arrived.append(joint_permute(sent, image_moves(step)))
    low = jnp.where(at["micro"], arrived[0], arrived[1])
    high = jnp.where(at["micro"], arrived[1], arrived[0])
    return jnp.concatenate([low, high], axis=0)


def from_images(rows_own, at, after):
    half = rows_own.shape[0] // 2
    low, high = rows_own[:half], rows_own[half:]
    arrived = []
    for step in range(2):
        sent = jnp.where(at["micro"], *((low, high) if step == 0 else (high, low)))
        arrived.append(joint_permute(sent, [(b, a) for a, b in image_moves(step)]))
    after, *arrived = lax.optimization_barrier((after, *arrived))
    return jnp.stack([jnp.where(at["even"], arrived[m], arrived[1 - m]) for m in range(2)]), after


def group_members():
    block = lax.axis_size("seq") // 4
    return [(turn, flip) for turn in range(block) for flip in range(2)][1:]


def group_moves(turn, flip):
    dp_count, seq_count = axis_sizes()
    block = seq_count // 4
    moves = []
    for d in range(dp_count):
        for z in range(seq_count):
            base = z - z % block
            moves.append(((d ^ flip, base + (z % block + turn) % block), (d, z)))
    return moves


def gather_group(own_rows):
    arrived = [joint_permute(own_rows, group_moves(*member)) for member in group_members()]
    return jnp.concatenate([own_rows] + arrived, axis=0)


def scatter_group(partial, own):
    total = partial[:own].astype(F32)
    for place, member in enumerate(group_members()):
        sent = partial[(place + 1) * own : (place + 2) * own]
        back = [(b, a) for a, b in group_moves(*member)]
        total = total + joint_permute(sent, back).astype(F32)
    return total.astype(BF16)


def slot_mask(lengths, slot_count):
    block = lax.axis_size("seq") // 4
    d, z = lax.axis_index("dp"), lax.axis_index("seq")
    c, group = d % 2, z // block
    theirs = swap_core(lengths[:, 0])
    counts = jnp.where(group % 2 == c, lengths[:, 0], theirs)
    counts = jnp.where(group // 2 == 0, counts[0], counts[1])
    places = jnp.arange(slot_count, dtype=jnp.int32)
    parts = []
    for turn, flip in [(0, 0)] + group_members():
        rank = (z % block + turn) % block * 2 + (c ^ flip)
        picked = lax.dynamic_slice_in_dim(counts, 2 * rank, 2, 0)
        parts.append((places[None, :] < picked[:, None]).astype(F32).reshape(-1, 1))
    return jnp.broadcast_to(jnp.concatenate(parts, axis=0), (len(parts) * 2 * slot_count, 128))


def to_section(value, steps):
    return lax.ppermute(value, "section", [(0, 1)] if steps == 1 else [(1, 0)])


def vector_slots(members, width):
    index = lax.axis_index("dp") * lax.axis_size("seq") + lax.axis_index("seq")
    count = lax.axis_size("dp") * lax.axis_size("seq")
    parts = []
    for member in members:
        length = member.shape[0]
        spread = jnp.zeros((count * length,), BF16)
        spread = lax.dynamic_update_slice_in_dim(spread, member, index * length, 0)
        parts.append(spread.reshape(-1, width))
    parts.append(jnp.zeros((4, width), BF16))
    return jnp.concatenate(parts, axis=0)


def own_slots(vectors, lengths, at):
    parts, start = [], 0
    for length, used, place in zip(lengths, (2, 6, 4), at["slots"]):
        flat = vectors[start : start + used].reshape(-1)
        parts.append(lax.dynamic_slice_in_dim(flat, place, length, 0))
        start += used
    return parts


def by_column(member, width):
    rows = member.shape[0]
    return member.reshape(rows, -1, width).transpose(1, 0, 2).reshape(-1, width)


def from_columns(block, rows):
    width = block.shape[1]
    return block.reshape(-1, rows, width).transpose(1, 0, 2).reshape(rows, -1)


def on_device(boundary, lengths, w_qkv, w_out, w_fc1, w_fc2, gains, shifts, fc1_bias):
    dp_count, seq_count = axis_sizes()
    outer_count = dp_count // 2
    lens = (gains.shape[1], shifts.shape[1], fc1_bias.shape[1])
    at = places(lens)
    place = at["operand"]
    slot_count = boundary.shape[3]
    own = 2 * slot_count
    total = lengths.shape[2] * slot_count
    rows, width = w_out.shape[1:]
    hidden = rows * 4 * dp_count * seq_count
    pairs = width // 128
    span = width // dp_count
    loose = outer_count if rows % 8 == 0 else 0
    if loose:
        piece_a, piece_b, piece_c = call_whole(
            pack_kernel,
            [place, w_qkv[0], w_out[0], w_fc1[0], w_fc2[0], gains, shifts, fc1_bias],
            [((4 * rows + 16, width), BF16)] + [((4 * rows, width), BF16)] * 2,
        )
    else:
        tail = vector_slots((gains[0], shifts[0], fc1_bias[0]), width)
        piece_a = jnp.concatenate([by_column(w_qkv[0], width), w_out[0], tail])
        piece_b, piece_c = by_column(w_fc1[0], width), w_fc2[0]
    piece_a, at = lax.optimization_barrier((piece_a, at))
    half_a = gather_step(piece_a[None], 0)
    near_c = jnp.stack(gather_outer(piece_c))
    half_a, piece_b, near_c = lax.optimization_barrier((half_a, piece_b, near_c))
    line_a = gather_from(half_a, 1)
    half_b = gather_step(piece_b[None], 0)
    line_a, half_b, near_c, blocks = lax.optimization_barrier(
        (line_a, half_b, near_c, boundary[0, :, 0])
    )
    mine_a = gather_outer(line_a)
    line_b = gather_from(half_b, 1)
    half_c = gather_step(near_c, 0)
    own_start = to_images(blocks, at)
    line_b, half_c, own_start, *mine_a = lax.optimization_barrier(
        (line_b, half_c, own_start, *mine_a)
    )
    mine_b = gather_outer(line_b)
    half_c = gather_from(half_c, 1, len(line_steps()) - 1)
    mine_c = [half_c, cross_line(half_c, line_steps()[-1])]
    mask = slot_mask(lengths, slot_count)
    all_start = gather_group(own_start)
    theirs_a = [swap_core(member) for member in mine_a]

    w_shape = ((4, width, width), BF16)
    tall_shape = ((hidden, width), BF16)
    vec_shape = ((16, width), F32)
    mid_shape = ((own, width), F32)
    low_shape = ((own, width), BF16)
    all_shape = ((total, width), BF16)
    q_shape = ((pairs, own, 128), BF16)
    k_shape = ((pairs, total, 128), BF16)
    qt_shape = ((pairs, 128, own), BF16)
    kt_shape = ((pairs, 128, total), BF16)
    p_shape = ((HEADS, total, own), BF16)
    h_shape = ((4, own, width), F32)
    active_shape = ((4, own, width), BF16)
    shared_b = ((outer_count, 8 * span, width), BF16)
    shared_a = ((outer_count, 4 * span + 16, width), BF16)

    head_scratch = [q_shape, k_shape, k_shape, kt_shape, qt_shape]
    if loose:
        middle, w_a, vectors = call(
            functools.partial(first_kernel, loose, rows),
            [("s", place), ("v", all_start), ("v", mask)]
            + [("v", member) for member in (*mine_a, *theirs_a)],
            [mid_shape, w_shape, vec_shape],
            head_scratch, 10**9, [line_b],
        )
        middle, mine_c[1], *mine_b[1:] = lax.optimization_barrier(
            (middle, mine_c[1], *mine_b[1:])
        )
        theirs_b = [swap_core(member) for member in mine_b]
        theirs_c = [swap_core(member) for member in mine_c]
        first_out, w_1, w_2 = call(
            functools.partial(second_kernel, loose, rows),
            [("s", place), ("v", middle), ("v", mask), ("v", vectors)]
            + [("v", member) for member in (*mine_b, *theirs_b, *mine_c, *theirs_c)],
            [low_shape, w_shape, tall_shape],
            [low_shape, mid_shape], 10**9,
        )
    else:
        theirs_b = [swap_core(member) for member in mine_b]
        theirs_c = [swap_core(member) for member in mine_c]
        ordered = assemble(mine_a, theirs_a)
        w_a = ordered[:, : 4 * rows].reshape(-1, 4, rows, width).transpose(1, 0, 2, 3)
        w_a = w_a.reshape(4, width, width)
        vectors = jnp.sum(ordered[:, 4 * rows :].astype(F32), axis=0)
        w_1 = assemble(mine_b, theirs_b).reshape(-1, 4, rows, width).transpose(1, 0, 2, 3)
        w_1 = w_1.reshape(4, width, width)
        apart = [
            [
                jnp.concatenate(member).reshape(seq_count, outer_count, -1, width)[:, k]
                for k in range(outer_count)
            ]
            for member in (mine_c, theirs_c)
        ]
        w_2 = assemble(*apart).reshape(hidden, width)
        (middle,) = call(
            functools.partial(first_kernel, loose, rows),
            [("s", place), ("v", all_start), ("v", mask), ("v", w_a), ("v", vectors)],
            [mid_shape], head_scratch, 10**9,
        )
        (first_out,) = call(
            functools.partial(second_kernel, loose, rows),
            [("s", place), ("v", middle), ("v", mask), ("v", vectors), ("v", w_1), ("v", w_2)],
            [low_shape], [low_shape, mid_shape], 10**9,
        )
    arrived = gather_group(to_section(first_out, 1))
    layer_in = jnp.where(at["first"], all_start, arrived)
    grad_scratch = [q_shape, qt_shape, k_shape, k_shape]
    saved = [mid_shape, low_shape, q_shape, k_shape, k_shape, qt_shape, kt_shape, p_shape]
    partial, middle, normed, q, k, v, ot, kt, p = call(
        middle_kernel,
        [("v", layer_in)]
        + [("v", member) for member in (mask, vectors, w_a, w_1, w_2, own_start)],
        [all_shape, *saved],
        [kt_shape, mid_shape, mid_shape, *grad_scratch], 4 * 10**9,
    )
    sent_back = scatter_group(partial, own)
    returned = to_section(sent_back, -1)
    layer_out, active, slope = call(
        output_kernel,
        [("v", member) for member in (middle, mask, vectors, w_1, w_2)],
        [low_shape, active_shape, h_shape], [low_shape, mid_shape], 2 * 10**9, [sent_back],
    )
    grad_out = jnp.where(at["first"], returned, own_start)
    kept_b, sent_b, grad_mid, grad_vectors = call(
        feed_grad_kernel,
        [("s", place), ("v", grad_out)]
        + [
            ("v", member)
            for member in (middle, vectors, mask, w_1, w_2, normed, active, slope)
        ],
        [shared_b, shared_b, mid_shape, vec_shape],
        [mid_shape, w_shape, tall_shape], 2 * 10**9,
    )
    came_b = swap_core(sent_b)
    both_c = kept_b[:, 4 * span :].astype(F32) + came_b[:, 4 * span :].astype(F32)
    state_c, sent_c = halve_parts(line_blocks(both_c.reshape(-1, width), outer_count), at, 0)
    kept_b, sent_b = scatter_core(kept_b, came_b, at, (0, 4 * span))
    partial, kept_a, sent_a = call(
        attend_grad_kernel,
        [("s", place)]
        + [
            ("v", member)
            for member in (
                grad_mid, w_a, ot, v, q, kt, p, k, layer_in, mask, vectors, grad_vectors
            )
        ],
        [all_shape, shared_a, shared_a],
        [*grad_scratch, w_shape, vec_shape], 10**10, [*sent_b, sent_c],
    )

    total_b = scatter_outer(kept_b, sent_b)
    state_c = halve_sum(state_c, sent_c, 0)
    total_b, state_c, sent_a, partial = lax.optimization_barrier(
        (total_b, state_c, sent_a, partial)
    )
    kept_a, sent_a = scatter_core(kept_a, swap_core(sent_a), at, None)
    grad_in = scatter_group(partial, own)
    total_b, state_c, *sent_a = lax.optimization_barrier((total_b, state_c, *sent_a))
    total_a = scatter_outer(kept_a, sent_a)
    state_b = halve_line(line_blocks(total_b, 4), at, 0)
    body_c = halve_rest(state_c, at, 1)[0].reshape(outer_count, -1, width)
    rows_last = jnp.where(at["first"], grad_in, layer_out)
    total_a, state_b, body_c, rows_last = lax.optimization_barrier(
        (total_a, state_b, body_c, rows_last)
    )
    state_a = halve_line(line_blocks(total_a, 4, 16), at, 0)
    summed_b = halve_rest(state_b, at, 1)[0].reshape(-1, width)
    summed_c = scatter_outer(
        pick(body_c, at["outer"][0], 0),
        [pick(body_c, index, 0).astype(BF16) for index in at["outer"][1:]],
    )
    state_a, summed_b, summed_c = lax.optimization_barrier((state_a, summed_b, summed_c))
    summed_a, summed_v = halve_rest(state_a, at, 1)
    rows_out, summed_v = from_images(rows_last, at, summed_v)
    summed_a = summed_a.reshape(-1, width)
    grads = (
        from_columns(summed_a[: 3 * rows], rows),
        summed_a[3 * rows :],
        from_columns(summed_b, rows),
        summed_c,
        *own_slots(summed_v, lens, at),
    )
    return (rows_out[None, :, None], *[member[None] for member in grads])


def solution(mesh):
    sharded = P("section", ("dp", "seq"), None)
    vector = P("section", ("dp", "seq"))
    images = P("section", None, "dp", "seq", None)
    grads = (sharded, sharded, sharded, sharded, vector, vector, vector)
    return jax.shard_map(
        on_device,
        mesh=mesh,
        in_specs=(images, P(None, "dp", None), *grads),
        out_specs=(images, *grads),
        check_vma=False,
    )
```

```python
import functools
import math
import jax
import jax.numpy as jnp
import numpy as np
from jax import lax
from jax.experimental import pallas as pl
from jax.experimental.pallas import tpu as pltpu
from jax.sharding import PartitionSpec as P

HEADS = 6
norm_eps = 1e-06
F32 = jnp.float32
BF16 = jnp.bfloat16


def mul(left, right, left_dim=1, right_dim=0):
    return lax.dot_general(
        left, right, (((left_dim,), (right_dim,)), ((), ())), preferred_element_type=F32
    )


def total_of(rows):
    return jnp.sum(rows, axis=0, keepdims=True)


def norm_parts(rows_in):
    centre = jnp.mean(rows_in, axis=-1, keepdims=True)
    centred = rows_in - centre
    spread = jnp.mean(centred * centred, axis=-1, keepdims=True)
    scale = lax.rsqrt(spread + norm_eps)
    return centred * scale, scale


def norm_grad(grad, gain, unit, scale):
    scaled = grad * gain
    inner = jnp.mean(scaled * unit, axis=-1, keepdims=True)
    return scale * (scaled - jnp.mean(scaled, axis=-1, keepdims=True) - unit * inner)


def gelu_cdf(hidden):
    return 0.5 + 0.5 * lax.erf(hidden * math.sqrt(0.5))


def row_of(vec_ref, index):
    return vec_ref[index : index + 1, :]


def head_halves(head_dim):
    lane = lax.broadcasted_iota(jnp.int32, (1, 128), 1)
    first_half = (lane < head_dim).astype(BF16)
    return (first_half, 1 - first_half)


def attend_forward(x_ref, mask_ref, wa_ref, vec_ref, refs, mid_ref):
    q_s, k_s, v_s, vt_s, ot_s, kt_s, p_s = refs
    own = q_s.shape[1]
    width = x_ref.shape[1]
    pairs = k_s.shape[0]
    head_dim = width // HEADS
    mask = mask_ref[:, :1]
    masked = x_ref[...].astype(F32) * mask
    unit, _ = norm_parts(masked)
    normed = (unit * row_of(vec_ref, 0) + row_of(vec_ref, 2)).astype(BF16)
    queries = (mul(normed[:own], wa_ref[0]) + row_of(vec_ref, 4)).astype(BF16)
    queries = (queries.astype(F32) * head_dim ** (-0.5)).astype(BF16)
    keys = mul(normed, wa_ref[1]).astype(BF16)
    values = (mul(normed, wa_ref[2]) + row_of(vec_ref, 5)).astype(BF16)
    for j in range(pairs):
        lanes = slice(j * 128, (j + 1) * 128)
        q_s[j] = queries[:, lanes]
        k_s[j] = keys[:, lanes]
        v_s[j] = values[:, lanes]
        vt_s[j] = values[:, lanes].T
        if kt_s is not None:
            kt_s[j] = keys[:, lanes].T
    halves = head_halves(head_dim)

    for j in range(pairs):
        bias = (mask_ref[:, :1] - 1.0) * 1e30
        for e in range(2):
            score = mul(k_s[j], q_s[j] * halves[e], 1, 1) + bias
            top = jnp.max(score, axis=0, keepdims=True)
            expo = jnp.exp(score - top)
            probs = (expo * (1.0 / total_of(expo))).astype(BF16)
            rows = slice(e * head_dim, (e + 1) * head_dim)
            ot_s[j, rows, :] = mul(vt_s[j, rows, :], probs).astype(BF16)
            if p_s is not None:
                p_s[2 * j + e] = probs

    attended = jnp.concatenate([ot_s[j].T for j in range(pairs)], axis=1)
    mid_ref[...] = masked[:own] + mul(attended, wa_ref[3]) + row_of(vec_ref, 6)


def gelu_slope(hidden, cdf):
    return cdf + hidden * jnp.exp(-0.5 * hidden * hidden) * (1.0 / math.sqrt(2 * math.pi))


def feed_forward(mid_ref, mask_ref, w1_ref, w2_ref, vec_ref, c_s, acc_s, stored, y_ref):
    own, width = mid_ref.shape
    unit, _ = norm_parts(mid_ref[...])
    c_s[...] = (unit * row_of(vec_ref, 1) + row_of(vec_ref, 3)).astype(BF16)
    acc_s[...] = jnp.zeros_like(acc_s)

    @pl.loop(0, w1_ref.shape[0])
    def _(k):
        hidden = mul(c_s[...], w1_ref[k]) + vec_ref[pl.ds(8 + k, 1), :]
        cdf = gelu_cdf(hidden)
        active = (hidden * cdf).astype(BF16)
        if stored is not None:
            stored[0][k] = active
            stored[1][k] = gelu_slope(hidden, cdf)
        rows = pl.ds(pl.multiple_of(k * width, 128), width)
        acc_s[...] += mul(active, w2_ref[rows, :])

    y_ref[...] = (
        (mid_ref[...] + acc_s[...] + row_of(vec_ref, 7)) * mask_ref[:own, :1]
    ).astype(BF16)


def feed_backward(
    mid_ref, mask_ref, dy_ref, w1_ref, w2_ref, vec_ref, c_s, acc_s, stored, gmid_ref, grads
):
    own, width = mid_ref.shape
    acc_s[...] = jnp.zeros_like(acc_s)
    g1_s, g2_s, gv_ref = grads or (None, None, None)

    @pl.loop(0, w1_ref.shape[0])
    def _(k):
        if stored is None:
            hidden = mul(c_s[...], w1_ref[k]) + vec_ref[pl.ds(8 + k, 1), :]
            slope = gelu_slope(hidden, gelu_cdf(hidden))
        else:
            slope = stored[1][k]
        grad_second = (dy_ref[...].astype(F32) * mask_ref[:own, :1]).astype(BF16)
        rows = pl.ds(pl.multiple_of(k * width, 128), width)
        grad_hidden = (mul(grad_second, w2_ref[rows, :], 1, 1) * slope).astype(BF16)
        acc_s[...] += mul(grad_hidden, w1_ref[k], 1, 1)
        if grads is not None:
            active = stored[0][k]
            g1_s[k] = mul(c_s[...], grad_hidden, 0, 0).astype(BF16)
            g2_s[rows, :] = mul(active, grad_second, 0, 0).astype(BF16)
            gv_ref[pl.ds(8 + k, 1), :] = total_of(grad_hidden.astype(F32))

    grad_y = dy_ref[...].astype(F32) * mask_ref[:own, :1]
    grad_c = acc_s[...]
    unit, scale = norm_parts(mid_ref[...])
    grad_mid = grad_y + norm_grad(grad_c, row_of(vec_ref, 1), unit, scale)
    gmid_ref[...] = grad_mid
    if grads is not None:
        gv_ref[1:2, :] = total_of(grad_c * unit)
        gv_ref[3:4, :] = total_of(grad_c)
        gv_ref[6:7, :] = total_of(grad_mid.astype(BF16).astype(F32))
        gv_ref[7:8, :] = total_of(grad_y.astype(BF16).astype(F32))


def attend_backward(x_ref, mask_ref, wa_ref, vec_ref, kept, scratch, gmid_ref, du_ref, grads):
    q_s, k_s, v_s, ot_s, kt_s, p_s = kept
    do_s, dq_s, dk_s, dv_s = scratch
    own, width = gmid_ref.shape
    pairs = do_s.shape[0]
    head_dim = width // HEADS
    grad_branch = gmid_ref[...].astype(BF16)
    grad_att = mul(grad_branch, wa_ref[3], 1, 1).astype(BF16)
    for j in range(pairs):
        do_s[j] = grad_att[:, j * 128 : (j + 1) * 128]
    if grads is not None:
        ga_s, gv_ref = grads
        for j in range(pairs):
            ga_s[3, j * 128 : (j + 1) * 128, :] = mul(ot_s[j], grad_branch).astype(BF16)
    halves = head_halves(head_dim)

    for j in range(pairs):
        grad_k = None
        for e in range(2):
            half_do = do_s[j] * halves[e]
            half_q = q_s[j] * halves[e]
            grad_p = mul(v_s[j], half_do, 1, 1)
            probs_low = p_s[2 * j + e]
            probs = probs_low.astype(F32)
            row_dot = total_of(probs * grad_p)
            grad_s = (probs * (grad_p - row_dot)).astype(BF16)
            rows = slice(e * head_dim, (e + 1) * head_dim)
            dq_s[j, rows, :] = (mul(kt_s[j, rows, :], grad_s) * head_dim ** (-0.5)).astype(BF16)
            part_k = mul(grad_s, half_q)
            part_v = mul(probs_low, half_do)
            grad_k, grad_v = (part_k, part_v) if grad_k is None else (grad_k + part_k, grad_v + part_v)
        dk_s[j] = grad_k.astype(BF16)
        dv_s[j] = grad_v.astype(BF16)

    grad_q = jnp.concatenate([dq_s[j].T for j in range(pairs)], axis=1)
    grad_k = jnp.concatenate([dk_s[j] for j in range(pairs)], axis=1)
    grad_v = jnp.concatenate([dv_s[j] for j in range(pairs)], axis=1)
    mask = mask_ref[:, :1]
    unit, scale = norm_parts(x_ref[...].astype(F32) * mask)
    if grads is not None:
        normed = (unit * row_of(vec_ref, 0) + row_of(vec_ref, 2)).astype(BF16)
        ga_s[0] = mul(normed[:own], grad_q, 0, 0).astype(BF16)
        turned = normed.T
        ga_s[1] = mul(turned, grad_k).astype(BF16)
        ga_s[2] = mul(turned, grad_v).astype(BF16)
        gv_ref[4:5, :] = total_of(grad_q.astype(F32))
        gv_ref[5:6, :] = total_of(grad_v.astype(F32))
    grad_n = mul(grad_k, wa_ref[1], 1, 1) + mul(grad_v, wa_ref[2], 1, 1)
    grad_n = jnp.concatenate([grad_n[:own] + mul(grad_q, wa_ref[0], 1, 1), grad_n[own:]], axis=0)
    if grads is not None:
        gv_ref[0:1, :] = total_of(grad_n * unit)
        gv_ref[2:3, :] = total_of(grad_n)
    grad_u = norm_grad(grad_n, row_of(vec_ref, 0), unit, scale)
    grad_u = jnp.concatenate([grad_u[:own] + gmid_ref[...], grad_u[own:]], axis=0)
    du_ref[...] = (grad_u * mask).astype(BF16)


def pack_kernel(place_ref, qkv_ref, out_ref, fc1_ref, fc2_ref, gains_ref, shifts_ref, bias_ref, a_ref, b_ref, c_ref):
    rows, width = out_ref.shape
    index = place_ref[3]

    def columns(ref, count):
        wide = ref[...].astype(F32)
        return [wide[:, s * width : (s + 1) * width] for s in range(count)]

    lane = lax.broadcasted_iota(jnp.int32, (1, width), 1)
    row = lax.broadcasted_iota(jnp.int32, (16, width), 0)
    tail, base = jnp.zeros((16, width), F32), 0
    for ref, used in ((gains_ref, 2), (shifts_ref, 6), (bias_ref, 4)):
        length = ref.shape[1]
        start = index * length
        first, offset = start // width, lax.rem(start, width)
        spread = jnp.concatenate(
            [ref[...].astype(F32), jnp.zeros((1, width - length), F32)], axis=1
        )
        spread = pltpu.roll(jnp.broadcast_to(spread, (8, width)), offset, 1)[:1]
        target = base + first + jnp.where(lane < offset, 1, 0)
        tail = tail + jnp.where(row == target, spread, 0.0)
        base += used
    blocks = columns(qkv_ref, 3) + [out_ref[...].astype(F32), tail]
    a_ref[...] = jnp.concatenate(blocks, axis=0).astype(BF16)
    b_ref[...] = jnp.concatenate(columns(fc1_ref, 4), axis=0).astype(BF16)
    c_ref[...] = fc2_ref[...]


def finish_kernel(place_ref, body_ref, rest_ref, came_ref, qkv_ref, out_ref, *vector_refs):
    rows, width = out_ref.shape[1:]
    index = place_ref[3]
    count = 4 * rows
    summed = body_ref[...] + came_ref[:count, :].astype(F32)
    vectors = rest_ref[...] + came_ref[count:, :].astype(F32)
    for s in range(3):
        qkv_ref[0, :, s * width : (s + 1) * width] = summed[s * rows : (s + 1) * rows]
    out_ref[0] = summed[3 * rows :]
    lane = lax.broadcasted_iota(jnp.int32, (8, width), 1)
    row = lax.broadcasted_iota(jnp.int32, (16, width), 0)
    base = 0
    for ref, used in zip(vector_refs, (2, 6, 4)):
        length = ref.shape[1]
        first, offset = index * length // width, lax.rem(index * length, width)

        def turned(which):
            picked = total_of(jnp.where(row == which, vectors, 0.0))
            picked = jnp.broadcast_to(picked, (8, width))
            return pltpu.roll(picked, lax.rem(width - offset, width), 1)

        whole = jnp.where(lane < width - offset, turned(base + first), turned(base + first + 1))
        ref[...] = whole[:1, :length]
        base += used


def piece_groups(place_ref, mine, theirs, turns):
    outer, core, line = place_ref[0], place_ref[1], place_ref[2]
    count = mine[0].shape[0]
    for side, members in enumerate((mine, theirs)):
        for turn in range(turns):
            index = lax.rem(outer + (turns - turn), turns) * 2 + (core if side == 0 else 1 - core)
            yield index, [
                members[turn][turned_bits(line ^ z, count)].astype(F32) for z in range(count)
            ]


def halved_groups(place_ref, mine, theirs, turns):
    outer, core, line = place_ref[0], place_ref[1], place_ref[2]
    count = mine[0].shape[0] // turns * 2
    for side, (even, odd) in enumerate((mine, theirs)):
        for turn in range(turns):
            index = lax.rem(outer + (turns - turn), turns) * 2 + (core if side == 0 else 1 - core)
            blocks = []
            for z in range(count):
                entry = turned_bits((line ^ z) // 2, count // 2) * turns + turn
                blocks.append(jnp.where((line ^ z) % 2 == 0, even[entry], odd[entry]).astype(F32))
            yield index, blocks


def first_kernel(loose, rows, ins, outs, scratch):
    place_ref, x_ref, mask_ref = ins[:3]
    if loose:
        mine, theirs = ins[3 : 3 + loose], ins[3 + loose :]
        mid_ref, wa_out, vec_out = outs
        wa_ref, vec_ref = wa_out, vec_out
        vector = None
        for index, blocks in piece_groups(place_ref, mine, theirs, loose):
            span = rows * len(blocks)
            start = pl.multiple_of(index * span, 16)
            for s in range(4):
                group = jnp.concatenate([b[s * rows : (s + 1) * rows] for b in blocks], axis=0)
                wa_ref[s, pl.ds(start, span), :] = group.astype(BF16)
            for b in blocks:
                tail = b[4 * rows : 4 * rows + 16]
                vector = tail if vector is None else vector + tail
        vec_ref[...] = vector
    else:
        wa_ref, vec_ref = (member for member in ins[3:])
        (mid_ref,) = outs
    attend_forward(x_ref, mask_ref, wa_ref, vec_ref, (*scratch, None, None), mid_ref)


def second_kernel(loose, rows, ins, outs, scratch):
    place_ref, mid_ref, mask_ref, vec_ref = ins[:4]
    c_s, acc_s = scratch
    if loose:
        sets = [ins[4 : 4 + loose], ins[4 + loose : 4 + 2 * loose], ins[-4:-2], ins[-2:]]
        y_ref, w1_ref, w2_ref = outs
        for index, blocks in piece_groups(place_ref, sets[0], sets[1], loose):
            span = rows * len(blocks)
            start = pl.multiple_of(index * span, 16)
            for s in range(4):
                group = jnp.concatenate([b[s * rows : (s + 1) * rows] for b in blocks], axis=0)
                w1_ref[s, pl.ds(start, span), :] = group.astype(BF16)
        for index, blocks in halved_groups(place_ref, sets[2], sets[3], loose):
            span = 4 * rows * len(blocks)
            group = jnp.concatenate(blocks, axis=0)
            w2_ref[pl.ds(pl.multiple_of(index * span, 16), span), :] = group.astype(BF16)
    else:
        w1_ref, w2_ref = ins[4:]
        (y_ref,) = outs
    feed_forward(mid_ref, mask_ref, w1_ref, w2_ref, vec_ref, c_s, acc_s, None, y_ref)


def middle_kernel(ins, outs, scratch):
    x_ref, mask_ref, vec_ref, wa_ref, w1_ref, w2_ref, dy_ref = ins
    du_ref, mid_ref, c_s, *kept = outs
    vt_s, acc_s, gmid_s, *grad_scratch = scratch
    q_s, k_s, v_s, ot_s, kt_s, p_s = kept
    attend_forward(
        x_ref, mask_ref, wa_ref, vec_ref, (q_s, k_s, v_s, vt_s, ot_s, kt_s, p_s), mid_ref
    )
    unit, _ = norm_parts(mid_ref[...])
    c_s[...] = (unit * row_of(vec_ref, 1) + row_of(vec_ref, 3)).astype(BF16)
    feed_backward(
        mid_ref, mask_ref, dy_ref, w1_ref, w2_ref, vec_ref, c_s, acc_s, None, gmid_s, None
    )
    attend_backward(x_ref, mask_ref, wa_ref, vec_ref, kept, grad_scratch, gmid_s, du_ref, None)


def output_kernel(ins, outs, scratch):
    mid_ref, mask_ref, vec_ref, w1_ref, w2_ref = ins
    y_ref, active_ref, slope_ref = outs
    feed_forward(
        mid_ref, mask_ref, w1_ref, w2_ref, vec_ref, *scratch, (active_ref, slope_ref), y_ref
    )


def share_out(core, blocks_of, outer_count, start, size, kept_ref, sent_ref):
    for o in range(outer_count):
        even, odd = blocks_of(2 * o), blocks_of(2 * o + 1)
        kept_ref[o, start : start + size, :] = jnp.where(core == 0, even, odd)
        sent_ref[o, start : start + size, :] = jnp.where(core == 0, odd, even)


def feed_grad_kernel(ins, outs, scratch):
    place_ref, dy_ref, mid_ref, vec_ref, mask_ref, w1_ref, w2_ref, c_ref, active_ref, slope_ref = ins
    kept_ref, sent_ref, gmid_ref, gv_ref = outs
    acc_s, g1_s, g2_s = scratch
    gv_ref[...] = jnp.zeros_like(gv_ref)
    outer_count = kept_ref.shape[0]
    span = w1_ref.shape[1] // (2 * outer_count)
    feed_backward(
        mid_ref, mask_ref, dy_ref, w1_ref, w2_ref, vec_ref, c_ref, acc_s,
        (active_ref, slope_ref), gmid_ref, (g1_s, g2_s, gv_ref),
    )
    core = place_ref[1]
    for s in range(4):
        share_out(
            core, lambda d: g1_s[s, d * span : (d + 1) * span, :], outer_count,
            s * span, span, kept_ref, sent_ref,
        )
    share_out(
        core, lambda d: g2_s[4 * d * span : 4 * (d + 1) * span, :], outer_count,
        4 * span, 4 * span, kept_ref, sent_ref,
    )


def attend_grad_kernel(ins, outs, scratch):
    place_ref, gmid_in, wa_in, ot_in, v_in, q_in, kt_in, p_in, k_in, x_in, mask_in, vec_in, gv_in = ins
    du_ref, kept_ref, sent_ref = outs
    do_s, dq_s, dk_s, dv_s, ga_s, gv_s = scratch
    gmid_ref, wa_ref, ot_s = gmid_in, wa_in, ot_in
    outer_count = kept_ref.shape[0]
    span = wa_ref.shape[1] // (2 * outer_count)
    gv_s[...] = gv_in[...]
    attend_backward(
        x_in, mask_in, wa_ref, vec_in, (q_in, k_in, v_in, ot_s, kt_in, p_in),
        (do_s, dq_s, dk_s, dv_s), gmid_ref, du_ref, (ga_s, gv_s),
    )
    core = place_ref[1]
    for s in range(4):
        share_out(
            core, lambda d: ga_s[s, d * span : (d + 1) * span, :], outer_count,
            s * span, span, kept_ref, sent_ref,
        )
    tail = gv_s[...].astype(BF16)
    for o in range(outer_count):
        kept_ref[o, 4 * span :, :] = tail
        sent_ref[o, 4 * span :, :] = tail


def call(kernel, operands, results, scratch, flops, after=()):
    space = {"s": pltpu.SMEM, "v": pltpu.VMEM}

    def body(*refs):
        refs = list(refs[len(after) :])
        given, refs = refs[: len(operands)], refs[len(operands) :]
        kernel(given, refs[: len(results)], refs[len(results) :])

    return pl.pallas_call(
        body,
        out_shape=[jax.ShapeDtypeStruct(*result) for result in results],
        in_specs=[pl.BlockSpec(memory_space=pl.ANY)] * len(after)
        + [pl.BlockSpec(memory_space=space[kind]) for kind, _ in operands],
        out_specs=[pl.BlockSpec(memory_space=pltpu.VMEM)] * len(results),
        scratch_shapes=[pltpu.VMEM(*shape) for shape in scratch],
        compiler_params=pltpu.CompilerParams(vmem_limit_bytes=VMEM_LIMIT),
        cost_estimate=pl.CostEstimate(flops=flops, bytes_accessed=4 * 10**6, transcendentals=10**6),
    )(*after, *[array for _, array in operands])


def call_whole(kernel, operands, shapes, flops):
    def block(shape):
        return pl.BlockSpec(shape, lambda i: (0,) * len(shape))

    return pl.pallas_call(
        kernel,
        grid=(1,),
        out_shape=[jax.ShapeDtypeStruct(*shape) for shape in shapes],
        in_specs=[pl.BlockSpec(memory_space=pltpu.SMEM)]
        + [block(operand.shape) for operand in operands[1:]],
        out_specs=[block(shape[0]) for shape in shapes],
        cost_estimate=pl.CostEstimate(flops=flops, bytes_accessed=10**6, transcendentals=0),
    )(*operands)


VMEM_LIMIT = 24 * 1024 * 1024


def axis_sizes():
    return lax.axis_size("dp"), lax.axis_size("seq")


def places(lengths):
    dp_count, seq_count = axis_sizes()
    outer_count = dp_count // 2
    d, z = lax.axis_index("dp"), lax.axis_index("seq")
    o, index = d // 2, d * seq_count + z
    block = seq_count // 4

    def unsigned(value):
        return value.astype(jnp.uint32)

    return {
        "first": lax.axis_index("section") == 0,
        "operand": jnp.stack([o, d % 2, z, index]).astype(jnp.int32),
        "outer": [unsigned((o + k) % outer_count) for k in range(outer_count)],
                "bits": [
            (unsigned(z // step % 2), unsigned(1 - z // step % 2)) for step in reversed(line_steps())
        ],
        "even": z % 2 == 0,
        "micro": z // block // 2 == 0,
        "slots": [unsigned(index * length) for length in lengths],
    }


def pick(value, index, axis, rows=None):
    starts = [np.uint32(0)] * value.ndim
    starts[axis] = index
    sizes = list(value.shape)
    sizes[axis] = 1
    if rows is not None:
        starts[axis + 1], sizes[axis + 1] = np.uint32(rows[0]), rows[1] - rows[0]
    return lax.dynamic_slice(value, starts, sizes).reshape(sizes[:axis] + sizes[axis + 1 :])


def swap_core(value):
    return lax.ppermute(value, "dp", [(d, d ^ 1) for d in range(lax.axis_size("dp"))])


def turn_outer(value, steps):
    count = lax.axis_size("dp")
    return lax.ppermute(value, "dp", [(d, (d + 2 * steps) % count) for d in range(count)])


def turn_line(value, steps):
    count = lax.axis_size("seq")
    return lax.ppermute(value, "seq", [(z, (z + steps) % count) for z in range(count)])


def joint_permute(value, moves):
    seq_count = lax.axis_size("seq")
    pairs = [(a[0] * seq_count + a[1], b[0] * seq_count + b[1]) for a, b in moves]
    return lax.ppermute(value, ("dp", "seq"), pairs)


def line_steps():
    count, steps = lax.axis_size("seq"), []
    while count > 1:
        count //= 2
        steps.append(count)
    return steps


def cross_line(value, distance):
    count = lax.axis_size("seq")
    return lax.ppermute(value, "seq", [(z, z ^ distance) for z in range(count)])


def gather_step(pieces, step):
    return jnp.concatenate([pieces, cross_line(pieces, line_steps()[step])])


def gather_from(pieces, step, stop=None):
    for later in range(step, len(line_steps()) if stop is None else stop):
        pieces = gather_step(pieces, later)
    return pieces


def turned_bits(value, count):
    result, low, high = value * 0, 1, count // 2
    while high:
        result = result + (value // high) % 2 * low
        low, high = low * 2, high // 2
    return result


def gather_outer(stacked):
    return [stacked] + [turn_outer(stacked, k) for k in range(1, lax.axis_size("dp") // 2)]


def assemble(mine, theirs):
    outer_count, seq_count = len(mine), lax.axis_size("seq")
    d, z = lax.axis_index("dp"), lax.axis_index("seq")
    o, c = d // 2, d % 2
    turned = jnp.stack([jnp.stack(mine), jnp.stack(theirs)])
    sides = (jnp.arange(2) + c) % 2
    outers = (o - jnp.arange(outer_count)) % outer_count
    lines = turned_bits(z ^ jnp.arange(seq_count), seq_count)
    ordered = turned[sides][:, outers][:, :, lines]
    return ordered.transpose(1, 0, 2, 3, 4).reshape((-1,) + mine[0].shape[1:])


def scatter_core(kept, came, at, rows):
    def both(index):
        mine, theirs = (
            pick(member, index, 0, rows).astype(F32) for member in (kept, came)
        )
        return mine + theirs

    return both(at["outer"][0]), [both(index).astype(BF16) for index in at["outer"][1:]]


def scatter_outer(total, sent):
    for k, member in enumerate(sent):
        total = total + turn_outer(member, k + 1).astype(F32)
    return total


def line_blocks(total, lead, tail=0):
    body, rest = total[: total.shape[0] - tail], total[total.shape[0] - tail :]
    return body.reshape(lead, lax.axis_size("seq"), -1, total.shape[1]), rest


def halve_parts(state, at, step):
    body, rest = state
    mine, other = at["bits"][step]
    lead, count, _, width = body.shape
    halves = body.reshape(lead, count // 2, 2, -1, width)
    body, sent = pick(halves, mine, 2), pick(halves, other, 2).reshape(-1, width)
    if rest.shape[0]:
        sent = jnp.concatenate([sent, rest])
    return (body, rest), sent.astype(BF16)


def halve_sum(state, sent, step):
    body, rest = state
    came = cross_line(sent, line_steps()[-1 - step]).astype(F32)
    tail = rest.shape[0]
    body = body + came[: came.shape[0] - tail].reshape(body.shape)
    return body, rest + came[came.shape[0] - tail :]


def halve_line(state, at, step):
    return halve_sum(*halve_parts(state, at, step), step)


def halve_rest(state, at, step):
    for later in range(step, len(at["bits"])):
        state = halve_line(state, at, later)
    return state


def image_moves(step):
    dp_count, seq_count = axis_sizes()
    block = seq_count // 4
    moves = []
    for d in range(dp_count):
        for z in range(seq_count):
            micro = (step + z) % 2
            rank = z // 2
            target = (d - d % 2 + rank % 2, (2 * micro + d % 2) * block + rank // 2)
            moves.append(((d, z), target))
    return moves


def to_images(blocks, at):
    arrived = []
    for step in range(2):
        sent = jnp.where(at["even"], blocks[step], blocks[1 - step])
        arrived.append(joint_permute(sent, image_moves(step)))
    low = jnp.where(at["micro"], arrived[0], arrived[1])
    high = jnp.where(at["micro"], arrived[1], arrived[0])
    return jnp.concatenate([low, high], axis=0)


def from_images(rows_own, at, after):
    half = rows_own.shape[0] // 2
    low, high = rows_own[:half], rows_own[half:]
    arrived = []
    for step in range(2):
        sent = jnp.where(at["micro"], *((low, high) if step == 0 else (high, low)))
        arrived.append(joint_permute(sent, [(b, a) for a, b in image_moves(step)]))
    after, *arrived = lax.optimization_barrier((after, *arrived))
    return jnp.stack([jnp.where(at["even"], arrived[m], arrived[1 - m]) for m in range(2)]), after


def group_members():
    block = lax.axis_size("seq") // 4
    return [(turn, flip) for turn in range(block) for flip in range(2)][1:]


def group_moves(turn, flip):
    dp_count, seq_count = axis_sizes()
    block = seq_count // 4
    moves = []
    for d in range(dp_count):
        for z in range(seq_count):
            base = z - z % block
            moves.append(((d ^ flip, base + (z % block + turn) % block), (d, z)))
    return moves


def gather_group(own_rows):
    arrived = [joint_permute(own_rows, group_moves(*member)) for member in group_members()]
    return jnp.concatenate([own_rows] + arrived, axis=0)


def scatter_group(partial, own):
    total = partial[:own].astype(F32)
    for place, member in enumerate(group_members()):
        sent = partial[(place + 1) * own : (place + 2) * own]
        back = [(b, a) for a, b in group_moves(*member)]
        total = total + joint_permute(sent, back).astype(F32)
    return total.astype(BF16)


def slot_mask(lengths, slot_count):
    block = lax.axis_size("seq") // 4
    d, z = lax.axis_index("dp"), lax.axis_index("seq")
    c, group = d % 2, z // block
    theirs = swap_core(lengths[:, 0])
    counts = jnp.where(group % 2 == c, lengths[:, 0], theirs)
    counts = jnp.where(group // 2 == 0, counts[0], counts[1])
    places = jnp.arange(slot_count, dtype=jnp.int32)
    parts = []
    for turn, flip in [(0, 0)] + group_members():
        rank = (z % block + turn) % block * 2 + (c ^ flip)
        picked = lax.dynamic_slice_in_dim(counts, 2 * rank, 2, 0)
        parts.append((places[None, :] < picked[:, None]).astype(F32).reshape(-1, 1))
    return jnp.broadcast_to(jnp.concatenate(parts, axis=0), (len(parts) * 2 * slot_count, 128))


def to_section(value, steps):
    return lax.ppermute(value, "section", [(0, 1)] if steps == 1 else [(1, 0)])


def vector_slots(members, width):
    index = lax.axis_index("dp") * lax.axis_size("seq") + lax.axis_index("seq")
    count = lax.axis_size("dp") * lax.axis_size("seq")
    parts = []
    for member in members:
        length = member.shape[0]
        spread = jnp.zeros((count * length,), BF16)
        spread = lax.dynamic_update_slice_in_dim(spread, member, index * length, 0)
        parts.append(spread.reshape(-1, width))
    parts.append(jnp.zeros((4, width), BF16))
    return jnp.concatenate(parts, axis=0)


def own_slots(vectors, lengths, at):
    parts, start = [], 0
    for length, used, place in zip(lengths, (2, 6, 4), at["slots"]):
        flat = vectors[start : start + used].reshape(-1)
        parts.append(lax.dynamic_slice_in_dim(flat, place, length, 0))
        start += used
    return parts


def by_column(member, width):
    rows = member.shape[0]
    return member.reshape(rows, -1, width).transpose(1, 0, 2).reshape(-1, width)


def from_columns(block, rows):
    width = block.shape[1]
    return block.reshape(-1, rows, width).transpose(1, 0, 2).reshape(rows, -1)


def on_device(boundary, lengths, w_qkv, w_out, w_fc1, w_fc2, gains, shifts, fc1_bias):
    dp_count, seq_count = axis_sizes()
    outer_count = dp_count // 2
    lens = (gains.shape[1], shifts.shape[1], fc1_bias.shape[1])
    at = places(lens)
    place = at["operand"]
    slot_count = boundary.shape[3]
    own = 2 * slot_count
    total = lengths.shape[2] * slot_count
    rows, width = w_out.shape[1:]
    hidden = rows * 4 * dp_count * seq_count
    pairs = width // 128
    span = width // dp_count
    loose = outer_count if rows % 8 == 0 else 0
    if loose:
        piece_a, piece_b, piece_c = call_whole(
            pack_kernel,
            [place, w_qkv[0], w_out[0], w_fc1[0], w_fc2[0], gains, shifts, fc1_bias],
            [((4 * rows + 16, width), BF16)] + [((4 * rows, width), BF16)] * 2,
            10**9,
        )
    else:
        tail = vector_slots((gains[0], shifts[0], fc1_bias[0]), width)
        piece_a = jnp.concatenate([by_column(w_qkv[0], width), w_out[0], tail])
        piece_b, piece_c = by_column(w_fc1[0], width), w_fc2[0]
    own_start = to_images(boundary[0, :, 0], at)
    piece_a, at = lax.optimization_barrier((piece_a, at))
    half_a = gather_step(piece_a[None], 0)
    near_c = jnp.stack(gather_outer(piece_c))
    half_a, piece_b, near_c, own_start = lax.optimization_barrier(
        (half_a, piece_b, near_c, own_start)
    )
    line_a = gather_from(half_a, 1)
    half_b = gather_step(piece_b[None], 0)
    line_a, half_b, near_c = lax.optimization_barrier((line_a, half_b, near_c))
    mine_a = gather_outer(line_a)
    line_b = gather_from(half_b, 1)
    half_c = gather_step(near_c, 0)
    line_b, half_c, *mine_a = lax.optimization_barrier((line_b, half_c, *mine_a))
    mine_b = gather_outer(line_b)
    half_c = gather_from(half_c, 1, len(line_steps()) - 1)
    mine_c = [half_c, cross_line(half_c, line_steps()[-1])]
    mask = slot_mask(lengths, slot_count)
    all_start = gather_group(own_start)
    theirs_a = [swap_core(member) for member in mine_a]

    w_shape = ((4, width, width), BF16)
    tall_shape = ((hidden, width), BF16)
    vec_shape = ((16, width), F32)
    mid_shape = ((own, width), F32)
    low_shape = ((own, width), BF16)
    all_shape = ((total, width), BF16)
    q_shape = ((pairs, own, 128), BF16)
    k_shape = ((pairs, total, 128), BF16)
    qt_shape = ((pairs, 128, own), BF16)
    kt_shape = ((pairs, 128, total), BF16)
    p_shape = ((HEADS, total, own), BF16)
    h_shape = ((4, own, width), F32)
    active_shape = ((4, own, width), BF16)
    shared_b = ((outer_count, 8 * span, width), BF16)
    shared_a = ((outer_count, 4 * span + 16, width), BF16)

    head_scratch = [q_shape, k_shape, k_shape, kt_shape, qt_shape]
    if loose:
        middle, w_a, vectors = call(
            functools.partial(first_kernel, loose, rows),
            [("s", place), ("v", all_start), ("v", mask)]
            + [("v", member) for member in (*mine_a, *theirs_a)],
            [mid_shape, w_shape, vec_shape],
            head_scratch, 10**9, [line_b],
        )
        middle, mine_c[1], *mine_b[1:] = lax.optimization_barrier(
            (middle, mine_c[1], *mine_b[1:])
        )
        theirs_b = [swap_core(member) for member in mine_b]
        theirs_c = [swap_core(member) for member in mine_c]
        first_out, w_1, w_2 = call(
            functools.partial(second_kernel, loose, rows),
            [("s", place), ("v", middle), ("v", mask), ("v", vectors)]
            + [("v", member) for member in (*mine_b, *theirs_b, *mine_c, *theirs_c)],
            [low_shape, w_shape, tall_shape],
            [low_shape, mid_shape], 10**9,
        )
    else:
        theirs_b = [swap_core(member) for member in mine_b]
        theirs_c = [swap_core(member) for member in mine_c]
        ordered = assemble(mine_a, theirs_a)
        w_a = ordered[:, : 4 * rows].reshape(-1, 4, rows, width).transpose(1, 0, 2, 3)
        w_a = w_a.reshape(4, width, width)
        vectors = jnp.sum(ordered[:, 4 * rows :].astype(F32), axis=0)
        w_1 = assemble(mine_b, theirs_b).reshape(-1, 4, rows, width).transpose(1, 0, 2, 3)
        w_1 = w_1.reshape(4, width, width)
        apart = [
            [
                jnp.concatenate(member).reshape(seq_count, outer_count, -1, width)[:, k]
                for k in range(outer_count)
            ]
            for member in (mine_c, theirs_c)
        ]
        w_2 = assemble(*apart).reshape(hidden, width)
        (middle,) = call(
            functools.partial(first_kernel, loose, rows),
            [("s", place), ("v", all_start), ("v", mask), ("v", w_a), ("v", vectors)],
            [mid_shape], head_scratch, 10**9,
        )
        (first_out,) = call(
            functools.partial(second_kernel, loose, rows),
            [("s", place), ("v", middle), ("v", mask), ("v", vectors), ("v", w_1), ("v", w_2)],
            [low_shape], [low_shape, mid_shape], 10**9,
        )
    arrived = gather_group(to_section(first_out, 1))
    layer_in = jnp.where(at["first"], all_start, arrived)
    grad_scratch = [q_shape, qt_shape, k_shape, k_shape]
    saved = [mid_shape, low_shape, q_shape, k_shape, k_shape, qt_shape, kt_shape, p_shape]
    partial, middle, normed, q, k, v, ot, kt, p = call(
        middle_kernel,
        [("v", layer_in)]
        + [("v", member) for member in (mask, vectors, w_a, w_1, w_2, own_start)],
        [all_shape, *saved],
        [kt_shape, mid_shape, mid_shape, *grad_scratch], 4 * 10**9,
    )
    sent_back = scatter_group(partial, own)
    returned = to_section(sent_back, -1)
    layer_out, active, slope = call(
        output_kernel,
        [("v", member) for member in (middle, mask, vectors, w_1, w_2)],
        [low_shape, active_shape, h_shape], [low_shape, mid_shape], 2 * 10**9, [sent_back],
    )
    grad_out = jnp.where(at["first"], returned, own_start)
    kept_b, sent_b, grad_mid, grad_vectors = call(
        feed_grad_kernel,
        [("s", place), ("v", grad_out)]
        + [
            ("v", member)
            for member in (middle, vectors, mask, w_1, w_2, normed, active, slope)
        ],
        [shared_b, shared_b, mid_shape, vec_shape],
        [mid_shape, w_shape, tall_shape], 2 * 10**9,
    )
    came_b = swap_core(sent_b)
    both_c = kept_b[:, 4 * span :].astype(F32) + came_b[:, 4 * span :].astype(F32)
    state_c, sent_c = halve_parts(line_blocks(both_c.reshape(-1, width), outer_count), at, 0)
    kept_b, sent_b = scatter_core(kept_b, came_b, at, (0, 4 * span))
    partial, kept_a, sent_a = call(
        attend_grad_kernel,
        [("s", place)]
        + [
            ("v", member)
            for member in (
                grad_mid, w_a, ot, v, q, kt, p, k, layer_in, mask, vectors, grad_vectors
            )
        ],
        [all_shape, shared_a, shared_a],
        [*grad_scratch, w_shape, vec_shape], 10**10, [*sent_b, sent_c],
    )

    total_b = scatter_outer(kept_b, sent_b)
    state_c = halve_sum(state_c, sent_c, 0)
    total_b, state_c, sent_a, partial = lax.optimization_barrier(
        (total_b, state_c, sent_a, partial)
    )
    kept_a, sent_a = scatter_core(kept_a, swap_core(sent_a), at, None)
    grad_in = scatter_group(partial, own)
    total_b, state_c, *sent_a = lax.optimization_barrier((total_b, state_c, *sent_a))
    total_a = scatter_outer(kept_a, sent_a)
    state_b = halve_line(line_blocks(total_b, 4), at, 0)
    body_c = halve_rest(state_c, at, 1)[0].reshape(outer_count, -1, width)
    rows_last = jnp.where(at["first"], grad_in, layer_out)
    total_a, state_b, body_c = lax.optimization_barrier((total_a, state_b, body_c))
    state_a = halve_line(line_blocks(total_a, 4, 16), at, 0)
    summed_b = halve_rest(state_b, at, 1)[0].reshape(-1, width)
    summed_c = scatter_outer(
        pick(body_c, at["outer"][0], 0),
        [pick(body_c, index, 0).astype(BF16) for index in at["outer"][1:]],
    )
    state_a, summed_b, summed_c = lax.optimization_barrier((state_a, summed_b, summed_c))
    last = len(at["bits"]) - 1
    for step in range(1, last):
        state_a = halve_line(state_a, at, step)
    (body, rest), sent_a = halve_parts(state_a, at, last)
    sent_a, body, rows_last = lax.optimization_barrier((sent_a, body, rows_last))
    if loose:
        came = cross_line(sent_a, line_steps()[-1 - last])
        finished = call_whole(
            finish_kernel,
            [place, body.reshape(-1, width), rest, came],
            [((1, rows, 3 * width), F32), ((1, rows, width), F32)]
            + [((1, length), F32) for length in lens],
            10**10,
        )
        rows_out, _ = from_images(rows_last, at, came)
    else:
        summed_a, summed_v = halve_sum((body, rest), sent_a, last)
        rows_out, summed_v = from_images(rows_last, at, summed_v)
        summed_a = summed_a.reshape(-1, width)
        finished = [
            member[None]
            for member in (
                from_columns(summed_a[: 3 * rows], rows),
                summed_a[3 * rows :],
                *own_slots(summed_v, lens, at),
            )
        ]
    grads = (*finished[:2], from_columns(summed_b, rows)[None], summed_c[None], *finished[2:])
    return (rows_out[None, :, None], *grads)


def solution(mesh):
    sharded = P("section", ("dp", "seq"), None)
    vector = P("section", ("dp", "seq"))
    images = P("section", None, "dp", "seq", None)
    grads = (sharded, sharded, sharded, sharded, vector, vector, vector)
    return jax.shard_map(
        on_device,
        mesh=mesh,
        in_specs=(images, P(None, "dp", None), *grads),
        out_specs=(images, *grads),
        check_vma=False,
    )
```

```python
import functools
import math
import jax
import jax.numpy as jnp
import numpy as np
from jax import lax
from jax.experimental import pallas as pl
from jax.experimental.pallas import tpu as pltpu
from jax.sharding import PartitionSpec as P

HEADS = 6
norm_eps = 1e-06
F32 = jnp.float32
BF16 = jnp.bfloat16


def mul(left, right, left_dim=1, right_dim=0):
    return lax.dot_general(
        left, right, (((left_dim,), (right_dim,)), ((), ())), preferred_element_type=F32
    )


def total_of(rows):
    return jnp.sum(rows, axis=0, keepdims=True)


def norm_parts(rows_in):
    centre = jnp.mean(rows_in, axis=-1, keepdims=True)
    centred = rows_in - centre
    spread = jnp.mean(centred * centred, axis=-1, keepdims=True)
    scale = lax.rsqrt(spread + norm_eps)
    return centred * scale, scale


def norm_grad(grad, gain, unit, scale):
    scaled = grad * gain
    inner = jnp.mean(scaled * unit, axis=-1, keepdims=True)
    return scale * (scaled - jnp.mean(scaled, axis=-1, keepdims=True) - unit * inner)


def gelu_cdf(hidden):
    return 0.5 + 0.5 * lax.erf(hidden * math.sqrt(0.5))


def row_of(vec_ref, index):
    return vec_ref[index : index + 1, :]


def head_halves(head_dim):
    lane = lax.broadcasted_iota(jnp.int32, (1, 128), 1)
    first_half = (lane < head_dim).astype(BF16)
    return (first_half, 1 - first_half)


def attend_forward(x_ref, mask_ref, wa_ref, vec_ref, refs, mid_ref):
    q_s, k_s, v_s, vt_s, ot_s, kt_s, p_s = refs
    own = q_s.shape[1]
    width = x_ref.shape[1]
    pairs = k_s.shape[0]
    head_dim = width // HEADS
    mask = mask_ref[:, :1]
    masked = x_ref[...].astype(F32) * mask
    unit, _ = norm_parts(masked)
    normed = (unit * row_of(vec_ref, 0) + row_of(vec_ref, 2)).astype(BF16)
    queries = (mul(normed[:own], wa_ref[0]) + row_of(vec_ref, 4)).astype(BF16)
    queries = (queries.astype(F32) * head_dim ** (-0.5)).astype(BF16)
    keys = mul(normed, wa_ref[1]).astype(BF16)
    values = (mul(normed, wa_ref[2]) + row_of(vec_ref, 5)).astype(BF16)
    for j in range(pairs):
        lanes = slice(j * 128, (j + 1) * 128)
        q_s[j] = queries[:, lanes]
        k_s[j] = keys[:, lanes]
        v_s[j] = values[:, lanes]
        vt_s[j] = values[:, lanes].T
        if kt_s is not None:
            kt_s[j] = keys[:, lanes].T
    halves = head_halves(head_dim)

    for j in range(pairs):
        bias = (mask_ref[:, :1] - 1.0) * 1e30
        for e in range(2):
            score = mul(k_s[j], q_s[j] * halves[e], 1, 1) + bias
            top = jnp.max(score, axis=0, keepdims=True)
            expo = jnp.exp(score - top)
            probs = (expo * (1.0 / total_of(expo))).astype(BF16)
            rows = slice(e * head_dim, (e + 1) * head_dim)
            ot_s[j, rows, :] = mul(vt_s[j, rows, :], probs).astype(BF16)
            if p_s is not None:
                p_s[2 * j + e] = probs

    attended = jnp.concatenate([ot_s[j].T for j in range(pairs)], axis=1)
    mid_ref[...] = masked[:own] + mul(attended, wa_ref[3]) + row_of(vec_ref, 6)


def gelu_slope(hidden, cdf):
    return cdf + hidden * jnp.exp(-0.5 * hidden * hidden) * (1.0 / math.sqrt(2 * math.pi))


def feed_forward(mid_ref, mask_ref, w1_ref, w2_ref, vec_ref, c_s, acc_s, stored, y_ref):
    own, width = mid_ref.shape
    unit, _ = norm_parts(mid_ref[...])
    c_s[...] = (unit * row_of(vec_ref, 1) + row_of(vec_ref, 3)).astype(BF16)
    acc_s[...] = jnp.zeros_like(acc_s)

    @pl.loop(0, w1_ref.shape[0])
    def _(k):
        hidden = mul(c_s[...], w1_ref[k]) + vec_ref[pl.ds(8 + k, 1), :]
        cdf = gelu_cdf(hidden)
        active = (hidden * cdf).astype(BF16)
        if stored is not None:
            stored[0][k] = active
            stored[1][k] = gelu_slope(hidden, cdf)
        rows = pl.ds(pl.multiple_of(k * width, 128), width)
        acc_s[...] += mul(active, w2_ref[rows, :])

    y_ref[...] = (
        (mid_ref[...] + acc_s[...] + row_of(vec_ref, 7)) * mask_ref[:own, :1]
    ).astype(BF16)


def feed_backward(
    mid_ref, mask_ref, dy_ref, w1_ref, w2_ref, vec_ref, c_s, acc_s, stored, gmid_ref, grads
):
    own, width = mid_ref.shape
    acc_s[...] = jnp.zeros_like(acc_s)
    g1_s, g2_s, gv_ref = grads or (None, None, None)

    @pl.loop(0, w1_ref.shape[0])
    def _(k):
        if stored is None:
            hidden = mul(c_s[...], w1_ref[k]) + vec_ref[pl.ds(8 + k, 1), :]
            slope = gelu_slope(hidden, gelu_cdf(hidden))
        else:
            slope = stored[1][k]
        grad_second = (dy_ref[...].astype(F32) * mask_ref[:own, :1]).astype(BF16)
        rows = pl.ds(pl.multiple_of(k * width, 128), width)
        grad_hidden = (mul(grad_second, w2_ref[rows, :], 1, 1) * slope).astype(BF16)
        acc_s[...] += mul(grad_hidden, w1_ref[k], 1, 1)
        if grads is not None:
            active = stored[0][k]
            g1_s[k] = mul(c_s[...], grad_hidden, 0, 0).astype(BF16)
            g2_s[rows, :] = mul(active, grad_second, 0, 0).astype(BF16)
            gv_ref[pl.ds(8 + k, 1), :] = total_of(grad_hidden.astype(F32))

    grad_y = dy_ref[...].astype(F32) * mask_ref[:own, :1]
    grad_c = acc_s[...]
    unit, scale = norm_parts(mid_ref[...])
    grad_mid = grad_y + norm_grad(grad_c, row_of(vec_ref, 1), unit, scale)
    gmid_ref[...] = grad_mid
    if grads is not None:
        gv_ref[1:2, :] = total_of(grad_c * unit)
        gv_ref[3:4, :] = total_of(grad_c)
        gv_ref[6:7, :] = total_of(grad_mid.astype(BF16).astype(F32))
        gv_ref[7:8, :] = total_of(grad_y.astype(BF16).astype(F32))


def attend_backward(x_ref, mask_ref, wa_ref, vec_ref, kept, scratch, gmid_ref, du_ref, grads):
    q_s, k_s, v_s, ot_s, kt_s, p_s = kept
    do_s, dq_s, dk_s, dv_s = scratch
    own, width = gmid_ref.shape
    pairs = do_s.shape[0]
    head_dim = width // HEADS
    grad_branch = gmid_ref[...].astype(BF16)
    grad_att = mul(grad_branch, wa_ref[3], 1, 1).astype(BF16)
    for j in range(pairs):
        do_s[j] = grad_att[:, j * 128 : (j + 1) * 128]
    if grads is not None:
        ga_s, gv_ref = grads
        for j in range(pairs):
            ga_s[3, j * 128 : (j + 1) * 128, :] = mul(ot_s[j], grad_branch).astype(BF16)
    halves = head_halves(head_dim)

    for j in range(pairs):
        grad_k = None
        for e in range(2):
            half_do = do_s[j] * halves[e]
            half_q = q_s[j] * halves[e]
            grad_p = mul(v_s[j], half_do, 1, 1)
            probs_low = p_s[2 * j + e]
            probs = probs_low.astype(F32)
            row_dot = total_of(probs * grad_p)
            grad_s = (probs * (grad_p - row_dot)).astype(BF16)
            rows = slice(e * head_dim, (e + 1) * head_dim)
            dq_s[j, rows, :] = (mul(kt_s[j, rows, :], grad_s) * head_dim ** (-0.5)).astype(BF16)
            part_k = mul(grad_s, half_q)
            part_v = mul(probs_low, half_do)
            grad_k, grad_v = (part_k, part_v) if grad_k is None else (grad_k + part_k, grad_v + part_v)
        dk_s[j] = grad_k.astype(BF16)
        dv_s[j] = grad_v.astype(BF16)

    grad_q = jnp.concatenate([dq_s[j].T for j in range(pairs)], axis=1)
    grad_k = jnp.concatenate([dk_s[j] for j in range(pairs)], axis=1)
    grad_v = jnp.concatenate([dv_s[j] for j in range(pairs)], axis=1)
    mask = mask_ref[:, :1]
    unit, scale = norm_parts(x_ref[...].astype(F32) * mask)
    if grads is not None:
        normed = (unit * row_of(vec_ref, 0) + row_of(vec_ref, 2)).astype(BF16)
        ga_s[0] = mul(normed[:own], grad_q, 0, 0).astype(BF16)
        turned = normed.T
        ga_s[1] = mul(turned, grad_k).astype(BF16)
        ga_s[2] = mul(turned, grad_v).astype(BF16)
        gv_ref[4:5, :] = total_of(grad_q.astype(F32))
        gv_ref[5:6, :] = total_of(grad_v.astype(F32))
    grad_n = mul(grad_k, wa_ref[1], 1, 1) + mul(grad_v, wa_ref[2], 1, 1)
    grad_n = jnp.concatenate([grad_n[:own] + mul(grad_q, wa_ref[0], 1, 1), grad_n[own:]], axis=0)
    if grads is not None:
        gv_ref[0:1, :] = total_of(grad_n * unit)
        gv_ref[2:3, :] = total_of(grad_n)
    grad_u = norm_grad(grad_n, row_of(vec_ref, 0), unit, scale)
    grad_u = jnp.concatenate([grad_u[:own] + gmid_ref[...], grad_u[own:]], axis=0)
    du_ref[...] = (grad_u * mask).astype(BF16)


def pack_kernel(place_ref, qkv_ref, out_ref, fc1_ref, fc2_ref, gains_ref, shifts_ref, bias_ref, a_ref, b_ref, c_ref):
    rows, width = out_ref.shape
    index = place_ref[3]

    def columns(ref, count):
        wide = ref[...].astype(F32)
        return [wide[:, s * width : (s + 1) * width] for s in range(count)]

    lane = lax.broadcasted_iota(jnp.int32, (1, width), 1)
    row = lax.broadcasted_iota(jnp.int32, (16, width), 0)
    tail, base = jnp.zeros((16, width), F32), 0
    for ref, used in ((gains_ref, 2), (shifts_ref, 6), (bias_ref, 4)):
        length = ref.shape[1]
        start = index * length
        first, offset = start // width, lax.rem(start, width)
        spread = jnp.concatenate(
            [ref[...].astype(F32), jnp.zeros((1, width - length), F32)], axis=1
        )
        spread = pltpu.roll(jnp.broadcast_to(spread, (8, width)), offset, 1)[:1]
        target = base + first + jnp.where(lane < offset, 1, 0)
        tail = tail + jnp.where(row == target, spread, 0.0)
        base += used
    blocks = columns(qkv_ref, 3) + [out_ref[...].astype(F32), tail]
    a_ref[...] = jnp.concatenate(blocks, axis=0).astype(BF16)
    b_ref[...] = jnp.concatenate(columns(fc1_ref, 4), axis=0).astype(BF16)
    c_ref[...] = fc2_ref[...]


def finish_kernel(place_ref, body_ref, rest_ref, came_ref, qkv_ref, out_ref, *vector_refs):
    rows, width = out_ref.shape[1:]
    index = place_ref[3]
    count = 4 * rows
    summed = body_ref[...] + came_ref[:count, :].astype(F32)
    vectors = rest_ref[...] + came_ref[count:, :].astype(F32)
    for s in range(3):
        qkv_ref[0, :, s * width : (s + 1) * width] = summed[s * rows : (s + 1) * rows]
    out_ref[0] = summed[3 * rows :]
    lane = lax.broadcasted_iota(jnp.int32, (8, width), 1)
    row = lax.broadcasted_iota(jnp.int32, (16, width), 0)
    base = 0
    for ref, used in zip(vector_refs, (2, 6, 4)):
        length = ref.shape[1]
        first, offset = index * length // width, lax.rem(index * length, width)

        def turned(which):
            picked = total_of(jnp.where(row == which, vectors, 0.0))
            picked = jnp.broadcast_to(picked, (8, width))
            return pltpu.roll(picked, lax.rem(width - offset, width), 1)

        whole = jnp.where(lane < width - offset, turned(base + first), turned(base + first + 1))
        ref[...] = whole[:1, :length]
        base += used


def piece_groups(place_ref, mine, theirs, turns):
    outer, core, line = place_ref[0], place_ref[1], place_ref[2]
    count = mine[0].shape[0]
    for side, members in enumerate((mine, theirs)):
        for turn in range(turns):
            index = lax.rem(outer + (turns - turn), turns) * 2 + (core if side == 0 else 1 - core)
            yield index, [
                members[turn][turned_bits(line ^ z, count)].astype(F32) for z in range(count)
            ]


def halved_groups(place_ref, mine, theirs, turns):
    outer, core, line = place_ref[0], place_ref[1], place_ref[2]
    count = mine[0].shape[0] // turns * 2
    for side, (even, odd) in enumerate((mine, theirs)):
        for turn in range(turns):
            index = lax.rem(outer + (turns - turn), turns) * 2 + (core if side == 0 else 1 - core)
            blocks = []
            for z in range(count):
                entry = turned_bits((line ^ z) // 2, count // 2) * turns + turn
                blocks.append(jnp.where((line ^ z) % 2 == 0, even[entry], odd[entry]).astype(F32))
            yield index, blocks


def first_kernel(loose, rows, ins, outs, scratch):
    place_ref, x_ref, mask_ref = ins[:3]
    if loose:
        mine, theirs = ins[3 : 3 + loose], ins[3 + loose :]
        mid_ref, wa_out, vec_out = outs
        wa_ref, vec_ref = wa_out, vec_out
        vector = None
        for index, blocks in piece_groups(place_ref, mine, theirs, loose):
            span = rows * len(blocks)
            start = pl.multiple_of(index * span, 16)
            for s in range(4):
                group = jnp.concatenate([b[s * rows : (s + 1) * rows] for b in blocks], axis=0)
                wa_ref[s, pl.ds(start, span), :] = group.astype(BF16)
            for b in blocks:
                tail = b[4 * rows : 4 * rows + 16]
                vector = tail if vector is None else vector + tail
        vec_ref[...] = vector
    else:
        wa_ref, vec_ref = (member for member in ins[3:])
        (mid_ref,) = outs
    attend_forward(x_ref, mask_ref, wa_ref, vec_ref, (*scratch, None, None), mid_ref)


def second_kernel(loose, rows, ins, outs, scratch):
    place_ref, mid_ref, mask_ref, vec_ref = ins[:4]
    c_s, acc_s = scratch
    if loose:
        sets = [ins[4 : 4 + loose], ins[4 + loose : 4 + 2 * loose], ins[-4:-2], ins[-2:]]
        y_ref, w1_ref, w2_ref = outs
        for index, blocks in piece_groups(place_ref, sets[0], sets[1], loose):
            span = rows * len(blocks)
            start = pl.multiple_of(index * span, 16)
            for s in range(4):
                group = jnp.concatenate([b[s * rows : (s + 1) * rows] for b in blocks], axis=0)
                w1_ref[s, pl.ds(start, span), :] = group.astype(BF16)
        for index, blocks in halved_groups(place_ref, sets[2], sets[3], loose):
            span = 4 * rows * len(blocks)
            group = jnp.concatenate(blocks, axis=0)
            w2_ref[pl.ds(pl.multiple_of(index * span, 16), span), :] = group.astype(BF16)
    else:
        w1_ref, w2_ref = ins[4:]
        (y_ref,) = outs
    feed_forward(mid_ref, mask_ref, w1_ref, w2_ref, vec_ref, c_s, acc_s, None, y_ref)


def middle_kernel(ins, outs, scratch):
    x_ref, mask_ref, vec_ref, wa_ref, w1_ref, w2_ref, dy_ref = ins
    du_ref, mid_ref, c_s, *kept = outs
    vt_s, acc_s, gmid_s, *grad_scratch = scratch
    q_s, k_s, v_s, ot_s, kt_s, p_s = kept
    attend_forward(
        x_ref, mask_ref, wa_ref, vec_ref, (q_s, k_s, v_s, vt_s, ot_s, kt_s, p_s), mid_ref
    )
    unit, _ = norm_parts(mid_ref[...])
    c_s[...] = (unit * row_of(vec_ref, 1) + row_of(vec_ref, 3)).astype(BF16)
    feed_backward(
        mid_ref, mask_ref, dy_ref, w1_ref, w2_ref, vec_ref, c_s, acc_s, None, gmid_s, None
    )
    attend_backward(x_ref, mask_ref, wa_ref, vec_ref, kept, grad_scratch, gmid_s, du_ref, None)


def output_kernel(ins, outs, scratch):
    mid_ref, mask_ref, vec_ref, w1_ref, w2_ref = ins
    y_ref, active_ref, slope_ref = outs
    feed_forward(
        mid_ref, mask_ref, w1_ref, w2_ref, vec_ref, *scratch, (active_ref, slope_ref), y_ref
    )


def share_out(core, blocks_of, outer_count, start, size, kept_ref, sent_ref):
    for o in range(outer_count):
        even, odd = blocks_of(2 * o), blocks_of(2 * o + 1)
        kept_ref[o, start : start + size, :] = jnp.where(core == 0, even, odd)
        sent_ref[o, start : start + size, :] = jnp.where(core == 0, odd, even)


def feed_grad_kernel(ins, outs, scratch):
    place_ref, dy_ref, mid_ref, vec_ref, mask_ref, w1_ref, w2_ref, c_ref, active_ref, slope_ref = ins
    kept_ref, sent_ref, gmid_ref, gv_ref = outs
    acc_s, g1_s, g2_s = scratch
    gv_ref[...] = jnp.zeros_like(gv_ref)
    outer_count = kept_ref.shape[0]
    span = w1_ref.shape[1] // (2 * outer_count)
    feed_backward(
        mid_ref, mask_ref, dy_ref, w1_ref, w2_ref, vec_ref, c_ref, acc_s,
        (active_ref, slope_ref), gmid_ref, (g1_s, g2_s, gv_ref),
    )
    core = place_ref[1]
    for s in range(4):
        share_out(
            core, lambda d: g1_s[s, d * span : (d + 1) * span, :], outer_count,
            s * span, span, kept_ref, sent_ref,
        )
    share_out(
        core, lambda d: g2_s[4 * d * span : 4 * (d + 1) * span, :], outer_count,
        4 * span, 4 * span, kept_ref, sent_ref,
    )


def attend_grad_kernel(ins, outs, scratch):
    place_ref, gmid_in, wa_in, ot_in, v_in, q_in, kt_in, p_in, k_in, x_in, mask_in, vec_in, gv_in = ins
    du_ref, kept_ref, sent_ref = outs
    do_s, dq_s, dk_s, dv_s, ga_s, gv_s = scratch
    gmid_ref, wa_ref, ot_s = gmid_in, wa_in, ot_in
    outer_count = kept_ref.shape[0]
    span = wa_ref.shape[1] // (2 * outer_count)
    gv_s[...] = gv_in[...]
    attend_backward(
        x_in, mask_in, wa_ref, vec_in, (q_in, k_in, v_in, ot_s, kt_in, p_in),
        (do_s, dq_s, dk_s, dv_s), gmid_ref, du_ref, (ga_s, gv_s),
    )
    core = place_ref[1]
    for s in range(4):
        share_out(
            core, lambda d: ga_s[s, d * span : (d + 1) * span, :], outer_count,
            s * span, span, kept_ref, sent_ref,
        )
    tail = gv_s[...].astype(BF16)
    for o in range(outer_count):
        kept_ref[o, 4 * span :, :] = tail
        sent_ref[o, 4 * span :, :] = tail


def call(kernel, operands, results, scratch, flops, after=()):
    space = {"s": pltpu.SMEM, "v": pltpu.VMEM}

    def body(*refs):
        refs = list(refs[len(after) :])
        given, refs = refs[: len(operands)], refs[len(operands) :]
        kernel(given, refs[: len(results)], refs[len(results) :])

    return pl.pallas_call(
        body,
        out_shape=[jax.ShapeDtypeStruct(*result) for result in results],
        in_specs=[pl.BlockSpec(memory_space=pl.ANY)] * len(after)
        + [pl.BlockSpec(memory_space=space[kind]) for kind, _ in operands],
        out_specs=[pl.BlockSpec(memory_space=pltpu.VMEM)] * len(results),
        scratch_shapes=[pltpu.VMEM(*shape) for shape in scratch],
        compiler_params=pltpu.CompilerParams(vmem_limit_bytes=VMEM_LIMIT),
        cost_estimate=pl.CostEstimate(flops=flops, bytes_accessed=4 * 10**6, transcendentals=10**6),
    )(*after, *[array for _, array in operands])


def call_whole(kernel, operands, shapes, flops):
    def block(shape):
        return pl.BlockSpec(shape, lambda i: (0,) * len(shape))

    return pl.pallas_call(
        kernel,
        grid=(1,),
        out_shape=[jax.ShapeDtypeStruct(*shape) for shape in shapes],
        in_specs=[pl.BlockSpec(memory_space=pltpu.SMEM)]
        + [block(operand.shape) for operand in operands[1:]],
        out_specs=[block(shape[0]) for shape in shapes],
        cost_estimate=pl.CostEstimate(flops=flops, bytes_accessed=10**6, transcendentals=0),
    )(*operands)


VMEM_LIMIT = 24 * 1024 * 1024


def axis_sizes():
    return lax.axis_size("dp"), lax.axis_size("seq")


def places(lengths):
    dp_count, seq_count = axis_sizes()
    outer_count = dp_count // 2
    d, z = lax.axis_index("dp"), lax.axis_index("seq")
    o, index = d // 2, d * seq_count + z
    block = seq_count // 4

    def unsigned(value):
        return value.astype(jnp.uint32)

    return {
        "first": lax.axis_index("section") == 0,
        "operand": jnp.stack([o, d % 2, z, index]).astype(jnp.int32),
        "outer": [unsigned((o + k) % outer_count) for k in range(outer_count)],
                "bits": [
            (unsigned(z // step % 2), unsigned(1 - z // step % 2)) for step in reversed(line_steps())
        ],
        "even": z % 2 == 0,
        "micro": z // block // 2 == 0,
        "slots": [unsigned(index * length) for length in lengths],
    }


def pick(value, index, axis, rows=None):
    starts = [np.uint32(0)] * value.ndim
    starts[axis] = index
    sizes = list(value.shape)
    sizes[axis] = 1
    if rows is not None:
        starts[axis + 1], sizes[axis + 1] = np.uint32(rows[0]), rows[1] - rows[0]
    return lax.dynamic_slice(value, starts, sizes).reshape(sizes[:axis] + sizes[axis + 1 :])


def swap_core(value):
    return lax.ppermute(value, "dp", [(d, d ^ 1) for d in range(lax.axis_size("dp"))])


def turn_outer(value, steps):
    count = lax.axis_size("dp")
    return lax.ppermute(value, "dp", [(d, (d + 2 * steps) % count) for d in range(count)])


def turn_line(value, steps):
    count = lax.axis_size("seq")
    return lax.ppermute(value, "seq", [(z, (z + steps) % count) for z in range(count)])


def joint_permute(value, moves):
    seq_count = lax.axis_size("seq")
    pairs = [(a[0] * seq_count + a[1], b[0] * seq_count + b[1]) for a, b in moves]
    return lax.ppermute(value, ("dp", "seq"), pairs)


def line_steps():
    count, steps = lax.axis_size("seq"), []
    while count > 1:
        count //= 2
        steps.append(count)
    return steps


def cross_line(value, distance):
    count = lax.axis_size("seq")
    return lax.ppermute(value, "seq", [(z, z ^ distance) for z in range(count)])


def gather_step(pieces, step):
    return jnp.concatenate([pieces, cross_line(pieces, line_steps()[step])])


def gather_from(pieces, step, stop=None):
    for later in range(step, len(line_steps()) if stop is None else stop):
        pieces = gather_step(pieces, later)
    return pieces


def turned_bits(value, count):
    result, low, high = value * 0, 1, count // 2
    while high:
        result = result + (value // high) % 2 * low
        low, high = low * 2, high // 2
    return result


def gather_outer(stacked):
    return [stacked] + [turn_outer(stacked, k) for k in range(1, lax.axis_size("dp") // 2)]


def assemble(mine, theirs):
    outer_count, seq_count = len(mine), lax.axis_size("seq")
    d, z = lax.axis_index("dp"), lax.axis_index("seq")
    o, c = d // 2, d % 2
    turned = jnp.stack([jnp.stack(mine), jnp.stack(theirs)])
    sides = (jnp.arange(2) + c) % 2
    outers = (o - jnp.arange(outer_count)) % outer_count
    lines = turned_bits(z ^ jnp.arange(seq_count), seq_count)
    ordered = turned[sides][:, outers][:, :, lines]
    return ordered.transpose(1, 0, 2, 3, 4).reshape((-1,) + mine[0].shape[1:])


def scatter_core(kept, came, at, rows):
    def both(index):
        mine, theirs = (
            pick(member, index, 0, rows).astype(F32) for member in (kept, came)
        )
        return mine + theirs

    return both(at["outer"][0]), [both(index).astype(BF16) for index in at["outer"][1:]]


def scatter_outer(total, sent):
    for k, member in enumerate(sent):
        total = total + turn_outer(member, k + 1).astype(F32)
    return total


def line_blocks(total, lead, tail=0):
    body, rest = total[: total.shape[0] - tail], total[total.shape[0] - tail :]
    return body.reshape(lead, lax.axis_size("seq"), -1, total.shape[1]), rest


def halve_parts(state, at, step):
    body, rest = state
    mine, other = at["bits"][step]
    lead, count, _, width = body.shape
    halves = body.reshape(lead, count // 2, 2, -1, width)
    body, sent = pick(halves, mine, 2), pick(halves, other, 2).reshape(-1, width)
    if rest.shape[0]:
        sent = jnp.concatenate([sent, rest])
    return (body, rest), sent.astype(BF16)


def halve_sum(state, sent, step):
    body, rest = state
    came = cross_line(sent, line_steps()[-1 - step]).astype(F32)
    tail = rest.shape[0]
    body = body + came[: came.shape[0] - tail].reshape(body.shape)
    return body, rest + came[came.shape[0] - tail :]


def halve_line(state, at, step):
    return halve_sum(*halve_parts(state, at, step), step)


def halve_rest(state, at, step):
    for later in range(step, len(at["bits"])):
        state = halve_line(state, at, later)
    return state


def image_moves(step):
    dp_count, seq_count = axis_sizes()
    block = seq_count // 4
    moves = []
    for d in range(dp_count):
        for z in range(seq_count):
            micro = (step + z) % 2
            rank = z // 2
            target = (d - d % 2 + rank % 2, (2 * micro + d % 2) * block + rank // 2)
            moves.append(((d, z), target))
    return moves


def to_images(blocks, at):
    arrived = []
    for step in range(2):
        sent = jnp.where(at["even"], blocks[step], blocks[1 - step])
        arrived.append(joint_permute(sent, image_moves(step)))
    low = jnp.where(at["micro"], arrived[0], arrived[1])
    high = jnp.where(at["micro"], arrived[1], arrived[0])
    return jnp.concatenate([low, high], axis=0)


def from_images(rows_own, at, after):
    half = rows_own.shape[0] // 2
    low, high = rows_own[:half], rows_own[half:]
    arrived = []
    for step in range(2):
        sent = jnp.where(at["micro"], *((low, high) if step == 0 else (high, low)))
        arrived.append(joint_permute(sent, [(b, a) for a, b in image_moves(step)]))
    after, *arrived = lax.optimization_barrier((after, *arrived))
    return jnp.stack([jnp.where(at["even"], arrived[m], arrived[1 - m]) for m in range(2)]), after


def group_members():
    block = lax.axis_size("seq") // 4
    return [(turn, flip) for turn in range(block) for flip in range(2)][1:]


def group_moves(turn, flip):
    dp_count, seq_count = axis_sizes()
    block = seq_count // 4
    moves = []
    for d in range(dp_count):
        for z in range(seq_count):
            base = z - z % block
            moves.append(((d ^ flip, base + (z % block + turn) % block), (d, z)))
    return moves


def gather_group(own_rows):
    arrived = [joint_permute(own_rows, group_moves(*member)) for member in group_members()]
    return jnp.concatenate([own_rows] + arrived, axis=0)


def scatter_group(partial, own):
    total = partial[:own].astype(F32)
    for place, member in enumerate(group_members()):
        sent = partial[(place + 1) * own : (place + 2) * own]
        back = [(b, a) for a, b in group_moves(*member)]
        total = total + joint_permute(sent, back).astype(F32)
    return total.astype(BF16)


def slot_mask(lengths, slot_count):
    block = lax.axis_size("seq") // 4
    d, z = lax.axis_index("dp"), lax.axis_index("seq")
    c, group = d % 2, z // block
    theirs = swap_core(lengths[:, 0])
    counts = jnp.where(group % 2 == c, lengths[:, 0], theirs)
    counts = jnp.where(group // 2 == 0, counts[0], counts[1])
    places = jnp.arange(slot_count, dtype=jnp.int32)
    parts = []
    for turn, flip in [(0, 0)] + group_members():
        rank = (z % block + turn) % block * 2 + (c ^ flip)
        picked = lax.dynamic_slice_in_dim(counts, 2 * rank, 2, 0)
        parts.append((places[None, :] < picked[:, None]).astype(F32).reshape(-1, 1))
    return jnp.broadcast_to(jnp.concatenate(parts, axis=0), (len(parts) * 2 * slot_count, 128))


def to_section(value, steps):
    return lax.ppermute(value, "section", [(0, 1)] if steps == 1 else [(1, 0)])


def vector_slots(members, width):
    index = lax.axis_index("dp") * lax.axis_size("seq") + lax.axis_index("seq")
    count = lax.axis_size("dp") * lax.axis_size("seq")
    parts = []
    for member in members:
        length = member.shape[0]
        spread = jnp.zeros((count * length,), BF16)
        spread = lax.dynamic_update_slice_in_dim(spread, member, index * length, 0)
        parts.append(spread.reshape(-1, width))
    parts.append(jnp.zeros((4, width), BF16))
    return jnp.concatenate(parts, axis=0)


def own_slots(vectors, lengths, at):
    parts, start = [], 0
    for length, used, place in zip(lengths, (2, 6, 4), at["slots"]):
        flat = vectors[start : start + used].reshape(-1)
        parts.append(lax.dynamic_slice_in_dim(flat, place, length, 0))
        start += used
    return parts


def by_column(member, width):
    rows = member.shape[0]
    return member.reshape(rows, -1, width).transpose(1, 0, 2).reshape(-1, width)


def from_columns(block, rows):
    width = block.shape[1]
    return block.reshape(-1, rows, width).transpose(1, 0, 2).reshape(rows, -1)


def on_device(boundary, lengths, w_qkv, w_out, w_fc1, w_fc2, gains, shifts, fc1_bias):
    dp_count, seq_count = axis_sizes()
    outer_count = dp_count // 2
    lens = (gains.shape[1], shifts.shape[1], fc1_bias.shape[1])
    at = places(lens)
    place = at["operand"]
    slot_count = boundary.shape[3]
    own = 2 * slot_count
    total = lengths.shape[2] * slot_count
    rows, width = w_out.shape[1:]
    hidden = rows * 4 * dp_count * seq_count
    pairs = width // 128
    span = width // dp_count
    loose = outer_count if rows % 8 == 0 else 0
    if loose:
        piece_a, piece_b, piece_c = call_whole(
            pack_kernel,
            [place, w_qkv[0], w_out[0], w_fc1[0], w_fc2[0], gains, shifts, fc1_bias],
            [((4 * rows + 16, width), BF16)] + [((4 * rows, width), BF16)] * 2,
            10**9,
        )
    else:
        tail = vector_slots((gains[0], shifts[0], fc1_bias[0]), width)
        piece_a = jnp.concatenate([by_column(w_qkv[0], width), w_out[0], tail])
        piece_b, piece_c = by_column(w_fc1[0], width), w_fc2[0]
    own_start = to_images(boundary[0, :, 0], at)
    piece_a, at = lax.optimization_barrier((piece_a, at))
    half_a = gather_step(piece_a[None], 0)
    near_c = jnp.stack(gather_outer(piece_c))
    half_a, piece_b, near_c = lax.optimization_barrier((half_a, piece_b, near_c))
    line_a = gather_from(half_a, 1)
    half_b = gather_step(piece_b[None], 0)
    line_a, half_b, near_c, own_start = lax.optimization_barrier(
        (line_a, half_b, near_c, own_start)
    )
    mine_a = gather_outer(line_a)
    line_b = gather_from(half_b, 1)
    half_c = gather_step(near_c, 0)
    line_b, half_c, *mine_a = lax.optimization_barrier((line_b, half_c, *mine_a))
    mine_b = gather_outer(line_b)
    half_c = gather_from(half_c, 1, len(line_steps()) - 1)
    mine_c = [half_c, cross_line(half_c, line_steps()[-1])]
    mask = slot_mask(lengths, slot_count)
    all_start = gather_group(own_start)
    theirs_a = [swap_core(member) for member in mine_a]

    w_shape = ((4, width, width), BF16)
    tall_shape = ((hidden, width), BF16)
    vec_shape = ((16, width), F32)
    mid_shape = ((own, width), F32)
    low_shape = ((own, width), BF16)
    all_shape = ((total, width), BF16)
    q_shape = ((pairs, own, 128), BF16)
    k_shape = ((pairs, total, 128), BF16)
    qt_shape = ((pairs, 128, own), BF16)
    kt_shape = ((pairs, 128, total), BF16)
    p_shape = ((HEADS, total, own), BF16)
    h_shape = ((4, own, width), F32)
    active_shape = ((4, own, width), BF16)
    shared_b = ((outer_count, 8 * span, width), BF16)
    shared_a = ((outer_count, 4 * span + 16, width), BF16)

    head_scratch = [q_shape, k_shape, k_shape, kt_shape, qt_shape]
    if loose:
        middle, w_a, vectors = call(
            functools.partial(first_kernel, loose, rows),
            [("s", place), ("v", all_start), ("v", mask)]
            + [("v", member) for member in (*mine_a, *theirs_a)],
            [mid_shape, w_shape, vec_shape],
            head_scratch, 10**9, [line_b],
        )
        middle, mine_c[1], *mine_b[1:] = lax.optimization_barrier(
            (middle, mine_c[1], *mine_b[1:])
        )
        theirs_b = [swap_core(member) for member in mine_b]
        theirs_c = [swap_core(member) for member in mine_c]
        first_out, w_1, w_2 = call(
            functools.partial(second_kernel, loose, rows),
            [("s", place), ("v", middle), ("v", mask), ("v", vectors)]
            + [("v", member) for member in (*mine_b, *theirs_b, *mine_c, *theirs_c)],
            [low_shape, w_shape, tall_shape],
            [low_shape, mid_shape], 10**9,
        )
    else:
        theirs_b = [swap_core(member) for member in mine_b]
        theirs_c = [swap_core(member) for member in mine_c]
        ordered = assemble(mine_a, theirs_a)
        w_a = ordered[:, : 4 * rows].reshape(-1, 4, rows, width).transpose(1, 0, 2, 3)
        w_a = w_a.reshape(4, width, width)
        vectors = jnp.sum(ordered[:, 4 * rows :].astype(F32), axis=0)
        w_1 = assemble(mine_b, theirs_b).reshape(-1, 4, rows, width).transpose(1, 0, 2, 3)
        w_1 = w_1.reshape(4, width, width)
        apart = [
            [
                jnp.concatenate(member).reshape(seq_count, outer_count, -1, width)[:, k]
                for k in range(outer_count)
            ]
            for member in (mine_c, theirs_c)
        ]
        w_2 = assemble(*apart).reshape(hidden, width)
        (middle,) = call(
            functools.partial(first_kernel, loose, rows),
            [("s", place), ("v", all_start), ("v", mask), ("v", w_a), ("v", vectors)],
            [mid_shape], head_scratch, 10**9,
        )
        (first_out,) = call(
            functools.partial(second_kernel, loose, rows),
            [("s", place), ("v", middle), ("v", mask), ("v", vectors), ("v", w_1), ("v", w_2)],
            [low_shape], [low_shape, mid_shape], 10**9,
        )
    arrived = gather_group(to_section(first_out, 1))
    layer_in = jnp.where(at["first"], all_start, arrived)
    grad_scratch = [q_shape, qt_shape, k_shape, k_shape]
    saved = [mid_shape, low_shape, q_shape, k_shape, k_shape, qt_shape, kt_shape, p_shape]
    partial, middle, normed, q, k, v, ot, kt, p = call(
        middle_kernel,
        [("v", layer_in)]
        + [("v", member) for member in (mask, vectors, w_a, w_1, w_2, own_start)],
        [all_shape, *saved],
        [kt_shape, mid_shape, mid_shape, *grad_scratch], 4 * 10**9,
    )
    sent_back = scatter_group(partial, own)
    returned = to_section(sent_back, -1)
    layer_out, active, slope = call(
        output_kernel,
        [("v", member) for member in (middle, mask, vectors, w_1, w_2)],
        [low_shape, active_shape, h_shape], [low_shape, mid_shape], 2 * 10**9, [sent_back],
    )
    grad_out = jnp.where(at["first"], returned, own_start)
    kept_b, sent_b, grad_mid, grad_vectors = call(
        feed_grad_kernel,
        [("s", place), ("v", grad_out)]
        + [
            ("v", member)
            for member in (middle, vectors, mask, w_1, w_2, normed, active, slope)
        ],
        [shared_b, shared_b, mid_shape, vec_shape],
        [mid_shape, w_shape, tall_shape], 2 * 10**9,
    )
    came_b = swap_core(sent_b)
    both_c = kept_b[:, 4 * span :].astype(F32) + came_b[:, 4 * span :].astype(F32)
    state_c, sent_c = halve_parts(line_blocks(both_c.reshape(-1, width), outer_count), at, 0)
    kept_b, sent_b = scatter_core(kept_b, came_b, at, (0, 4 * span))
    partial, kept_a, sent_a = call(
        attend_grad_kernel,
        [("s", place)]
        + [
            ("v", member)
            for member in (
                grad_mid, w_a, ot, v, q, kt, p, k, layer_in, mask, vectors, grad_vectors
            )
        ],
        [all_shape, shared_a, shared_a],
        [*grad_scratch, w_shape, vec_shape], 10**10, [*sent_b, sent_c],
    )

    total_b = scatter_outer(kept_b, sent_b)
    state_c = halve_sum(state_c, sent_c, 0)
    total_b, state_c, sent_a, partial = lax.optimization_barrier(
        (total_b, state_c, sent_a, partial)
    )
    kept_a, sent_a = scatter_core(kept_a, swap_core(sent_a), at, None)
    grad_in = scatter_group(partial, own)
    total_b, state_c, *sent_a = lax.optimization_barrier((total_b, state_c, *sent_a))
    total_a = scatter_outer(kept_a, sent_a)
    state_b = halve_line(line_blocks(total_b, 4), at, 0)
    body_c = halve_rest(state_c, at, 1)[0].reshape(outer_count, -1, width)
    rows_last = jnp.where(at["first"], grad_in, layer_out)
    total_a, state_b, body_c = lax.optimization_barrier((total_a, state_b, body_c))
    state_a = halve_line(line_blocks(total_a, 4, 16), at, 0)
    summed_b = halve_rest(state_b, at, 1)[0].reshape(-1, width)
    summed_c = scatter_outer(
        pick(body_c, at["outer"][0], 0),
        [pick(body_c, index, 0).astype(BF16) for index in at["outer"][1:]],
    )
    state_a, summed_b, summed_c = lax.optimization_barrier((state_a, summed_b, summed_c))
    last = len(at["bits"]) - 1
    for step in range(1, last):
        state_a = halve_line(state_a, at, step)
    (body, rest), sent_a = halve_parts(state_a, at, last)
    sent_a, body, rows_last = lax.optimization_barrier((sent_a, body, rows_last))
    if loose:
        came = cross_line(sent_a, line_steps()[-1 - last])
        finished = call_whole(
            finish_kernel,
            [place, body.reshape(-1, width), rest, came],
            [((1, rows, 3 * width), F32), ((1, rows, width), F32)]
            + [((1, length), F32) for length in lens],
            10**10,
        )
        rows_out, _ = from_images(rows_last, at, came)
    else:
        summed_a, summed_v = halve_sum((body, rest), sent_a, last)
        rows_out, summed_v = from_images(rows_last, at, summed_v)
        summed_a = summed_a.reshape(-1, width)
        finished = [
            member[None]
            for member in (
                from_columns(summed_a[: 3 * rows], rows),
                summed_a[3 * rows :],
                *own_slots(summed_v, lens, at),
            )
        ]
    grads = (*finished[:2], from_columns(summed_b, rows)[None], summed_c[None], *finished[2:])
    return (rows_out[None, :, None], *grads)


def solution(mesh):
    sharded = P("section", ("dp", "seq"), None)
    vector = P("section", ("dp", "seq"))
    images = P("section", None, "dp", "seq", None)
    grads = (sharded, sharded, sharded, sharded, vector, vector, vector)
    return jax.shard_map(
        on_device,
        mesh=mesh,
        in_specs=(images, P(None, "dp", None), *grads),
        out_specs=(images, *grads),
        check_vma=False,
    )
```
